32 devices in a mesh: dom: 16 (over z, x, core), lag: 2 (over y).
Axes of the slice: x: 2, y: 2, z: 4, core: 2. Of those that a mesh axis runs over, the one named last changes fastest.
Arguments:
- delayed_crowd_history: bfloat16 [2, 64, 512, 128], P('lag', None, 'dom'), may hold values from -6 to 6
- predicted_crowd_array: bfloat16 [64, 512, 128], P('lag', 'dom'), may hold values from -40 to 40
- probe_target_spot: int32 [256, 256], P('dom'), may hold values from 0 to 255
- alive_probe_places: int32 [256], P('dom'), may hold values from 64 to 256, as said below
- probed_heat_levels: float32 [256, 256], P('dom'), may hold values from -6 to 6
- probe_reciprocal_spread: float32 [256, 256], P('dom'), may hold values from 0.1 to 1.6
- decay_extent_squares: int32 [256], P('dom'), may hold values from 16 to 32
Outputs:
- smoothed: bfloat16 [2, 64, 512, 128], P('lag', None, 'dom')
The draws below stay inside these ranges and needn't reach their ends.
Inputs may be any that keep to these rules, and one draw needn't show every extreme that they name: `alive_probe_places`: live observations of a patch occupy its first slots.
All inputs are finite; a program needn't handle non-finite values.
Results may differ from the reference program's by a relative error of at most 0.0062.
Values may be sent and summed in bfloat16 or wider, within the bound.
No kernel may reach another device: no remote copies, remote signals or barrier semaphores. Data moves between devices by JAX's collectives and lax.ppermute only.
A program may use at most 64 MiB of HBM per device.

```python
import math
import jax
import jax.numpy as jnp
from jax import lax

MEM = 64
PATCH = 16
COLS = 128
SENSOR_LIMIT = 256
RADIUS = 32
NS_STEPS = 4
REACH = 2
NROWS = 512
SUBDOMAINS = 256
LAGS = 2


def draw_predicted_crowd_array(key, part):
    key_member, key_cell, key_base, key_noise = jax.random.split(jax.random.fold_in(key, 11), 4)
    log_low = math.log(0.4)
    log_high = math.log(3.0)
    member_scale = jnp.exp(jax.random.uniform(key_member, (MEM, 1, 1), jnp.float32, log_low, log_high))
    cell_scale = jnp.exp(jax.random.uniform(key_cell, (1, NROWS, COLS), jnp.float32, math.log(0.5), math.log(2.0)))
    background = jax.random.normal(key_base, (1, NROWS, COLS), jnp.float32)
    noise_field = jax.random.normal(key_noise, (MEM, NROWS, COLS), jnp.float32)
    values = jnp.clip(background + member_scale * cell_scale * noise_field, -40.0, 40.0)
    return values.astype(jnp.bfloat16)


def draw_alive_probe_places(key, part):
    key_count, key_place = jax.random.split(jax.random.fold_in(key, 23))
    counts = jax.random.randint(key_count, (SUBDOMAINS,), SENSOR_LIMIT // 4, SENSOR_LIMIT + 1, jnp.int32)
    chosen = jax.random.permutation(key_place, SUBDOMAINS)
    counts = counts.at[chosen[0]].set(SENSOR_LIMIT)
    return counts.at[chosen[1]].set(SENSOR_LIMIT // 4)


def draw_decay_extent_squares(key, part):
    key_value, key_place = jax.random.split(jax.random.fold_in(key, 37))
    radii = jax.random.randint(key_value, (SUBDOMAINS,), RADIUS // 2, RADIUS + 1, jnp.int32)
    chosen = jax.random.permutation(key_place, SUBDOMAINS)
    radii = radii.at[chosen[0]].set(RADIUS)
    return radii.at[chosen[1]].set(RADIUS // 2)


def place_ends(drawn, rng, least, largest):
    longest = drawn.shape.index(max(drawn.shape))
    spots = []
    for shift in (0, 1):
        where = [jax.random.randint(jax.random.fold_in(rng, axis), (), 0, length) for axis, length in enumerate(drawn.shape)]
        where[longest] = (where[longest] + shift) % drawn.shape[longest]
        spots.append(tuple(where))
    return drawn.at[spots[0]].set(least).at[spots[1]].set(largest)


def block_levels(own_key, shape, cuts, least, top_value):
    def one(position, blocks):
        heights = jax.random.uniform(jax.random.fold_in(jax.random.fold_in(own_key, 6), position), (blocks,), jnp.float32, least / len(cuts), top_value / len(cuts))
        return jnp.repeat(jnp.exp(heights), shape[position] // blocks).reshape((-1,) + (1,) * (len(shape) - position - 1))

    gain = one(*cuts[0])
    for cut in cuts[1:]:
        gain = gain * one(*cut)
    return gain


def noise(own_key, shape, width, limit, cuts=(), kind=jnp.bfloat16):
    level = block_levels(own_key, shape, cuts, -0.22, 0.18) if cuts else 1.0
    drawn = jax.random.normal(own_key, shape, jnp.float32) * width * level
    return jnp.minimum(jnp.maximum(drawn, -limit), limit).astype(kind)


def setup_inputs(seed: int = 0) -> dict:
    arg_keys = jax.random.split(jax.random.key(seed), 8)
    return {
        "delayed_crowd_history": noise(arg_keys[0], (LAGS, MEM, NROWS, COLS), 1.0, 6.0, ((0, 2), (2, 16))),
        "predicted_crowd_array": draw_predicted_crowd_array(jax.random.fold_in(arg_keys[7], 71), 0),
        "probe_target_spot": place_ends(jax.random.randint(arg_keys[2], (SUBDOMAINS, SENSOR_LIMIT), 0, PATCH * PATCH), jax.random.fold_in(arg_keys[2], 1), 0, (PATCH * PATCH) - 1).astype(jnp.int32),
        "alive_probe_places": draw_alive_probe_places(jax.random.fold_in(arg_keys[7], 71), 0),
        "probed_heat_levels": noise(arg_keys[4], (SUBDOMAINS, SENSOR_LIMIT), 1.0, 6.0, ((0, 16),), jnp.float32),
        "probe_reciprocal_spread": jnp.clip(jnp.exp(math.log(1.6) - 2.7725887 * jax.random.uniform(arg_keys[5], (SUBDOMAINS, SENSOR_LIMIT), jnp.float32) ** block_levels(arg_keys[5], (SUBDOMAINS, SENSOR_LIMIT), ((0, 16),), -0.2, 0.2)), 0.1, 1.6),
        "decay_extent_squares": draw_decay_extent_squares(jax.random.fold_in(arg_keys[7], 71), 0),
    }


def inverse_root(gram_part, right_side):
    crowd_members_number = gram_part.shape[-1]
    identity = jnp.eye(crowd_members_number, dtype=jnp.float32)
    frobenius = jnp.sqrt(lax.optimization_barrier(jnp.sum(gram_part * gram_part, axis=(1, 2))))
    bound_value = crowd_members_number - 1.0 + frobenius
    iterate = (gram_part + (crowd_members_number - 1.0) * identity) / bound_value[:, None, None]
    root_iter = jnp.broadcast_to(identity, gram_part.shape)
    for sweep_index in range(NS_STEPS):
        correction = 1.5 * identity - 0.5 * jnp.matmul(root_iter, iterate, precision=lax.Precision.HIGHEST)
        iterate = jnp.matmul(iterate, correction, precision=lax.Precision.HIGHEST)
        root_iter = jnp.matmul(correction, root_iter, precision=lax.Precision.HIGHEST)
    inner_prod = jnp.matmul(root_iter, right_side[:, :, None], precision=lax.Precision.HIGHEST)
    mean_weights = jnp.matmul(root_iter, inner_prod, precision=lax.Precision.HIGHEST)[:, :, 0] / bound_value[:, None]
    spread = jnp.sqrt(crowd_members_number - 1.0) / jnp.sqrt(bound_value)
    return (spread[:, None, None] * root_iter + mean_weights[:, :, None]).astype(jnp.bfloat16)

def reference(delayed_crowd_history, predicted_crowd_array, probe_target_spot, alive_probe_places, probed_heat_levels, probe_reciprocal_spread, decay_extent_squares):
    crowd_members_number, tile_vertical_extent, tile_lateral_extent = predicted_crowd_array.shape
    patch_rows = tile_vertical_extent // PATCH
    patch_cols = tile_lateral_extent // PATCH
    patch_total = patch_rows * patch_cols
    slot_count = probe_target_spot.shape[1]
    index_patch = jnp.arange(patch_total, dtype=jnp.int32)
    row_in = probe_target_spot // PATCH
    col_in = probe_target_spot % PATCH
    lattice_node_place = (((index_patch // patch_cols)[:, None] * PATCH + row_in) * tile_lateral_extent + (index_patch % patch_cols)[:, None] * PATCH + col_in).astype(jnp.int32)
    probed_markers = jnp.take(predicted_crowd_array.reshape(crowd_members_number, tile_vertical_extent * tile_lateral_extent), lattice_node_place.reshape(-1), axis=1)
    probed_markers = probed_markers.reshape(crowd_members_number, patch_total, slot_count)
    average_reading = lax.optimization_barrier(jnp.sum(probed_markers, axis=0, dtype=jnp.float32)) / crowd_members_number
    obs_anomaly = lax.optimization_barrier((probed_markers.astype(jnp.float32) - average_reading).astype(jnp.bfloat16))
    usable_entry = jnp.arange(slot_count, dtype=jnp.int32)[None, :] < alive_probe_places[:, None]
    obs_weight = lax.optimization_barrier(jnp.where(usable_entry, probe_reciprocal_spread, 0.0).astype(jnp.bfloat16))
    departure_vector = lax.optimization_barrier(jnp.where(usable_entry, probe_reciprocal_spread * (probed_heat_levels - average_reading), 0.0).astype(jnp.bfloat16))
    pad_plan = ((REACH, REACH), (REACH, REACH), (0, 0))
    anomaly_pad = jnp.pad(obs_anomaly.reshape(crowd_members_number, patch_rows, patch_cols, slot_count), ((0, 0),) + pad_plan)
    weight_pad = jnp.pad(obs_weight.reshape(patch_rows, patch_cols, slot_count), pad_plan)
    innov_pad = jnp.pad(departure_vector.reshape(patch_rows, patch_cols, slot_count), pad_plan)
    rowin_pad = jnp.pad(row_in.reshape(patch_rows, patch_cols, slot_count).astype(jnp.float32), pad_plan)
    colin_pad = jnp.pad(col_in.reshape(patch_rows, patch_cols, slot_count).astype(jnp.float32), pad_plan)
    radius = decay_extent_squares.reshape(patch_rows, patch_cols, 1).astype(jnp.float32)
    gram_sum = jnp.zeros((patch_rows, patch_cols, crowd_members_number, crowd_members_number), jnp.float32)
    right_side = jnp.zeros((patch_rows, patch_cols, crowd_members_number), jnp.float32)
    reach_width = 2 * REACH + 1
    for shift_row in range(reach_width):
        for shift_col in range(reach_width):
            anomaly_near = anomaly_pad[:, shift_row:shift_row + patch_rows, shift_col:shift_col + patch_cols, :]
            weight_near = weight_pad[shift_row:shift_row + patch_rows, shift_col:shift_col + patch_cols, :]
            innov_near = innov_pad[shift_row:shift_row + patch_rows, shift_col:shift_col + patch_cols, :]
            rowin_near = rowin_pad[shift_row:shift_row + patch_rows, shift_col:shift_col + patch_cols, :]
            colin_near = colin_pad[shift_row:shift_row + patch_rows, shift_col:shift_col + patch_cols, :]
            row_offset = (shift_row - REACH) * PATCH + rowin_near - 7.5
            col_offset = (shift_col - REACH) * PATCH + colin_near - 7.5
            taper_weight = jnp.square(jnp.maximum(0.0, 1.0 - (jnp.square(row_offset) + jnp.square(col_offset)) / jnp.square(radius)))
            scaled = lax.optimization_barrier((taper_weight * weight_near.astype(jnp.float32) * anomaly_near.astype(jnp.float32)).astype(jnp.bfloat16))
            weighted = lax.optimization_barrier((taper_weight * innov_near.astype(jnp.float32)).astype(jnp.bfloat16))
            gram_sum = gram_sum + jnp.einsum('mxyo,nxyo->xymn', scaled.astype(jnp.float32), anomaly_near.astype(jnp.float32))
            right_side = right_side + jnp.einsum('mxyo,xyo->xym', anomaly_near.astype(jnp.float32), weighted.astype(jnp.float32))
    transform = inverse_root(gram_sum.reshape(patch_total, crowd_members_number, crowd_members_number), right_side.reshape(patch_total, crowd_members_number))
    transform = lax.optimization_barrier(transform)
    mixing = transform.reshape(patch_rows, patch_cols, crowd_members_number, crowd_members_number).astype(jnp.float32)

    def smooth(lag_state):
        lag_mean = lax.optimization_barrier(jnp.sum(lag_state, axis=0, dtype=jnp.float32)) / crowd_members_number
        lag_anomaly = lax.optimization_barrier((lag_state.astype(jnp.float32) - lag_mean).astype(jnp.bfloat16))
        patch_grid = lag_anomaly.astype(jnp.float32).reshape(crowd_members_number, patch_rows, PATCH, patch_cols, PATCH)
        updated = jnp.einsum('maibj,abmn->naibj', patch_grid, mixing)
        return (updated.reshape(crowd_members_number, tile_vertical_extent, tile_lateral_extent) + lag_mean).astype(jnp.bfloat16)
    return lax.map(smooth, delayed_crowd_history)
```

```python
import functools

import jax
import jax.numpy as jnp
from jax import lax
from jax.experimental import pallas as pl
from jax.experimental.pallas import tpu as pltpu
from jax.sharding import PartitionSpec as P

PATCH = 16
NS_STEPS = 4
RADIUS = 32
SIDE = RADIUS - PATCH // 2

NT = (((1,), (1,)), ((), ()))
NN = (((1,), (0,)), ((), ()))
f32 = jnp.float32
bf16 = jnp.bfloat16


def mm(a, b, dims=NN):
    return lax.dot_general(a, b, dims, preferred_element_type=f32)


def split(x):
    high = x.astype(bf16)
    return high, (x - high.astype(f32)).astype(bf16)


def mm3(a, b):
    a_high, a_low = split(a)
    b_high, b_low = split(b)
    rows = a.shape[0]
    first = mm(jnp.concatenate([a_high, a_low], 0), b_high)
    return first[:rows] + (first[rows:] + mm(a_high, b_low))


def prepare_kernel(cols, alive_ref, spot_ref, level_ref, prec_ref, hist_ref, field_ref, lag_ref, mean_ref, flat_ref):
    patches, slots = spot_ref.shape
    patch_cols = cols // PATCH
    patch_rows = patches // patch_cols
    spot = spot_ref[...]
    row_in = spot // PATCH
    col_in = spot % PATCH
    slot_index = lax.broadcasted_iota(jnp.int32, (1, slots), 1)
    iota_row = lax.broadcasted_iota(jnp.int32, (PATCH, slots), 0)
    iota_col = lax.broadcasted_iota(jnp.int32, (cols, slots), 0)
    for a in range(patch_rows):
        total = jnp.zeros((4 * PATCH, cols), f32)
        for b in range(patch_cols):
            p = a * patch_cols + b
            prec = jnp.where(slot_index < alive_ref[p], prec_ref[p : p + 1, :], 0.0)
            level = prec * level_ref[p : p + 1, :]
            prec_high = prec.astype(bf16).astype(f32)
            level_high = level.astype(bf16).astype(f32)
            on_row = row_in[p : p + 1, :] == iota_row
            pieces = [
                jnp.where(on_row, piece, 0.0).astype(bf16)
                for piece in (prec_high, prec - prec_high, level_high, level - level_high)
            ]
            on_col = jnp.where(col_in[p : p + 1, :] + b * PATCH == iota_col, 1.0, 0.0).astype(bf16)
            total = total + mm(jnp.concatenate(pieces, 0), on_col, NT)
        rows = slice(a * PATCH, (a + 1) * PATCH)
        field_ref[0, rows, :] = total[:PATCH] + total[PATCH : 2 * PATCH]
        field_ref[1, rows, :] = total[2 * PATCH : 3 * PATCH] + total[3 * PATCH :]
    members, tile_rows, _ = hist_ref.shape
    state = hist_ref[...].astype(f32)
    mean = jnp.sum(state, axis=0) / members
    mean_ref[...] = mean
    flat_ref[...] = (state - mean[None]).reshape(members * tile_rows, cols)
    for r in range(tile_rows):
        lag_ref[r] = flat_ref[pl.ds(r, members, stride=tile_rows), :].astype(bf16)


def segment(flat_ref, fields, first_row, centre_row, col_square, inverse_square, total, group):
    rows, cols = fields.shape[1:]
    members = flat_ref.shape[0] // rows
    patches = col_square.shape[0]
    state = flat_ref[...].reshape(members, rows, cols)
    mean = jnp.sum(state, axis=0) / members
    flat_ref[...] = (state - mean[None]).reshape(members * rows, cols)
    weight = fields[0]
    innovation = fields[1] - mean * weight
    for start in range(0, rows, group):
        anomalies, lefts = [], []
        for r in range(start, start + group):
            anomaly = flat_ref[pl.ds(r, members, stride=rows), :].astype(bf16)
            offset = (first_row + r).astype(f32) - centre_row
            taper = jnp.square(jnp.maximum(0.0, 1.0 - (offset * offset + col_square) * inverse_square))
            scale = taper * weight[r : r + 1]
            blocks = anomaly.reshape(members // PATCH, PATCH, cols)
            left = [
                (blocks * jnp.broadcast_to(scale[q : q + 1], (PATCH, cols)).astype(bf16)[None]).reshape(members, cols)
                for q in range(patches)
            ]
            tail = taper * innovation[r : r + 1]
            left.append(jnp.concatenate([tail, jnp.zeros((PATCH - patches, cols), f32)], 0).astype(bf16))
            anomalies.append(anomaly)
            lefts.append(jnp.concatenate(left, 0))
        total = total + mm(jnp.concatenate(lefts, 1), jnp.concatenate(anomalies, 1), NT)
    return total


def transforms(total, patches, out_ref):
    members = total.shape[1]
    degree = members - 1.0
    row = lax.broadcasted_iota(jnp.int32, (members, members), 0)
    col = lax.broadcasted_iota(jnp.int32, (members, members), 1)
    identity = jnp.where(row == col, 1.0, 0.0)
    iterates, bounds, sides = [], [], []
    for q in range(patches):
        gram = total[q * members : (q + 1) * members]
        squares = jnp.sum(jnp.sum(gram * gram, axis=1, keepdims=True), axis=0, keepdims=True)
        bound = degree + jnp.sqrt(squares)
        bounds.append(bound)
        iterates.append((gram + degree * identity) / bound)
        at = patches * members + q
        sides.append(total[at : at + 1])
    roots = [None] * patches
    for step in range(NS_STEPS):
        for q in range(patches):
            product = iterates[q] if roots[q] is None else mm3(roots[q], iterates[q])
            correction = 1.5 * identity - 0.5 * product
            if step < NS_STEPS - 1:
                iterates[q] = mm3(iterates[q], correction)
            roots[q] = correction if roots[q] is None else mm3(correction, roots[q])
    ready = []
    for q in range(patches):
        side = jnp.broadcast_to(sides[q], (8, members))
        weights = mm3(mm3(side, roots[q]), roots[q])[:1] / bounds[q]
        spread = jnp.sqrt(degree * jnp.ones_like(bounds[q])) / jnp.sqrt(bounds[q])
        ready.append(spread * roots[q] + weights)
    for pair in range(patches // 2):
        both = jnp.concatenate([ready[2 * pair], ready[2 * pair + 1]], 1)
        out_ref[pair * members : (pair + 1) * members, :] = both.astype(bf16)


def gram_kernel(shares, patch_cols, place_ref, radius_ref, *refs):
    members_part, tile_rows, cols = refs[0].shape
    own, refs = refs[:shares], refs[shares:]
    big, refs = refs[:shares], refs[shares:]
    small, refs = refs[:shares], refs[shares:]
    field_own, field_big, field_small, out_ref, flat_own, flat_big, flat_small = refs
    lag = place_ref[0]
    patches = out_ref.shape[0] * 2 // (members_part * shares)
    members = members_part * shares
    first_patch = lag * patches
    patch_row = first_patch // patch_cols
    for parts, flat in ((own, flat_own), (big, flat_big), (small, flat_small)):
        rows = parts[0].shape[1]
        for k, part in enumerate(parts):
            share = lax.rem(lag + k, shares)
            at = pl.multiple_of(share * (members_part * rows), 8)
            flat[pl.ds(at, members_part * rows), :] = part[...].reshape(members_part * rows, cols).astype(f32)
    q_row = lax.broadcasted_iota(jnp.int32, (patches, cols), 0)
    col = lax.broadcasted_iota(jnp.int32, (patches, cols), 1)
    radius = jnp.zeros((patches, cols), f32)
    for q in range(patches):
        radius = jnp.where(q_row == q, radius_ref[first_patch + q].astype(f32), radius)
    centre_col = ((first_patch % patch_cols) + q_row).astype(f32) * PATCH + (PATCH - 1) / 2
    col_square = jnp.square(col.astype(f32) - centre_col)
    inverse_square = 1.0 / jnp.square(radius)
    centre_row = patch_row.astype(f32) * PATCH + (PATCH - 1) / 2
    big_first = jnp.where(patch_row == 0, -big[0].shape[1], tile_rows)
    small_first = jnp.where(patch_row == 0, tile_rows, -small[0].shape[1])
    total = jnp.zeros((patches * members + PATCH, members), f32)
    for flat, field, first in (
        (flat_own, field_own, jnp.int32(0)),
        (flat_big, field_big, big_first),
        (flat_small, field_small, small_first),
    ):
        total = segment(flat, field[...], first, centre_row, col_square, inverse_square, total, 8)
    transforms(total, patches, out_ref)


def smooth_kernel(shares, place_ref, lag_ref, mean_ref, *refs):
    parts, refs = refs[:shares], refs[shares:]
    out_ref, mixing_ref, flat_ref = refs
    tile_rows, members, cols = lag_ref.shape
    here = place_ref[0]
    rows = parts[0].shape[0]
    for k, part in enumerate(parts):
        at = pl.multiple_of(lax.rem(here + k, shares) * rows, 16)
        mixing_ref[pl.ds(at, rows), :] = part[...]
    lane = lax.broadcasted_iota(jnp.int32, (members, cols), 1) // PATCH
    even = jnp.where(lane % 2 == 0, 1.0, 0.0).astype(bf16)
    odd = jnp.where(lane % 2 == 1, 1.0, 0.0).astype(bf16)
    pairs = cols // (2 * PATCH)
    for a in range(tile_rows // PATCH):
        mixing = mixing_ref[a * pairs * members : (a + 1) * pairs * members, :]
        for r in range(a * PATCH, (a + 1) * PATCH, 2):
            right = jnp.concatenate(
                [jnp.concatenate([lag_ref[i] * even, lag_ref[i] * odd], 0) for i in (r, r + 1)], 1
            )
            spread = mm(mixing, right)
            for i in (0, 1):
                part = spread[:, i * cols : (i + 1) * cols]
                chosen = part[:members]
                for pair in range(1, pairs):
                    chosen = jnp.where(lane // 2 == pair, part[pair * members : (pair + 1) * members], chosen)
                flat_ref[pl.ds(r + i, members, stride=tile_rows), :] = chosen + mean_ref[r + i : r + i + 1, :]
    out_ref[...] = flat_ref[...].reshape(1, members, tile_rows, cols).astype(bf16)


def shards(history, forecast, spot, alive, levels, precision, radius):
    shares = lax.axis_size("lag")
    tiles = lax.axis_size("dom")
    lag = lax.axis_index("lag")
    members_part, tile_rows, cols = forecast.shape
    members = members_part * shares
    patch_cols = cols // PATCH
    patch_total = (tile_rows // PATCH) * patch_cols
    mine = patch_total // shares
    patch_row = (lag * mine) // patch_cols
    place = lag.reshape(1)
    big_rows = SIDE
    small_rows = SIDE - PATCH
    up, down = [], []
    for l in range(shares):
        towards = up if (l * mine) // patch_cols == 0 else down
        towards.append(l)
    forward = [(t * shares, (t + 1) * shares) for t in range(tiles - 1)]
    big_pairs = [(s + l, t + l) for s, t in forward for l in up] + [(t + l, s + l) for s, t in forward for l in down]
    small_pairs = [(t, s) for s, t in big_pairs]
    axes = ("dom", "lag")

    def halos(block):
        big = lax.dynamic_slice_in_dim(block, (1 - patch_row) * (tile_rows - big_rows), big_rows, 1)
        small = lax.dynamic_slice_in_dim(block, patch_row * (tile_rows - small_rows), small_rows, 1)
        return lax.ppermute(big, axes, big_pairs), lax.ppermute(small, axes, small_pairs)

    def gather(block):
        parts = [block]
        for k in range(1, shares):
            parts.append(lax.ppermute(block, "lag", [((i + k) % shares, i) for i in range(shares)]))
        return parts

    own = gather(forecast)
    smem = pl.BlockSpec(memory_space=pltpu.SMEM)
    vmem = pl.BlockSpec(memory_space=pltpu.VMEM)
    params = pltpu.CompilerParams(vmem_limit_bytes=32 * 2**20)
    fields, lag_rows, lag_mean = pl.pallas_call(
        functools.partial(prepare_kernel, cols),
        in_specs=[smem, vmem, vmem, vmem, vmem],
        out_specs=[vmem, vmem, vmem],
        out_shape=[
            jax.ShapeDtypeStruct((2, tile_rows, cols), f32),
            jax.ShapeDtypeStruct((tile_rows, members, cols), bf16),
            jax.ShapeDtypeStruct((tile_rows, cols), f32),
        ],
        scratch_shapes=[pltpu.VMEM((members * tile_rows, cols), f32)],
        compiler_params=params,
        name="prepare",
    )(alive, spot, levels, precision, history[0])
    sides = [halos(block) for block in own]
    field_big, field_small = halos(fields)
    parts = own + [side[0] for side in sides] + [side[1] for side in sides]
    mixing = pl.pallas_call(
        functools.partial(gram_kernel, shares, patch_cols),
        in_specs=[smem, smem] + [vmem] * (3 * shares + 3),
        out_specs=vmem,
        out_shape=jax.ShapeDtypeStruct((mine // 2 * members, 2 * members), bf16),
        scratch_shapes=[pltpu.VMEM((members * rows, cols), f32) for rows in (tile_rows, big_rows, small_rows)],
        compiler_params=params,
        name="gram",
    )(place, radius, *parts, fields, field_big, field_small)
    return pl.pallas_call(
        functools.partial(smooth_kernel, shares),
        in_specs=[smem] + [vmem] * (2 + shares),
        out_specs=vmem,
        out_shape=jax.ShapeDtypeStruct((1, members, tile_rows, cols), bf16),
        scratch_shapes=[
            pltpu.VMEM((patch_total // 2 * members, 2 * members), bf16),
            pltpu.VMEM((members * tile_rows, cols), f32),
        ],
        compiler_params=params,
        name="smooth",
    )(place, lag_rows, lag_mean, *gather(mixing))


def solution(mesh):
    in_specs = (
        P("lag", None, "dom", None),
        P("lag", "dom", None),
        P("dom", None),
        P("dom"),
        P("dom", None),
        P("dom", None),
        P("dom"),
    )
    out_specs = P("lag", None, "dom", None)
    return jax.shard_map(shards, mesh=mesh, in_specs=in_specs, out_specs=out_specs, check_vma=False)
```

```python
import functools

import jax
import jax.numpy as jnp
from jax import lax
from jax.experimental import pallas as pl
from jax.experimental.pallas import tpu as pltpu
from jax.sharding import PartitionSpec as P

PATCH = 16
NS_STEPS = 4
RADIUS = 32
FAR = RADIUS - PATCH // 2
NEAR = FAR - PATCH

NT = (((1,), (1,)), ((), ()))
NN = (((1,), (0,)), ((), ()))
f32 = jnp.float32
bf16 = jnp.bfloat16


def mm(a, b, dims=NN):
    return lax.dot_general(a, b, dims, preferred_element_type=f32)


def split(x):
    high = x.astype(bf16)
    return high, (x - high.astype(f32)).astype(bf16)


def prepare_kernel(cols, alive_ref, spot_ref, level_ref, prec_ref, hist_ref, field_ref, lag_ref, mean_ref, flat_ref):
    patches, slots = spot_ref.shape
    patch_cols = cols // PATCH
    patch_rows = patches // patch_cols
    spot = spot_ref[...]
    row_in = spot // PATCH
    col_in = spot % PATCH
    slot_index = lax.broadcasted_iota(jnp.int32, (1, slots), 1)
    iota_row = lax.broadcasted_iota(jnp.int32, (PATCH, slots), 0)
    iota_col = lax.broadcasted_iota(jnp.int32, (cols, slots), 0)
    for a in range(patch_rows):
        total = jnp.zeros((4 * PATCH, cols), f32)
        for b in range(patch_cols):
            p = a * patch_cols + b
            prec = jnp.where(slot_index < alive_ref[p], prec_ref[p : p + 1, :], 0.0)
            level = prec * level_ref[p : p + 1, :]
            prec_high = prec.astype(bf16).astype(f32)
            level_high = level.astype(bf16).astype(f32)
            on_row = row_in[p : p + 1, :] == iota_row
            pieces = [
                jnp.where(on_row, piece, 0.0).astype(bf16)
                for piece in (prec_high, prec - prec_high, level_high, level - level_high)
            ]
            on_col = jnp.where(col_in[p : p + 1, :] + b * PATCH == iota_col, 1.0, 0.0).astype(bf16)
            total = total + mm(jnp.concatenate(pieces, 0), on_col, NT)
        rows = slice(a * PATCH, (a + 1) * PATCH)
        field_ref[0, rows, :] = total[:PATCH] + total[PATCH : 2 * PATCH]
        field_ref[1, rows, :] = total[2 * PATCH : 3 * PATCH] + total[3 * PATCH :]
    members, tile_rows, _ = hist_ref.shape
    state = hist_ref[...].astype(f32)
    mean = jnp.sum(state, axis=0) / members
    mean_ref[...] = mean
    flat_ref[...] = (state - mean[None]).reshape(members * tile_rows, cols)
    for r in range(tile_rows):
        lag_ref[r] = flat_ref[pl.ds(r, members, stride=tile_rows), :].astype(bf16)


def pack_kernel(shares, place_ref, *refs):
    parts, refs = refs[:shares], refs[shares:]
    field_ref, mine_ref, mine_field_ref, message_ref, flat_ref, held_ref = refs
    share_members, tile_rows, cols = parts[0].shape
    members = share_members * shares
    lag, group = place_ref[0], place_ref[1]
    states = [part[...].astype(f32) for part in parts]
    mean = functools.reduce(jnp.add, [jnp.sum(state, axis=0) for state in states]) / members
    for k, state in enumerate(states):
        at = pl.multiple_of(lax.rem(lag + k, shares) * (share_members * tile_rows), 8)
        flat_ref[pl.ds(at, share_members * tile_rows), :] = (state - mean[None]).reshape(-1, cols)
    weight = field_ref[0]
    held_ref[0] = weight
    held_ref[1] = field_ref[1] - mean * weight

    def row(r):
        return flat_ref[pl.ds(r, members, stride=tile_rows), :].astype(bf16)

    half = mine_ref.shape[0]
    first = pl.multiple_of(group * half, 8)
    for i in range(half):
        mine_ref[i] = row(first + i)
    mine_field_ref[0] = held_ref[0, pl.ds(first, half), :]
    mine_field_ref[1] = held_ref[1, pl.ds(first, half), :]
    near = pl.multiple_of((1 - group) * (tile_rows - NEAR), 8)
    far = tile_rows - FAR
    for i in range(NEAR):
        message_ref[i] = row(near + i)
    for i in range(FAR - NEAR):
        message_ref[NEAR + i] = row(far + i)
    for k in range(2):
        rows = jnp.concatenate([held_ref[k, pl.ds(near, NEAR), :], held_ref[k, far : far + FAR - NEAR, :]], 0)
        high, low = split(rows)
        rest = jnp.zeros((members - 2 * FAR, cols), bf16)
        message_ref[FAR + k] = jnp.concatenate([high, low, rest], 0)


def taper_plan(group, relative, patch_cols, cols, radius_ref):
    patch_row = group if relative == 0 else 1 - group
    q_row = lax.broadcasted_iota(jnp.int32, (patch_cols, cols), 0)
    col = lax.broadcasted_iota(jnp.int32, (patch_cols, cols), 1)
    radius = jnp.zeros((patch_cols, cols), f32)
    for q in range(patch_cols):
        radius = jnp.where(q_row == q, radius_ref[patch_row * patch_cols + q].astype(f32), radius)
    middle = (PATCH - 1) / 2
    col_square = jnp.square(col.astype(f32) - (q_row.astype(f32) * PATCH + middle))
    return patch_row.astype(f32) * PATCH + middle, col_square, 1.0 / jnp.square(radius)


def accumulate(total, plan, anomalies, weight, innovation, first_row):
    centre_row, col_square, inverse_square = plan
    patches, cols = col_square.shape
    lefts = []
    for i, anomaly in enumerate(anomalies):
        members = anomaly.shape[0]
        offset = (first_row + i).astype(f32) - centre_row
        taper = jnp.square(jnp.maximum(0.0, 1.0 - (offset * offset + col_square) * inverse_square))
        scale = taper * weight[i : i + 1]
        blocks = anomaly.reshape(members // PATCH, PATCH, cols)
        left = [
            (blocks * jnp.broadcast_to(scale[q : q + 1], (PATCH, cols)).astype(bf16)[None]).reshape(members, cols)
            for q in range(patches)
        ]
        tail = taper * innovation[i : i + 1]
        left.append(jnp.concatenate([tail, jnp.zeros((PATCH - patches, cols), f32)], 0).astype(bf16))
        lefts.append(jnp.concatenate(left, 0))
    return total + mm(jnp.concatenate(lefts, 1), jnp.concatenate(anomalies, 1), NT)


STEP = 8


def own_kernel(place_ref, radius_ref, mine_ref, field_ref, out_ref):
    half, members, cols = mine_ref.shape
    patch_cols = cols // PATCH
    group = place_ref[1]
    totals = [jnp.zeros(out_ref.shape[1:], f32) for _ in range(2)]
    plans = [taper_plan(group, relative, patch_cols, cols, radius_ref) for relative in range(2)]
    for start in range(0, half, STEP):
        rows = slice(start, start + STEP)
        anomalies = [mine_ref[i] for i in range(start, start + STEP)]
        for relative in range(2):
            totals[relative] = accumulate(
                totals[relative], plans[relative], anomalies, field_ref[0, rows, :], field_ref[1, rows, :], group * half + start
            )
    out_ref[0] = totals[0]
    out_ref[1] = totals[1]


def halo_kernel(tile_rows, place_ref, radius_ref, message_ref, own_ref, total_ref, send_ref):
    _, members, cols = message_ref.shape
    patch_cols = cols // PATCH
    group = place_ref[1]
    totals = [own_ref[0], own_ref[1]]
    plans = [taper_plan(group, relative, patch_cols, cols, radius_ref) for relative in range(2)]
    fields = []
    for k in range(2):
        rows = message_ref[FAR + k].astype(f32)
        fields.append(rows[:FAR] + rows[FAR : 2 * FAR])
    for start in range(0, FAR, STEP):
        anomalies = [message_ref[i] for i in range(start, start + STEP)]
        rows = slice(start, start + STEP)
        if start < NEAR:
            first = jnp.where(group == 0, -NEAR, tile_rows) + start
        else:
            first = jnp.where(group == 0, -FAR, tile_rows + NEAR) + start - NEAR
        for relative in range(2 if start < NEAR else 1):
            totals[relative] = accumulate(
                totals[relative], plans[relative], anomalies, fields[0][rows], fields[1][rows], first
            )
    sides = []
    pairs = patch_cols // 2
    for relative, total in enumerate(totals):
        patch_row = group if relative == 0 else 1 - group
        grams, side = [], []
        for pair in range(pairs):
            at = 2 * pair * members
            grams.append(jnp.concatenate([total[at : at + members], total[at + members : at + 2 * members]], 1))
            at = patch_cols * members + 2 * pair
            side.append(jnp.concatenate([total[at : at + 1], total[at + 1 : at + 2]], 1))
        sides.append(jnp.concatenate(side, 0))
        gram = jnp.concatenate(grams, 0)
        rows = pl.ds(pl.multiple_of(patch_row * (pairs * members), 16), pairs * members)
        total_ref[rows, :] = gram
        send_ref[rows, :] = gram.astype(bf16)
    side = jnp.concatenate(
        [jnp.where(group == 0, sides[0], sides[1]), jnp.where(group == 0, sides[1], sides[0])], 0
    )
    at = 2 * pairs * members
    total_ref[at:, :] = side
    send_ref[at:, :] = jnp.concatenate(split(side), 0)


def finish_kernel(total_ref, other_ref, lag_ref, mean_ref, out_ref, flat_ref):
    tile_rows, members, cols = lag_ref.shape
    degree = members - 1.0
    pair_count = total_ref.shape[0] // members
    grams_end = pair_count * members
    row = lax.broadcasted_iota(jnp.int32, (members, 2 * members), 0)
    lane = lax.broadcasted_iota(jnp.int32, (members, 2 * members), 1)
    identity = jnp.where(row == lane % members, 1.0, 0.0)
    left_mask = jnp.where(lane < members, 1.0, 0.0).astype(bf16)
    right_mask = jnp.where(lane < members, 0.0, 1.0).astype(bf16)

    def blocks(y):
        return jnp.concatenate([y * left_mask, y * right_mask], 0)

    def right(y):
        high, low = split(y)
        return blocks(high), blocks(low)

    def product(lefts, factor):
        high, low = factor
        rows = lefts[0][0].shape[0]
        first = mm(jnp.concatenate([part for pair in lefts for part in pair], 0), high)
        second = mm(jnp.concatenate([pair[0] for pair in lefts], 0), low)
        return [
            first[2 * k * rows : (2 * k + 1) * rows]
            + (first[(2 * k + 1) * rows : (2 * k + 2) * rows] + second[k * rows : (k + 1) * rows])
            for k in range(len(lefts))
        ]

    pairs = range(pair_count)
    grams = [
        total_ref[p * members : (p + 1) * members, :] + other_ref[p * members : (p + 1) * members, :].astype(f32)
        for p in pairs
    ]
    ends = [other_ref[grams_end + k * pair_count : grams_end + (k + 1) * pair_count, :].astype(f32) for k in range(2)]
    sides = total_ref[grams_end:, :] + (ends[0] + ends[1])
    squares = jnp.concatenate([jnp.sum(gram * gram, axis=0, keepdims=True) for gram in grams], 0)
    at_left = lax.broadcasted_iota(jnp.int32, squares.shape, 1) < members
    norm_left = jnp.sum(jnp.where(at_left, squares, 0.0), axis=1, keepdims=True)
    norm_right = jnp.sum(jnp.where(at_left, 0.0, squares), axis=1, keepdims=True)
    bound = degree + jnp.sqrt(jnp.where(at_left, norm_left, norm_right))
    spread = jnp.sqrt(degree / bound)
    iterates = [(grams[p] + degree * identity) / bound[p : p + 1] for p in pairs]
    corrections = [1.5 * identity - 0.5 * iterates[p] for p in pairs]
    factors = [right(corrections[p]) for p in pairs]
    iterates = [product([split(iterates[p])], factors[p])[0] for p in pairs]
    roots = corrections
    for step in range(1, NS_STEPS):
        halves = [split(roots[p]) for p in pairs]
        corrections = [1.5 * identity - 0.5 * product([halves[p]], right(iterates[p]))[0] for p in pairs]
        factors = [right(corrections[p]) for p in pairs]
        if step < NS_STEPS - 1:
            both = [product([split(iterates[p]), halves[p]], factors[p]) for p in pairs]
            iterates = [pair[0] for pair in both]
            roots = [pair[1] for pair in both]
        else:
            roots = [product([halves[p]], factors[p])[0] for p in pairs]
    mixings = []
    for p in pairs:
        factor = right(roots[p])
        side = jnp.broadcast_to(sides[p : p + 1], (PATCH, cols))
        inner = product([split(side)], factor)[0]
        weights = product([split(inner)], factor)[0][:1] / bound[p : p + 1]
        mixings.append((spread[p : p + 1] * roots[p] + weights).astype(bf16))

    patch = lax.broadcasted_iota(jnp.int32, (members, cols), 1) // PATCH
    even = jnp.where(patch % 2 == 0, 1.0, 0.0).astype(bf16)
    odd = jnp.where(patch % 2 == 1, 1.0, 0.0).astype(bf16)
    per_row = cols // (2 * PATCH)
    for a in range(tile_rows // PATCH):
        mixing = jnp.concatenate(mixings[a * per_row : (a + 1) * per_row], 0)
        for r in range(a * PATCH, (a + 1) * PATCH, 2):
            state = jnp.concatenate(
                [jnp.concatenate([lag_ref[i] * even, lag_ref[i] * odd], 0) for i in (r, r + 1)], 1
            )
            spread_out = mm(mixing, state)
            for i in (0, 1):
                part = spread_out[:, i * cols : (i + 1) * cols]
                chosen = part[:members]
                for pair in range(1, per_row):
                    chosen = jnp.where(patch // 2 == pair, part[pair * members : (pair + 1) * members], chosen)
                flat_ref[pl.ds(r + i, members, stride=tile_rows), :] = chosen + mean_ref[r + i : r + i + 1, :]
    out_ref[...] = flat_ref[...].reshape(1, members, tile_rows, cols).astype(bf16)


def shards(history, forecast, spot, alive, levels, precision, radius):
    shares = lax.axis_size("lag")
    tiles = lax.axis_size("dom")
    lag = lax.axis_index("lag")
    share_members, tile_rows, cols = forecast.shape
    members = share_members * shares
    patch_cols = cols // PATCH
    half = tile_rows // 2
    per_group = shares // 2
    place = jnp.stack([lag, lag // per_group])
    forward = [(t * shares, (t + 1) * shares) for t in range(tiles - 1)]
    halo_pairs = [(s + l, t + l) for s, t in forward for l in range(per_group)]
    halo_pairs += [(t + l, s + l) for s, t in forward for l in range(per_group, shares)]

    def call(kernel, name, in_specs, out_shape, scratch=()):
        return pl.pallas_call(
            kernel,
            in_specs=in_specs,
            out_specs=jax.tree.map(lambda _: vmem, out_shape),
            out_shape=out_shape,
            scratch_shapes=scratch,
            compiler_params=pltpu.CompilerParams(vmem_limit_bytes=32 * 2**20),
            name=name,
        )

    shape = jax.ShapeDtypeStruct
    smem = pl.BlockSpec(memory_space=pltpu.SMEM)
    vmem = pl.BlockSpec(memory_space=pltpu.VMEM)
    parts = [forecast]
    for k in range(1, shares):
        parts.append(lax.ppermute(forecast, "lag", [((i + k) % shares, i) for i in range(shares)]))
    fields, lag_rows, lag_mean = call(
        functools.partial(prepare_kernel, cols),
        "prepare",
        [smem, vmem, vmem, vmem, vmem],
        [
            shape((2, tile_rows, cols), f32),
            shape((tile_rows, members, cols), bf16),
            shape((tile_rows, cols), f32),
        ],
        [pltpu.VMEM((members * tile_rows, cols), f32)],
    )(alive, spot, levels, precision, history[0])
    mine, mine_field, message = call(
        functools.partial(pack_kernel, shares),
        "pack",
        [smem] + [vmem] * (shares + 1),
        [
            shape((half, members, cols), bf16),
            shape((2, half, cols), f32),
            shape((FAR + 2, members, cols), bf16),
        ],
        [pltpu.VMEM((members * tile_rows, cols), f32), pltpu.VMEM((2, tile_rows, cols), f32)],
    )(place, *parts, fields)
    message = lax.ppermute(message, ("dom", "lag"), halo_pairs)
    own = call(
        own_kernel,
        "own_gram",
        [smem, smem, vmem, vmem],
        shape((2, patch_cols * members + PATCH, members), f32),
    )(place, radius, mine, mine_field)
    pair_rows = patch_cols * members
    total, send = call(
        functools.partial(halo_kernel, tile_rows),
        "halo_gram",
        [smem, smem, vmem, vmem],
        [
            shape((pair_rows + patch_cols, 2 * members), f32),
            shape((pair_rows + 2 * patch_cols, 2 * members), bf16),
        ],
    )(place, radius, message, own)
    other = lax.ppermute(send, "lag", [(i, (i + per_group) % shares) for i in range(shares)])
    return call(
        finish_kernel,
        "finish",
        [vmem] * 4,
        shape((1, members, tile_rows, cols), bf16),
        [pltpu.VMEM((members * tile_rows, cols), f32)],
    )(total, other, lag_rows, lag_mean)


def solution(mesh):
    in_specs = (
        P("lag", None, "dom", None),
        P("lag", "dom", None),
        P("dom", None),
        P("dom"),
        P("dom", None),
        P("dom", None),
        P("dom"),
    )
    out_specs = P("lag", None, "dom", None)
    return jax.shard_map(shards, mesh=mesh, in_specs=in_specs, out_specs=out_specs, check_vma=False)
```

```python
import functools

import jax
import jax.numpy as jnp
from jax import lax
from jax.experimental import pallas as pl
from jax.experimental.pallas import tpu as pltpu
from jax.sharding import PartitionSpec as P

PATCH = 16
NS_STEPS = 4
RADIUS = 32
FAR = RADIUS - PATCH // 2
NEAR = FAR - PATCH
MIDDLE = (PATCH - 1) / 2

NT = (((1,), (1,)), ((), ()))
NN = (((1,), (0,)), ((), ()))
f32 = jnp.float32
bf16 = jnp.bfloat16


def mm(a, b, dims=NN):
    return lax.dot_general(a, b, dims, preferred_element_type=f32)


def split(x):
    high = x.astype(bf16)
    return high, (x - high.astype(f32)).astype(bf16)


def fields_kernel(cols, alive_hbm, spot_hbm, level_hbm, prec_hbm, field_ref, alive_ref, spot_ref, level_ref, prec_ref, sem):
    copies = [
        pltpu.make_async_copy(source, target, sem.at[k])
        for k, (source, target) in enumerate(
            ((alive_hbm, alive_ref), (spot_hbm, spot_ref), (level_hbm, level_ref), (prec_hbm, prec_ref))
        )
    ]
    for copy in copies:
        copy.start()
    for copy in copies:
        copy.wait()
    patches, slots = spot_ref.shape
    patch_cols = cols // PATCH
    patch_rows = patches // patch_cols
    spot = spot_ref[...]
    row_in = spot // PATCH
    col_in = spot % PATCH
    slot_index = lax.broadcasted_iota(jnp.int32, (1, slots), 1)
    iota_row = lax.broadcasted_iota(jnp.int32, (PATCH, slots), 0)
    iota_col = lax.broadcasted_iota(jnp.int32, (cols, slots), 0)
    for a in range(patch_rows):
        total = jnp.zeros((4 * PATCH, cols), f32)
        for b in range(patch_cols):
            p = a * patch_cols + b
            prec = jnp.where(slot_index < alive_ref[p], prec_ref[p : p + 1, :], 0.0)
            level = prec * level_ref[p : p + 1, :]
            prec_high = prec.astype(bf16).astype(f32)
            level_high = level.astype(bf16).astype(f32)
            on_row = row_in[p : p + 1, :] == iota_row
            pieces = [
                jnp.where(on_row, piece, 0.0).astype(bf16)
                for piece in (prec_high, prec - prec_high, level_high, level - level_high)
            ]
            on_col = jnp.where(col_in[p : p + 1, :] + b * PATCH == iota_col, 1.0, 0.0).astype(bf16)
            total = total + mm(jnp.concatenate(pieces, 0), on_col, NT)
        rows = slice(a * PATCH, (a + 1) * PATCH)
        field_ref[0, rows, :] = total[:PATCH] + total[PATCH : 2 * PATCH]
        field_ref[1, rows, :] = total[2 * PATCH : 3 * PATCH] + total[3 * PATCH :]


def state_kernel(after_ref, hist_hbm, lag_ref, mean_ref, hist_ref, flat_ref, sem):
    copy = pltpu.make_async_copy(hist_hbm, hist_ref, sem)
    copy.start()
    copy.wait()
    members, tile_rows, cols = hist_ref.shape
    state = hist_ref[...].astype(f32)
    mean = jnp.sum(state, axis=0) / members
    mean_ref[...] = mean
    flat_ref[...] = (state - mean[None]).reshape(members * tile_rows, cols)
    for r in range(tile_rows):
        lag_ref[r] = flat_ref[pl.ds(r, members, stride=tile_rows), :].astype(bf16)


def taper_plan(centre_row, first_patch, patch_cols, cols, radius_ref):
    q_row = lax.broadcasted_iota(jnp.int32, (patch_cols, cols), 0)
    col = lax.broadcasted_iota(jnp.int32, (patch_cols, cols), 1)
    radius = jnp.zeros((patch_cols, cols), f32)
    for q in range(patch_cols):
        radius = jnp.where(q_row == q, radius_ref[first_patch + q].astype(f32), radius)
    col_square = jnp.square(col.astype(f32) - (q_row.astype(f32) * PATCH + MIDDLE))
    return centre_row, col_square, 1.0 / jnp.square(radius)


def accumulate(total, plan, anomalies, weight, innovation, first_row):
    centre_row, col_square, inverse_square = plan
    patches, cols = col_square.shape
    lefts = []
    for i, anomaly in enumerate(anomalies):
        members = anomaly.shape[0]
        offset = (first_row + i).astype(f32) - centre_row
        taper = jnp.square(jnp.maximum(0.0, 1.0 - (offset * offset + col_square) * inverse_square))
        scale = taper * weight[i : i + 1]
        blocks = anomaly.reshape(members // PATCH, PATCH, cols)
        left = [
            (blocks * jnp.broadcast_to(scale[q : q + 1], (PATCH, cols)).astype(bf16)[None]).reshape(members, cols)
            for q in range(patches)
        ]
        tail = taper * innovation[i : i + 1]
        left.append(jnp.concatenate([tail, jnp.zeros((PATCH - patches, cols), f32)], 0).astype(bf16))
        lefts.append(jnp.concatenate(left, 0))
    return total + mm(jnp.concatenate(lefts, 1), jnp.concatenate(anomalies, 1), NT)


STEP = 8


def paired(totals, members, patch_cols):
    pairs = patch_cols // 2
    grams, sides = [], []
    for total in totals:
        for pair in range(pairs):
            at = 2 * pair * members
            grams.append(jnp.concatenate([total[at : at + members], total[at + members : at + 2 * members]], 1))
        for pair in range(pairs):
            at = patch_cols * members + 2 * pair
            sides.append(jnp.concatenate([total[at : at + 1], total[at + 1 : at + 2]], 1))
    return jnp.concatenate(grams, 0), jnp.concatenate(sides, 0)


def message_of(grams, sides):
    return jnp.concatenate([grams.astype(bf16), *split(sides)], 0)


def read_message(ref, side_count):
    at = ref.shape[0] - 2 * side_count
    high, low = ref[at : at + side_count, :].astype(f32), ref[at + side_count :, :].astype(f32)
    return jnp.concatenate([ref[:at, :].astype(f32), high + low], 0)


def outward_kernel(shares, place_ref, radius_ref, *refs):
    parts, refs = refs[:shares], refs[shares:]
    field_ref, near_ref, far_ref, held_ref, message_ref, flat_ref, total_ref = refs
    share_members, tile_rows, cols = parts[0].shape
    members = share_members * shares
    patch_cols = cols // PATCH
    lag, group = place_ref[0], place_ref[1]
    states = [part[...].astype(f32) for part in parts]
    mean = functools.reduce(jnp.add, [jnp.sum(state, axis=0) for state in states]) / members
    for k, state in enumerate(states):
        at = pl.multiple_of(lax.rem(lag + k, shares) * (share_members * tile_rows), 8)
        flat_ref[pl.ds(at, share_members * tile_rows), :] = (state - mean[None]).reshape(-1, cols)
    weight = field_ref[0]
    held_ref[0] = weight
    held_ref[1] = field_ref[1] - mean * weight

    def row(r):
        return flat_ref[pl.ds(r, members, stride=tile_rows), :].astype(bf16)

    near = pl.multiple_of(group * (tile_rows - NEAR), 8)
    sign = 1 - 2 * group
    middle = jnp.where(group == 0, MIDDLE - PATCH, MIDDLE + tile_rows)
    first_near = (1 - group) * patch_cols
    plans = [
        taper_plan(middle, first_near, patch_cols, cols, radius_ref),
        taper_plan(middle - (sign * PATCH).astype(f32), patch_cols - first_near, patch_cols, cols, radius_ref),
    ]
    anomalies = [row(near + i) for i in range(NEAR)]
    for i, anomaly in enumerate(anomalies):
        near_ref[i] = anomaly
    weights, innovations = (held_ref[k, pl.ds(near, NEAR), :] for k in range(2))
    blank = jnp.zeros(total_ref.shape[1:], f32)
    totals = [accumulate(blank, plan, anomalies, weights, innovations, near) for plan in plans]
    for start in range(NEAR, FAR, STEP):
        anomalies = [row(start + i) for i in range(STEP)]
        for i, anomaly in enumerate(anomalies):
            far_ref[start - NEAR + i] = anomaly
        rows = slice(start, start + STEP)
        totals[0] = accumulate(totals[0], plans[0], anomalies, held_ref[0, rows, :], held_ref[1, rows, :], jnp.int32(start))
    total_ref[1 - group] = totals[0]
    total_ref[group] = totals[1]
    message_ref[...] = message_of(*paired([total_ref[0], total_ref[1]], members, patch_cols))


def own_kernel(place_ref, radius_ref, near_ref, far_ref, field_ref, out_ref):
    members, cols = near_ref.shape[1:]
    tile_rows = field_ref.shape[1]
    patch_cols = cols // PATCH
    group = place_ref[1]
    plans = [
        taper_plan(MIDDLE + a * PATCH, a * patch_cols, patch_cols, cols, radius_ref) for a in range(tile_rows // PATCH)
    ]
    near = pl.multiple_of(group * (tile_rows - NEAR), 8)
    far = pl.multiple_of(NEAR + group * (FAR - 2 * NEAR), 8)
    totals = [jnp.zeros((patch_cols * members + PATCH, members), f32) for _ in plans]
    for first, anomalies in (
        (near, [near_ref[i] for i in range(NEAR)]),
        (far, [far_ref[far - NEAR + i] for i in range(tile_rows // 2 - NEAR)]),
    ):
        fields = [field_ref[k, pl.ds(first, len(anomalies)), :] for k in range(2)]
        totals = [accumulate(total, plan, anomalies, *fields, first) for total, plan in zip(totals, plans)]
    out_ref[...] = jnp.concatenate(paired(totals, members, patch_cols), 0)


def join_kernel(own_ref, message_ref, total_ref, send_ref):
    sides = message_ref.shape[0] - own_ref.shape[0]
    total = own_ref[...] + read_message(message_ref, sides)
    total_ref[...] = total
    send_ref[...] = message_of(total[: total.shape[0] - sides], total[total.shape[0] - sides :])


def finish_kernel(total_ref, other_ref, lag_ref, mean_ref, out_ref, flat_ref):
    tile_rows, members, cols = lag_ref.shape
    degree = members - 1.0
    pair_count = total_ref.shape[0] // members
    grams_end = pair_count * members
    row = lax.broadcasted_iota(jnp.int32, (members, 2 * members), 0)
    lane = lax.broadcasted_iota(jnp.int32, (members, 2 * members), 1)
    identity = jnp.where(row == lane % members, 1.0, 0.0)
    left_mask = jnp.where(lane < members, 1.0, 0.0).astype(bf16)
    right_mask = jnp.where(lane < members, 0.0, 1.0).astype(bf16)

    def blocks(y):
        return jnp.concatenate([y * left_mask, y * right_mask], 0)

    def right(y):
        high, low = split(y)
        return blocks(high), blocks(low)

    def product(lefts, factor):
        high, low = factor
        rows = lefts[0][0].shape[0]
        first = mm(jnp.concatenate([part for pair in lefts for part in pair], 0), high)
        second = mm(jnp.concatenate([pair[0] for pair in lefts], 0), low)
        return [
            first[2 * k * rows : (2 * k + 1) * rows]
            + (first[(2 * k + 1) * rows : (2 * k + 2) * rows] + second[k * rows : (k + 1) * rows])
            for k in range(len(lefts))
        ]

    pairs = range(pair_count)
    total = total_ref[...] + read_message(other_ref, pair_count)
    grams = [total[p * members : (p + 1) * members] for p in pairs]
    sides = total[grams_end:]
    squares = jnp.concatenate([jnp.sum(gram * gram, axis=0, keepdims=True) for gram in grams], 0)
    at_left = lax.broadcasted_iota(jnp.int32, squares.shape, 1) < members
    norm_left = jnp.sum(jnp.where(at_left, squares, 0.0), axis=1, keepdims=True)
    norm_right = jnp.sum(jnp.where(at_left, 0.0, squares), axis=1, keepdims=True)
    bound = degree + jnp.sqrt(jnp.where(at_left, norm_left, norm_right))
    spread = jnp.sqrt(degree / bound)
    iterates = [(grams[p] + degree * identity) / bound[p : p + 1] for p in pairs]
    corrections = [1.5 * identity - 0.5 * iterates[p] for p in pairs]
    factors = [right(corrections[p]) for p in pairs]
    iterates = [product([split(iterates[p])], factors[p])[0] for p in pairs]
    roots = corrections
    for step in range(1, NS_STEPS):
        halves = [split(roots[p]) for p in pairs]
        corrections = [1.5 * identity - 0.5 * product([halves[p]], right(iterates[p]))[0] for p in pairs]
        factors = [right(corrections[p]) for p in pairs]
        if step < NS_STEPS - 1:
            both = [product([split(iterates[p]), halves[p]], factors[p]) for p in pairs]
            iterates = [pair[0] for pair in both]
            roots = [pair[1] for pair in both]
        else:
            roots = [product([halves[p]], factors[p])[0] for p in pairs]
    mixings = []
    for p in pairs:
        factor = right(roots[p])
        side = jnp.broadcast_to(sides[p : p + 1], (PATCH, cols))
        inner = product([split(side)], factor)[0]
        weights = product([split(inner)], factor)[0][:1] / bound[p : p + 1]
        mixings.append((spread[p : p + 1] * roots[p] + weights).astype(bf16))

    patch = lax.broadcasted_iota(jnp.int32, (members, cols), 1) // PATCH
    even = jnp.where(patch % 2 == 0, 1.0, 0.0).astype(bf16)
    odd = jnp.where(patch % 2 == 1, 1.0, 0.0).astype(bf16)
    per_row = cols // (2 * PATCH)
    for a in range(tile_rows // PATCH):
        mixing = jnp.concatenate(mixings[a * per_row : (a + 1) * per_row], 0)
        for r in range(a * PATCH, (a + 1) * PATCH, 2):
            state = jnp.concatenate(
                [jnp.concatenate([lag_ref[i] * even, lag_ref[i] * odd], 0) for i in (r, r + 1)], 1
            )
            spread_out = mm(mixing, state)
            for i in (0, 1):
                part = spread_out[:, i * cols : (i + 1) * cols]
                chosen = part[:members]
                for pair in range(1, per_row):
                    chosen = jnp.where(patch // 2 == pair, part[pair * members : (pair + 1) * members], chosen)
                flat_ref[pl.ds(r + i, members, stride=tile_rows), :] = chosen + mean_ref[r + i : r + i + 1, :]
    out_ref[...] = flat_ref[...].reshape(1, members, tile_rows, cols).astype(bf16)


def shards(history, forecast, spot, alive, levels, precision, radius):
    shares = lax.axis_size("lag")
    tiles = lax.axis_size("dom")
    lag = lax.axis_index("lag")
    share_members, tile_rows, cols = forecast.shape
    members = share_members * shares
    patch_cols = cols // PATCH
    per_group = shares // 2
    place = jnp.stack([lag, lag // per_group])
    forward = [(t * shares, (t + 1) * shares) for t in range(tiles - 1)]
    halo_pairs = [(t + l, s + l) for s, t in forward for l in range(per_group)]
    halo_pairs += [(s + l, t + l) for s, t in forward for l in range(per_group, shares)]

    def call(kernel, name, in_specs, out_shape, scratch=()):
        return pl.pallas_call(
            kernel,
            in_specs=in_specs,
            out_specs=jax.tree.map(lambda _: vmem, out_shape),
            out_shape=out_shape,
            scratch_shapes=scratch,
            compiler_params=pltpu.CompilerParams(vmem_limit_bytes=32 * 2**20),
            name=name,
        )

    shape = jax.ShapeDtypeStruct
    smem = pl.BlockSpec(memory_space=pltpu.SMEM)
    vmem = pl.BlockSpec(memory_space=pltpu.VMEM)
    hbm = pl.BlockSpec(memory_space=pltpu.HBM)
    parts = [forecast]
    for k in range(1, shares):
        parts.append(lax.ppermute(forecast, "lag", [((i + k) % shares, i) for i in range(shares)]))
    next_radius = lax.ppermute(radius, ("dom", "lag"), [(s, t) for t, s in halo_pairs])
    fields = call(
        functools.partial(fields_kernel, cols),
        "fields",
        [hbm] * 4,
        shape((2, tile_rows, cols), f32),
        [
            pltpu.SMEM(alive.shape, jnp.int32),
            pltpu.VMEM(spot.shape, jnp.int32),
            pltpu.VMEM(levels.shape, f32),
            pltpu.VMEM(precision.shape, f32),
            pltpu.SemaphoreType.DMA((4,)),
        ],
    )(alive, spot, levels, precision)
    pair_rows = patch_cols * members
    near, far, held, message = call(
        functools.partial(outward_kernel, shares),
        "outward_gram",
        [smem, smem] + [vmem] * (shares + 1),
        [
            shape((NEAR, members, cols), bf16),
            shape((FAR - NEAR, members, cols), bf16),
            shape((2, tile_rows, cols), f32),
            shape((pair_rows + 2 * patch_cols, 2 * members), bf16),
        ],
        [
            pltpu.VMEM((members * tile_rows, cols), f32),
            pltpu.VMEM((2, patch_cols * members + PATCH, members), f32),
        ],
    )(place, next_radius, *parts, fields)
    message = lax.ppermute(message, ("dom", "lag"), halo_pairs)
    own = call(
        own_kernel,
        "own_gram",
        [smem, smem] + [vmem] * 3,
        shape((pair_rows + patch_cols, 2 * members), f32),
    )(place, radius, near, far, held)
    lag_rows, lag_mean = call(
        state_kernel,
        "state",
        [hbm, hbm],
        [shape((tile_rows, members, cols), bf16), shape((tile_rows, cols), f32)],
        [
            pltpu.VMEM((members, tile_rows, cols), bf16),
            pltpu.VMEM((members * tile_rows, cols), f32),
            pltpu.SemaphoreType.DMA,
        ],
    )(held, history[0])
    total, send = call(
        join_kernel,
        "join",
        [vmem, vmem],
        [
            shape((pair_rows + patch_cols, 2 * members), f32),
            shape((pair_rows + 2 * patch_cols, 2 * members), bf16),
        ],
    )(own, message)
    other = lax.ppermute(send, "lag", [(i, (i + per_group) % shares) for i in range(shares)])
    return call(
        finish_kernel,
        "finish",
        [vmem] * 4,
        shape((1, members, tile_rows, cols), bf16),
        [pltpu.VMEM((members * tile_rows, cols), f32)],
    )(total, other, lag_rows, lag_mean)


def solution(mesh):
    in_specs = (
        P("lag", None, "dom", None),
        P("lag", "dom", None),
        P("dom", None),
        P("dom"),
        P("dom", None),
        P("dom", None),
        P("dom"),
    )
    out_specs = P("lag", None, "dom", None)
    return jax.shard_map(shards, mesh=mesh, in_specs=in_specs, out_specs=out_specs, check_vma=False)
```

```python
import functools

import jax
import jax.numpy as jnp
from jax import lax
from jax.experimental import pallas as pl
from jax.experimental.pallas import tpu as pltpu
from jax.sharding import PartitionSpec as P

PATCH = 16
NS_STEPS = 4
RADIUS = 32
FAR = RADIUS - PATCH // 2
NEAR = FAR - PATCH
MIDDLE = (PATCH - 1) / 2

NT = (((1,), (1,)), ((), ()))
NN = (((1,), (0,)), ((), ()))
f32 = jnp.float32
bf16 = jnp.bfloat16


def mm(a, b, dims=NN):
    return lax.dot_general(a, b, dims, preferred_element_type=f32)


def split(x):
    high = x.astype(bf16)
    return high, (x - high.astype(f32)).astype(bf16)


def fields_kernel(cols, table_ref, part_ref, field_ref, sum_ref):
    sum_ref[...] = jnp.sum(part_ref[...].astype(f32), axis=0)
    patches, slots = table_ref.shape[1:]
    patch_cols = cols // PATCH
    patch_rows = patches // patch_cols
    spot = table_ref[2].astype(jnp.int32)
    row_in = spot // PATCH
    col_in = spot % PATCH
    iota_row = lax.broadcasted_iota(jnp.int32, (PATCH, slots), 0)
    iota_col = lax.broadcasted_iota(jnp.int32, (cols, slots), 0)
    for a in range(patch_rows):
        total = jnp.zeros((4 * PATCH, cols), f32)
        for b in range(patch_cols):
            p = a * patch_cols + b
            prec = table_ref[0, p : p + 1, :]
            level = table_ref[1, p : p + 1, :]
            prec_high = prec.astype(bf16).astype(f32)
            level_high = level.astype(bf16).astype(f32)
            on_row = row_in[p : p + 1, :] == iota_row
            pieces = [
                jnp.where(on_row, piece, 0.0).astype(bf16)
                for piece in (prec_high, prec - prec_high, level_high, level - level_high)
            ]
            on_col = jnp.where(col_in[p : p + 1, :] + b * PATCH == iota_col, 1.0, 0.0).astype(bf16)
            total = total + mm(jnp.concatenate(pieces, 0), on_col, NT)
        rows = slice(a * PATCH, (a + 1) * PATCH)
        field_ref[0, rows, :] = total[:PATCH] + total[PATCH : 2 * PATCH]
        field_ref[1, rows, :] = total[2 * PATCH : 3 * PATCH] + total[3 * PATCH :]


def state_kernel(after_ref, hist_hbm, lag_ref, mean_ref, hist_ref, flat_ref, sem):
    copy = pltpu.make_async_copy(hist_hbm, hist_ref, sem)
    copy.start()
    copy.wait()
    members, tile_rows, cols = hist_ref.shape
    state = hist_ref[...].astype(f32)
    mean = jnp.sum(state, axis=0) / members
    mean_ref[...] = mean
    flat_ref[...] = (state - mean[None]).reshape(members * tile_rows, cols)
    for r in range(tile_rows):
        lag_ref[r] = flat_ref[pl.ds(r, members, stride=tile_rows), :].astype(bf16)


def taper_plan(centre_row, first_patch, patch_cols, cols, place_ref):
    q_row = lax.broadcasted_iota(jnp.int32, (patch_cols, cols), 0)
    col = lax.broadcasted_iota(jnp.int32, (patch_cols, cols), 1)
    radius = jnp.zeros((patch_cols, cols), f32)
    for q in range(patch_cols):
        radius = jnp.where(q_row == q, place_ref[2 + first_patch + q].astype(f32), radius)
    col_square = jnp.square(col.astype(f32) - (q_row.astype(f32) * PATCH + MIDDLE))
    return centre_row, col_square, 1.0 / jnp.square(radius)


def accumulate(total, plan, anomalies, weight, innovation, first_row):
    centre_row, col_square, inverse_square = plan
    patches, cols = col_square.shape
    lefts = []
    for i, anomaly in enumerate(anomalies):
        members = anomaly.shape[0]
        offset = (first_row + i).astype(f32) - centre_row
        taper = jnp.square(jnp.maximum(0.0, 1.0 - (offset * offset + col_square) * inverse_square))
        scale = taper * weight[i : i + 1]
        blocks = anomaly.reshape(members // PATCH, PATCH, cols)
        left = [
            (blocks * jnp.broadcast_to(scale[q : q + 1], (PATCH, cols)).astype(bf16)[None]).reshape(members, cols)
            for q in range(patches)
        ]
        tail = taper * innovation[i : i + 1]
        left.append(jnp.concatenate([tail, jnp.zeros((PATCH - patches, cols), f32)], 0).astype(bf16))
        lefts.append(jnp.concatenate(left, 0))
    return total + mm(jnp.concatenate(lefts, 1), jnp.concatenate(anomalies, 1), NT)


STEP = 8


def paired(totals, members, patch_cols):
    pairs = patch_cols // 2
    grams, sides = [], []
    for total in totals:
        for pair in range(pairs):
            at = 2 * pair * members
            grams.append(jnp.concatenate([total[at : at + members], total[at + members : at + 2 * members]], 1))
        for pair in range(pairs):
            at = patch_cols * members + 2 * pair
            sides.append(jnp.concatenate([total[at : at + 1], total[at + 1 : at + 2]], 1))
    return jnp.concatenate(grams, 0), jnp.concatenate(sides, 0)


def message_of(grams, sides):
    return jnp.concatenate([grams.astype(bf16), *split(sides)], 0)


def read_message(ref, side_count):
    at = ref.shape[0] - 2 * side_count
    high, low = ref[at : at + side_count, :].astype(f32), ref[at + side_count :, :].astype(f32)
    return jnp.concatenate([ref[:at, :].astype(f32), high + low], 0)


def outward_kernel(shares, place_ref, *refs):
    parts, refs = refs[:shares], refs[shares:]
    sum_ref, field_ref, near_ref, far_ref, held_ref, message_ref, flat_ref, total_ref = refs
    share_members, tile_rows, cols = parts[0].shape
    members = share_members * shares
    patch_cols = cols // PATCH
    lag, group = place_ref[0], place_ref[1]
    states = [part[...].astype(f32) for part in parts]
    mean = functools.reduce(jnp.add, [jnp.sum(state, axis=0) for state in states[1:]], sum_ref[...]) / members
    for k, state in enumerate(states):
        at = pl.multiple_of(lax.rem(lag + k, shares) * (share_members * tile_rows), 8)
        flat_ref[pl.ds(at, share_members * tile_rows), :] = (state - mean[None]).reshape(-1, cols)
    weight = field_ref[0]
    held_ref[0] = weight
    held_ref[1] = field_ref[1] - mean * weight

    def row(r):
        return flat_ref[pl.ds(r, members, stride=tile_rows), :].astype(bf16)

    near = pl.multiple_of(group * (tile_rows - NEAR), 8)
    sign = 1 - 2 * group
    middle = jnp.where(group == 0, MIDDLE - PATCH, MIDDLE + tile_rows)
    first_near = (1 - group) * patch_cols
    next_patches = (tile_rows // PATCH) * patch_cols
    plans = [
        taper_plan(middle, next_patches + first_near, patch_cols, cols, place_ref),
        taper_plan(middle - (sign * PATCH).astype(f32), next_patches + patch_cols - first_near, patch_cols, cols, place_ref),
    ]
    anomalies = [row(near + i) for i in range(NEAR)]
    for i, anomaly in enumerate(anomalies):
        near_ref[i] = anomaly
    weights, innovations = (held_ref[k, pl.ds(near, NEAR), :] for k in range(2))
    blank = jnp.zeros(total_ref.shape[1:], f32)
    totals = [accumulate(blank, plan, anomalies, weights, innovations, near) for plan in plans]
    for start in range(NEAR, FAR, STEP):
        anomalies = [row(start + i) for i in range(STEP)]
        for i, anomaly in enumerate(anomalies):
            far_ref[start - NEAR + i] = anomaly
        rows = slice(start, start + STEP)
        totals[0] = accumulate(totals[0], plans[0], anomalies, held_ref[0, rows, :], held_ref[1, rows, :], jnp.int32(start))
    total_ref[1 - group] = totals[0]
    total_ref[group] = totals[1]
    message_ref[...] = message_of(*paired([total_ref[0], total_ref[1]], members, patch_cols))


def own_kernel(place_ref, near_ref, far_ref, field_ref, out_ref):
    members, cols = near_ref.shape[1:]
    tile_rows = field_ref.shape[1]
    patch_cols = cols // PATCH
    group = place_ref[1]
    plans = [
        taper_plan(MIDDLE + a * PATCH, a * patch_cols, patch_cols, cols, place_ref) for a in range(tile_rows // PATCH)
    ]
    near = pl.multiple_of(group * (tile_rows - NEAR), 8)
    far = pl.multiple_of(NEAR + group * (FAR - 2 * NEAR), 8)
    totals = [jnp.zeros((patch_cols * members + PATCH, members), f32) for _ in plans]
    for first, anomalies in (
        (near, [near_ref[i] for i in range(NEAR)]),
        (far, [far_ref[far - NEAR + i] for i in range(tile_rows // 2 - NEAR)]),
    ):
        fields = [field_ref[k, pl.ds(first, len(anomalies)), :] for k in range(2)]
        totals = [accumulate(total, plan, anomalies, *fields, first) for total, plan in zip(totals, plans)]
    out_ref[...] = jnp.concatenate(paired(totals, members, patch_cols), 0)


def join_kernel(own_ref, message_ref, total_ref, send_ref):
    sides = message_ref.shape[0] - own_ref.shape[0]
    total = own_ref[...] + read_message(message_ref, sides)
    total_ref[...] = total
    send_ref[...] = message_of(total[: total.shape[0] - sides], total[total.shape[0] - sides :])


def finish_kernel(total_ref, other_ref, lag_ref, mean_ref, out_ref, flat_ref):
    tile_rows, members, cols = lag_ref.shape
    degree = members - 1.0
    pair_count = total_ref.shape[0] // members
    grams_end = pair_count * members
    row = lax.broadcasted_iota(jnp.int32, (members, 2 * members), 0)
    lane = lax.broadcasted_iota(jnp.int32, (members, 2 * members), 1)
    identity = jnp.where(row == lane % members, 1.0, 0.0)
    left_mask = jnp.where(lane < members, 1.0, 0.0).astype(bf16)
    right_mask = jnp.where(lane < members, 0.0, 1.0).astype(bf16)

    def blocks(y):
        return jnp.concatenate([y * left_mask, y * right_mask], 0)

    def right(y):
        high, low = split(y)
        return blocks(high), blocks(low)

    def product(lefts, factor):
        high, low = factor
        rows = lefts[0][0].shape[0]
        first = mm(jnp.concatenate([part for pair in lefts for part in pair], 0), high)
        second = mm(jnp.concatenate([pair[0] for pair in lefts], 0), low)
        return [
            first[2 * k * rows : (2 * k + 1) * rows]
            + (first[(2 * k + 1) * rows : (2 * k + 2) * rows] + second[k * rows : (k + 1) * rows])
            for k in range(len(lefts))
        ]

    pairs = range(pair_count)
    total = total_ref[...] + read_message(other_ref, pair_count)
    grams = [total[p * members : (p + 1) * members] for p in pairs]
    sides = total[grams_end:]
    squares = jnp.concatenate([jnp.sum(gram * gram, axis=0, keepdims=True) for gram in grams], 0)
    at_left = lax.broadcasted_iota(jnp.int32, squares.shape, 1) < members
    norm_left = jnp.sum(jnp.where(at_left, squares, 0.0), axis=1, keepdims=True)
    norm_right = jnp.sum(jnp.where(at_left, 0.0, squares), axis=1, keepdims=True)
    bound = degree + jnp.sqrt(jnp.where(at_left, norm_left, norm_right))
    spread = jnp.sqrt(degree / bound)
    iterates = [(grams[p] + degree * identity) / bound[p : p + 1] for p in pairs]
    corrections = [1.5 * identity - 0.5 * iterates[p] for p in pairs]
    factors = [right(corrections[p]) for p in pairs]
    iterates = [product([split(iterates[p])], factors[p])[0] for p in pairs]
    roots = corrections
    for step in range(1, NS_STEPS):
        halves = [split(roots[p]) for p in pairs]
        corrections = [1.5 * identity - 0.5 * product([halves[p]], right(iterates[p]))[0] for p in pairs]
        factors = [right(corrections[p]) for p in pairs]
        if step < NS_STEPS - 1:
            both = [product([split(iterates[p]), halves[p]], factors[p]) for p in pairs]
            iterates = [pair[0] for pair in both]
            roots = [pair[1] for pair in both]
        else:
            roots = [product([halves[p]], factors[p])[0] for p in pairs]
    mixings = []
    for p in pairs:
        factor = right(roots[p])
        side = jnp.broadcast_to(sides[p : p + 1], (PATCH, cols))
        inner = product([split(side)], factor)[0]
        weights = product([split(inner)], factor)[0][:1] / bound[p : p + 1]
        mixings.append((spread[p : p + 1] * roots[p] + weights).astype(bf16))

    patch = lax.broadcasted_iota(jnp.int32, (members, cols), 1) // PATCH
    even = jnp.where(patch % 2 == 0, 1.0, 0.0).astype(bf16)
    odd = jnp.where(patch % 2 == 1, 1.0, 0.0).astype(bf16)
    per_row = cols // (2 * PATCH)
    for a in range(tile_rows // PATCH):
        mixing = jnp.concatenate(mixings[a * per_row : (a + 1) * per_row], 0)
        for r in range(a * PATCH, (a + 1) * PATCH, 2):
            state = jnp.concatenate(
                [jnp.concatenate([lag_ref[i] * even, lag_ref[i] * odd], 0) for i in (r, r + 1)], 1
            )
            spread_out = mm(mixing, state)
            for i in (0, 1):
                part = spread_out[:, i * cols : (i + 1) * cols]
                chosen = part[:members]
                for pair in range(1, per_row):
                    chosen = jnp.where(patch // 2 == pair, part[pair * members : (pair + 1) * members], chosen)
                flat_ref[pl.ds(r + i, members, stride=tile_rows), :] = chosen + mean_ref[r + i : r + i + 1, :]
    out_ref[...] = flat_ref[...].reshape(1, members, tile_rows, cols).astype(bf16)


def shards(history, forecast, spot, alive, levels, precision, radius):
    shares = lax.axis_size("lag")
    tiles = lax.axis_size("dom")
    lag = lax.axis_index("lag")
    share_members, tile_rows, cols = forecast.shape
    members = share_members * shares
    patch_cols = cols // PATCH
    per_group = shares // 2
    group = (lag // per_group) ^ (lax.axis_index("dom") % 2)
    halo_pairs = []
    for t in range(tiles):
        for l in range(shares):
            target = t + 1 if (l // per_group) ^ (t % 2) else t - 1
            if 0 <= target < tiles:
                halo_pairs.append((t * shares + l, target * shares + l))

    def call(kernel, name, in_specs, out_shape, scratch=()):
        return pl.pallas_call(
            kernel,
            in_specs=in_specs,
            out_specs=jax.tree.map(lambda _: vmem, out_shape),
            out_shape=out_shape,
            scratch_shapes=scratch,
            compiler_params=pltpu.CompilerParams(vmem_limit_bytes=32 * 2**20),
            name=name,
        )

    shape = jax.ShapeDtypeStruct
    smem = pl.BlockSpec(memory_space=pltpu.SMEM)
    vmem = pl.BlockSpec(memory_space=pltpu.VMEM)
    hbm = pl.BlockSpec(memory_space=pltpu.HBM)
    parts = [forecast]
    for k in range(1, shares):
        parts.append(lax.ppermute(forecast, "lag", [((i + k) % shares, i) for i in range(shares)]))
    next_radius = lax.ppermute(radius, ("dom", "lag"), halo_pairs)
    place = jnp.concatenate([jnp.stack([lag, group]), radius, next_radius])
    live = lax.broadcasted_iota(jnp.int32, spot.shape, 1) < alive[:, None]
    weights = jnp.where(live, precision, 0.0)
    kind = lax.broadcasted_iota(jnp.int32, (3, *spot.shape), 0)
    tables = jnp.where(kind == 0, weights[None], jnp.where(kind == 1, (weights * levels)[None], spot.astype(f32)[None]))
    fields, own_sum = call(
        functools.partial(fields_kernel, cols),
        "fields",
        [vmem, vmem],
        [shape((2, tile_rows, cols), f32), shape((tile_rows, cols), f32)],
    )(tables, forecast)
    pair_rows = patch_cols * members
    near, far, held, message = call(
        functools.partial(outward_kernel, shares),
        "outward_gram",
        [smem] + [vmem] * (shares + 2),
        [
            shape((NEAR, members, cols), bf16),
            shape((FAR - NEAR, members, cols), bf16),
            shape((2, tile_rows, cols), f32),
            shape((pair_rows + 2 * patch_cols, 2 * members), bf16),
        ],
        [
            pltpu.VMEM((members * tile_rows, cols), f32),
            pltpu.VMEM((2, patch_cols * members + PATCH, members), f32),
        ],
    )(place, *parts, own_sum, fields)
    message = lax.ppermute(message, ("dom", "lag"), halo_pairs)
    own = call(
        own_kernel,
        "own_gram",
        [smem] + [vmem] * 3,
        shape((pair_rows + patch_cols, 2 * members), f32),
    )(place, near, far, held)
    lag_rows, lag_mean = call(
        state_kernel,
        "state",
        [hbm, hbm],
        [shape((tile_rows, members, cols), bf16), shape((tile_rows, cols), f32)],
        [
            pltpu.VMEM((members, tile_rows, cols), bf16),
            pltpu.VMEM((members * tile_rows, cols), f32),
            pltpu.SemaphoreType.DMA,
        ],
    )(held, history[0])
    total, send = call(
        join_kernel,
        "join",
        [vmem, vmem],
        [
            shape((pair_rows + patch_cols, 2 * members), f32),
            shape((pair_rows + 2 * patch_cols, 2 * members), bf16),
        ],
    )(own, message)
    other = lax.ppermute(send, "lag", [(i, (i + per_group) % shares) for i in range(shares)])
    return call(
        finish_kernel,
        "finish",
        [vmem] * 4,
        shape((1, members, tile_rows, cols), bf16),
        [pltpu.VMEM((members * tile_rows, cols), f32)],
    )(total, other, lag_rows, lag_mean)


def solution(mesh):
    in_specs = (
        P("lag", None, "dom", None),
        P("lag", "dom", None),
        P("dom", None),
        P("dom"),
        P("dom", None),
        P("dom", None),
        P("dom"),
    )
    out_specs = P("lag", None, "dom", None)
    return jax.shard_map(shards, mesh=mesh, in_specs=in_specs, out_specs=out_specs, check_vma=False)
```

```python
import functools

import jax
import jax.numpy as jnp
from jax import lax
from jax.experimental import pallas as pl
from jax.experimental.pallas import tpu as pltpu
from jax.sharding import PartitionSpec as P

PATCH = 16
NS_STEPS = 4
RADIUS = 32
FAR = RADIUS - PATCH // 2
NEAR = FAR - PATCH
MIDDLE = (PATCH - 1) / 2

NT = (((1,), (1,)), ((), ()))
NN = (((1,), (0,)), ((), ()))
f32 = jnp.float32
bf16 = jnp.bfloat16


def mm(a, b, dims=NN):
    return lax.dot_general(a, b, dims, preferred_element_type=f32)


def split(x):
    high = x.astype(bf16)
    return high, (x - high.astype(f32)).astype(bf16)


def fields_kernel(cols, table_ref, part_ref, field_ref, sum_ref):
    sum_ref[...] = jnp.sum(part_ref[...].astype(f32), axis=0)
    patches, slots = table_ref.shape[1:]
    patch_cols = cols // PATCH
    patch_rows = patches // patch_cols
    spot = table_ref[2].astype(jnp.int32)
    row_in = spot // PATCH
    col_in = spot % PATCH
    iota_row = lax.broadcasted_iota(jnp.int32, (PATCH, slots), 0)
    iota_col = lax.broadcasted_iota(jnp.int32, (cols, slots), 0)
    for a in range(patch_rows):
        total = jnp.zeros((4 * PATCH, cols), f32)
        for b in range(patch_cols):
            p = a * patch_cols + b
            prec = table_ref[0, p : p + 1, :]
            level = table_ref[1, p : p + 1, :]
            prec_high = prec.astype(bf16).astype(f32)
            level_high = level.astype(bf16).astype(f32)
            on_row = row_in[p : p + 1, :] == iota_row
            pieces = [
                jnp.where(on_row, piece, 0.0).astype(bf16)
                for piece in (prec_high, prec - prec_high, level_high, level - level_high)
            ]
            on_col = jnp.where(col_in[p : p + 1, :] + b * PATCH == iota_col, 1.0, 0.0).astype(bf16)
            total = total + mm(jnp.concatenate(pieces, 0), on_col, NT)
        rows = slice(a * PATCH, (a + 1) * PATCH)
        field_ref[0, rows, :] = total[:PATCH] + total[PATCH : 2 * PATCH]
        field_ref[1, rows, :] = total[2 * PATCH : 3 * PATCH] + total[3 * PATCH :]


def state_kernel(after_ref, hist_hbm, lag_ref, mean_ref, hist_ref, flat_ref, sem):
    copy = pltpu.make_async_copy(hist_hbm, hist_ref, sem)
    copy.start()
    copy.wait()
    members, tile_rows, cols = hist_ref.shape
    state = hist_ref[...].astype(f32)
    mean = jnp.sum(state, axis=0) / members
    mean_ref[...] = mean
    flat_ref[...] = (state - mean[None]).reshape(members * tile_rows, cols)
    for r in range(tile_rows):
        lag_ref[r] = flat_ref[pl.ds(r, members, stride=tile_rows), :].astype(bf16)


def taper_plan(centre_row, first_patch, patch_cols, cols, place_ref):
    q_row = lax.broadcasted_iota(jnp.int32, (patch_cols, cols), 0)
    col = lax.broadcasted_iota(jnp.int32, (patch_cols, cols), 1)
    radius = jnp.zeros((patch_cols, cols), f32)
    for q in range(patch_cols):
        radius = jnp.where(q_row == q, place_ref[3 + first_patch + q].astype(f32), radius)
    col_square = jnp.square(col.astype(f32) - (q_row.astype(f32) * PATCH + MIDDLE))
    return centre_row, col_square, 1.0 / jnp.square(radius)


def accumulate(total, plan, anomalies, weight, innovation, first_row):
    centre_row, col_square, inverse_square = plan
    patches, cols = col_square.shape
    lefts = []
    for i, anomaly in enumerate(anomalies):
        members = anomaly.shape[0]
        offset = (first_row + i).astype(f32) - centre_row
        taper = jnp.square(jnp.maximum(0.0, 1.0 - (offset * offset + col_square) * inverse_square))
        scale = taper * weight[i : i + 1]
        blocks = anomaly.reshape(members // PATCH, PATCH, cols)
        left = [
            (blocks * jnp.broadcast_to(scale[q : q + 1], (PATCH, cols)).astype(bf16)[None]).reshape(members, cols)
            for q in range(patches)
        ]
        tail = taper * innovation[i : i + 1]
        left.append(jnp.concatenate([tail, jnp.zeros((PATCH - patches, cols), f32)], 0).astype(bf16))
        lefts.append(jnp.concatenate(left, 0))
    return total + mm(jnp.concatenate(lefts, 1), jnp.concatenate(anomalies, 1), NT)


STEP = 8


def paired(totals, members, patch_cols):
    pairs = patch_cols // 2
    grams, sides = [], []
    for total in totals:
        for pair in range(pairs):
            at = 2 * pair * members
            grams.append(jnp.concatenate([total[at : at + members], total[at + members : at + 2 * members]], 1))
        for pair in range(pairs):
            at = patch_cols * members + 2 * pair
            sides.append(jnp.concatenate([total[at : at + 1], total[at + 1 : at + 2]], 1))
    return jnp.concatenate(grams, 0), jnp.concatenate(sides, 0)


def message_of(grams, sides):
    return jnp.concatenate([grams.astype(bf16), *split(sides)], 0)


def read_message(ref, side_count):
    at = ref.shape[0] - 2 * side_count
    high, low = ref[at : at + side_count, :].astype(f32), ref[at + side_count :, :].astype(f32)
    return jnp.concatenate([ref[:at, :].astype(f32), high + low], 0)


def outward_kernel(shares, place_ref, *refs):
    parts, refs = refs[:shares], refs[shares:]
    sum_ref, field_ref, near_ref, far_ref, held_ref, message_ref, flat_ref, total_ref = refs
    share_members, tile_rows, cols = parts[0].shape
    members = share_members * shares
    patch_cols = cols // PATCH
    lag, group = place_ref[0], place_ref[1]
    states = [part[...].astype(f32) for part in parts]
    mean = functools.reduce(jnp.add, [jnp.sum(state, axis=0) for state in states[1:]], sum_ref[...]) / members
    for k, state in enumerate(states):
        at = pl.multiple_of(lax.rem(lag + k, shares) * (share_members * tile_rows), 8)
        flat_ref[pl.ds(at, share_members * tile_rows), :] = (state - mean[None]).reshape(-1, cols)
    weight = field_ref[0]
    held_ref[0] = weight
    held_ref[1] = field_ref[1] - mean * weight

    def row(r):
        return flat_ref[pl.ds(r, members, stride=tile_rows), :].astype(bf16)

    near = pl.multiple_of(group * (tile_rows - NEAR), 8)
    sign = 1 - 2 * group
    middle = jnp.where(group == 0, MIDDLE - PATCH, MIDDLE + tile_rows)
    first_near = (1 - group) * patch_cols
    next_patches = (tile_rows // PATCH) * patch_cols
    plans = [
        taper_plan(middle, next_patches + first_near, patch_cols, cols, place_ref),
        taper_plan(middle - (sign * PATCH).astype(f32), next_patches + patch_cols - first_near, patch_cols, cols, place_ref),
    ]
    anomalies = [row(near + i) for i in range(NEAR)]
    for i, anomaly in enumerate(anomalies):
        near_ref[i] = anomaly
    weights, innovations = (held_ref[k, pl.ds(near, NEAR), :] for k in range(2))
    blank = jnp.zeros(total_ref.shape[1:], f32)
    totals = [accumulate(blank, plan, anomalies, weights, innovations, near) for plan in plans]
    for start in range(NEAR, FAR, STEP):
        anomalies = [row(start + i) for i in range(STEP)]
        for i, anomaly in enumerate(anomalies):
            far_ref[start - NEAR + i] = anomaly
        rows = slice(start, start + STEP)
        totals[0] = accumulate(totals[0], plans[0], anomalies, held_ref[0, rows, :], held_ref[1, rows, :], jnp.int32(start))
    total_ref[1 - group] = totals[0]
    total_ref[group] = totals[1]
    message_ref[...] = message_of(*paired([total_ref[0], total_ref[1]], members, patch_cols))


def own_kernel(place_ref, near_ref, far_ref, field_ref, out_ref):
    members, cols = near_ref.shape[1:]
    tile_rows = field_ref.shape[1]
    patch_cols = cols // PATCH
    group = place_ref[1]
    plans = [
        taper_plan(MIDDLE + a * PATCH, a * patch_cols, patch_cols, cols, place_ref) for a in range(tile_rows // PATCH)
    ]
    near = pl.multiple_of(group * (tile_rows - NEAR), 8)
    far = pl.multiple_of(NEAR + group * (FAR - 2 * NEAR), 8)
    totals = [jnp.zeros((patch_cols * members + PATCH, members), f32) for _ in plans]
    for first, anomalies in (
        (near, [near_ref[i] for i in range(NEAR)]),
        (far, [far_ref[far - NEAR + i] for i in range(tile_rows // 2 - NEAR)]),
    ):
        fields = [field_ref[k, pl.ds(first, len(anomalies)), :] for k in range(2)]
        totals = [accumulate(total, plan, anomalies, *fields, first) for total, plan in zip(totals, plans)]
    out_ref[...] = jnp.concatenate(paired(totals, members, patch_cols), 0)


def join_kernel(place_ref, own_ref, message_ref, total_ref, send_ref):
    sides = message_ref.shape[0] - own_ref.shape[0]
    total = own_ref[...] + jnp.where(place_ref[2] == 1, read_message(message_ref, sides), 0.0)
    total_ref[...] = total
    send_ref[...] = message_of(total[: total.shape[0] - sides], total[total.shape[0] - sides :])


def finish_kernel(total_ref, other_ref, lag_ref, mean_ref, out_ref, flat_ref):
    tile_rows, members, cols = lag_ref.shape
    degree = members - 1.0
    pair_count = total_ref.shape[0] // members
    grams_end = pair_count * members
    row = lax.broadcasted_iota(jnp.int32, (members, 2 * members), 0)
    lane = lax.broadcasted_iota(jnp.int32, (members, 2 * members), 1)
    identity = jnp.where(row == lane % members, 1.0, 0.0)
    left_mask = jnp.where(lane < members, 1.0, 0.0).astype(bf16)
    right_mask = jnp.where(lane < members, 0.0, 1.0).astype(bf16)

    def blocks(y):
        return jnp.concatenate([y * left_mask, y * right_mask], 0)

    def right(y):
        high, low = split(y)
        return blocks(high), blocks(low)

    def product(lefts, factor):
        high, low = factor
        rows = lefts[0][0].shape[0]
        first = mm(jnp.concatenate([part for pair in lefts for part in pair], 0), high)
        second = mm(jnp.concatenate([pair[0] for pair in lefts], 0), low)
        return [
            first[2 * k * rows : (2 * k + 1) * rows]
            + (first[(2 * k + 1) * rows : (2 * k + 2) * rows] + second[k * rows : (k + 1) * rows])
            for k in range(len(lefts))
        ]

    pairs = range(pair_count)
    total = total_ref[...] + read_message(other_ref, pair_count)
    grams = [total[p * members : (p + 1) * members] for p in pairs]
    sides = total[grams_end:]
    squares = jnp.concatenate([jnp.sum(gram * gram, axis=0, keepdims=True) for gram in grams], 0)
    at_left = lax.broadcasted_iota(jnp.int32, squares.shape, 1) < members
    norm_left = jnp.sum(jnp.where(at_left, squares, 0.0), axis=1, keepdims=True)
    norm_right = jnp.sum(jnp.where(at_left, 0.0, squares), axis=1, keepdims=True)
    bound = degree + jnp.sqrt(jnp.where(at_left, norm_left, norm_right))
    spread = jnp.sqrt(degree / bound)
    iterates = [(grams[p] + degree * identity) / bound[p : p + 1] for p in pairs]
    corrections = [1.5 * identity - 0.5 * iterates[p] for p in pairs]
    factors = [right(corrections[p]) for p in pairs]
    iterates = [product([split(iterates[p])], factors[p])[0] for p in pairs]
    roots = corrections
    for step in range(1, NS_STEPS):
        halves = [split(roots[p]) for p in pairs]
        corrections = [1.5 * identity - 0.5 * product([halves[p]], right(iterates[p]))[0] for p in pairs]
        factors = [right(corrections[p]) for p in pairs]
        if step < NS_STEPS - 1:
            both = [product([split(iterates[p]), halves[p]], factors[p]) for p in pairs]
            iterates = [pair[0] for pair in both]
            roots = [pair[1] for pair in both]
        else:
            roots = [product([halves[p]], factors[p])[0] for p in pairs]
    mixings = []
    for p in pairs:
        factor = right(roots[p])
        side = jnp.broadcast_to(sides[p : p + 1], (PATCH, cols))
        inner = product([split(side)], factor)[0]
        weights = product([split(inner)], factor)[0][:1] / bound[p : p + 1]
        mixings.append((spread[p : p + 1] * roots[p] + weights).astype(bf16))

    patch = lax.broadcasted_iota(jnp.int32, (members, cols), 1) // PATCH
    even = jnp.where(patch % 2 == 0, 1.0, 0.0).astype(bf16)
    odd = jnp.where(patch % 2 == 1, 1.0, 0.0).astype(bf16)
    per_row = cols // (2 * PATCH)
    for a in range(tile_rows // PATCH):
        mixing = jnp.concatenate(mixings[a * per_row : (a + 1) * per_row], 0)
        for r in range(a * PATCH, (a + 1) * PATCH, 2):
            state = jnp.concatenate(
                [jnp.concatenate([lag_ref[i] * even, lag_ref[i] * odd], 0) for i in (r, r + 1)], 1
            )
            spread_out = mm(mixing, state)
            for i in (0, 1):
                part = spread_out[:, i * cols : (i + 1) * cols]
                chosen = part[:members]
                for pair in range(1, per_row):
                    chosen = jnp.where(patch // 2 == pair, part[pair * members : (pair + 1) * members], chosen)
                flat_ref[pl.ds(r + i, members, stride=tile_rows), :] = chosen + mean_ref[r + i : r + i + 1, :]
    out_ref[...] = flat_ref[...].reshape(1, members, tile_rows, cols).astype(bf16)


def shards(history, forecast, spot, alive, levels, precision, radius):
    shares = lax.axis_size("lag")
    tiles = lax.axis_size("dom")
    lag = lax.axis_index("lag")
    share_members, tile_rows, cols = forecast.shape
    members = share_members * shares
    patch_cols = cols // PATCH
    per_group = shares // 2
    group = lag // per_group
    tile = lax.axis_index("dom")
    served = jnp.where(group == 0, tile < tiles - 1, tile > 0).astype(jnp.int32)
    halo_pairs = []
    for t in range(tiles):
        for l in range(shares):
            step = 1 if l >= per_group else -1
            if 0 <= t + step < tiles:
                target = (t + step) * shares + l
            else:
                target = t * shares + (l + per_group) % shares
            halo_pairs.append((t * shares + l, target))

    def call(kernel, name, in_specs, out_shape, scratch=()):
        return pl.pallas_call(
            kernel,
            in_specs=in_specs,
            out_specs=jax.tree.map(lambda _: vmem, out_shape),
            out_shape=out_shape,
            scratch_shapes=scratch,
            compiler_params=pltpu.CompilerParams(vmem_limit_bytes=32 * 2**20),
            name=name,
        )

    shape = jax.ShapeDtypeStruct
    smem = pl.BlockSpec(memory_space=pltpu.SMEM)
    vmem = pl.BlockSpec(memory_space=pltpu.VMEM)
    hbm = pl.BlockSpec(memory_space=pltpu.HBM)
    parts = [forecast]
    for k in range(1, shares):
        parts.append(lax.ppermute(forecast, "lag", [((i + k) % shares, i) for i in range(shares)]))
    live = lax.broadcasted_iota(jnp.int32, spot.shape, 1) < alive[:, None]
    weights = jnp.where(live, precision, 0.0)
    kind = lax.broadcasted_iota(jnp.int32, (3, *spot.shape), 0)
    tables = jnp.where(kind == 0, weights[None], jnp.where(kind == 1, (weights * levels)[None], spot.astype(f32)[None]))
    own_radius, tables = lax.optimization_barrier((radius, tables))
    next_radius = lax.ppermute(own_radius, ("dom", "lag"), [(t, s) for s, t in halo_pairs])
    place = jnp.concatenate([jnp.stack([lag, group, served]), radius, next_radius])
    fields, own_sum = call(
        functools.partial(fields_kernel, cols),
        "fields",
        [vmem, vmem],
        [shape((2, tile_rows, cols), f32), shape((tile_rows, cols), f32)],
    )(tables, forecast)
    pair_rows = patch_cols * members
    near, far, held, message = call(
        functools.partial(outward_kernel, shares),
        "outward_gram",
        [smem] + [vmem] * (shares + 2),
        [
            shape((NEAR, members, cols), bf16),
            shape((FAR - NEAR, members, cols), bf16),
            shape((2, tile_rows, cols), f32),
            shape((pair_rows + 2 * patch_cols, 2 * members), bf16),
        ],
        [
            pltpu.VMEM((members * tile_rows, cols), f32),
            pltpu.VMEM((2, patch_cols * members + PATCH, members), f32),
        ],
    )(place, *parts, own_sum, fields)
    message = lax.ppermute(message, ("dom", "lag"), halo_pairs)
    own = call(
        own_kernel,
        "own_gram",
        [smem] + [vmem] * 3,
        shape((pair_rows + patch_cols, 2 * members), f32),
    )(place, near, far, held)
    lag_rows, lag_mean = call(
        state_kernel,
        "state",
        [hbm, hbm],
        [shape((tile_rows, members, cols), bf16), shape((tile_rows, cols), f32)],
        [
            pltpu.VMEM((members, tile_rows, cols), bf16),
            pltpu.VMEM((members * tile_rows, cols), f32),
            pltpu.SemaphoreType.DMA,
        ],
    )(held, history[0])
    total, send = call(
        join_kernel,
        "join",
        [smem, vmem, vmem],
        [
            shape((pair_rows + patch_cols, 2 * members), f32),
            shape((pair_rows + 2 * patch_cols, 2 * members), bf16),
        ],
    )(place, own, message)
    other = lax.ppermute(send, "lag", [(i, (i + per_group) % shares) for i in range(shares)])
    return call(
        finish_kernel,
        "finish",
        [vmem] * 4,
        shape((1, members, tile_rows, cols), bf16),
        [pltpu.VMEM((members * tile_rows, cols), f32)],
    )(total, other, lag_rows, lag_mean)


def solution(mesh):
    in_specs = (
        P("lag", None, "dom", None),
        P("lag", "dom", None),
        P("dom", None),
        P("dom"),
        P("dom", None),
        P("dom", None),
        P("dom"),
    )
    out_specs = P("lag", None, "dom", None)
    return jax.shard_map(shards, mesh=mesh, in_specs=in_specs, out_specs=out_specs, check_vma=False)
```

```python
import functools

import jax
import jax.numpy as jnp
from jax import lax
from jax.experimental import pallas as pl
from jax.experimental.pallas import tpu as pltpu
from jax.sharding import PartitionSpec as P

PATCH = 16
NS_STEPS = 4
RADIUS = 32
FAR = RADIUS - PATCH // 2
NEAR = FAR - PATCH
MIDDLE = (PATCH - 1) / 2

NT = (((1,), (1,)), ((), ()))
NN = (((1,), (0,)), ((), ()))
f32 = jnp.float32
bf16 = jnp.bfloat16


def mm(a, b, dims=NN):
    return lax.dot_general(a, b, dims, preferred_element_type=f32)


def split(x):
    high = x.astype(bf16)
    return high, (x - high.astype(f32)).astype(bf16)


def fields_kernel(cols, table_ref, part_ref, field_ref, sum_ref):
    sum_ref[...] = jnp.sum(part_ref[...].astype(f32), axis=0)
    patches, slots = table_ref.shape[1:]
    patch_cols = cols // PATCH
    patch_rows = patches // patch_cols
    spot = table_ref[2].astype(jnp.int32)
    row_in = spot // PATCH
    col_in = spot % PATCH
    iota_row = lax.broadcasted_iota(jnp.int32, (PATCH, slots), 0)
    iota_col = lax.broadcasted_iota(jnp.int32, (cols, slots), 0)
    for a in range(patch_rows):
        total = jnp.zeros((4 * PATCH, cols), f32)
        for b in range(patch_cols):
            p = a * patch_cols + b
            prec = table_ref[0, p : p + 1, :]
            level = table_ref[1, p : p + 1, :]
            prec_high = prec.astype(bf16).astype(f32)
            level_high = level.astype(bf16).astype(f32)
            on_row = row_in[p : p + 1, :] == iota_row
            pieces = [
                jnp.where(on_row, piece, 0.0).astype(bf16)
                for piece in (prec_high, prec - prec_high, level_high, level - level_high)
            ]
            on_col = jnp.where(col_in[p : p + 1, :] + b * PATCH == iota_col, 1.0, 0.0).astype(bf16)
            total = total + mm(jnp.concatenate(pieces, 0), on_col, NT)
        rows = slice(a * PATCH, (a + 1) * PATCH)
        field_ref[0, rows, :] = total[:PATCH] + total[PATCH : 2 * PATCH]
        field_ref[1, rows, :] = total[2 * PATCH : 3 * PATCH] + total[3 * PATCH :]


def state_kernel(after_ref, hist_ref, lag_ref, mean_ref, flat_ref):
    members, tile_rows, cols = hist_ref.shape
    state = hist_ref[...].astype(f32)
    mean = jnp.sum(state, axis=0) / members
    mean_ref[...] = mean
    flat_ref[...] = (state - mean[None]).reshape(members * tile_rows, cols)
    for r in range(tile_rows):
        lag_ref[r] = flat_ref[pl.ds(r, members, stride=tile_rows), :].astype(bf16)


def half_of_lags():
    return lax.axis_index("lag") // (lax.axis_size("lag") // 2)


def ring(tiles, shares, turn):
    half = shares // 2
    pairs = []
    for t in range(tiles):
        for l in range(shares):
            target = t + (1 if (l // half) ^ turn else -1)
            if 0 <= target < tiles:
                pairs.append((t * shares + l, target * shares + l))
            else:
                pairs.append((t * shares + l, t * shares + (l + half) % shares))
    return pairs


def taper_plan(centre_row, inverse_square):
    q_row = lax.broadcasted_iota(jnp.int32, inverse_square.shape, 0)
    col = lax.broadcasted_iota(jnp.int32, inverse_square.shape, 1)
    col_square = jnp.square(col.astype(f32) - (q_row.astype(f32) * PATCH + MIDDLE))
    return centre_row, col_square, inverse_square


def accumulate(total, plan, anomalies, weight, innovation, first_row):
    centre_row, col_square, inverse_square = plan
    patches, cols = col_square.shape
    lefts = []
    for i, anomaly in enumerate(anomalies):
        members = anomaly.shape[0]
        offset = (first_row + i).astype(f32) - centre_row
        taper = jnp.square(jnp.maximum(0.0, 1.0 - (offset * offset + col_square) * inverse_square))
        scale = taper * weight[i : i + 1]
        blocks = anomaly.reshape(members // PATCH, PATCH, cols)
        left = [
            (blocks * jnp.broadcast_to(scale[q : q + 1], (PATCH, cols)).astype(bf16)[None]).reshape(members, cols)
            for q in range(patches)
        ]
        tail = taper * innovation[i : i + 1]
        left.append(jnp.concatenate([tail, jnp.zeros((PATCH - patches, cols), f32)], 0).astype(bf16))
        lefts.append(jnp.concatenate(left, 0))
    return total + mm(jnp.concatenate(lefts, 1), jnp.concatenate(anomalies, 1), NT)


STEP = 8


def paired(totals, members, patch_cols):
    pairs = patch_cols // 2
    grams, sides = [], []
    for total in totals:
        for pair in range(pairs):
            at = 2 * pair * members
            grams.append(jnp.concatenate([total[at : at + members], total[at + members : at + 2 * members]], 1))
        for pair in range(pairs):
            at = patch_cols * members + 2 * pair
            sides.append(jnp.concatenate([total[at : at + 1], total[at + 1 : at + 2]], 1))
    return jnp.concatenate(grams, 0), jnp.concatenate(sides, 0)


def message_of(grams, sides):
    return jnp.concatenate([grams.astype(bf16), *split(sides)], 0)


def read_message(ref, side_count):
    at = ref.shape[0] - 2 * side_count
    high, low = ref[at : at + side_count, :].astype(f32), ref[at + side_count :, :].astype(f32)
    return jnp.concatenate([ref[:at, :].astype(f32), high + low], 0)


def outward(turn, rows_ref, held_ref, inverse_ref, message_ref, total_ref):
    tile_rows, members, cols = rows_ref.shape
    patch_cols = cols // PATCH
    down = half_of_lags() ^ turn
    near = pl.multiple_of(down * (tile_rows - NEAR), 8)
    middle = jnp.where(down == 0, MIDDLE - PATCH, MIDDLE + tile_rows)
    plans = [
        taper_plan(middle, inverse_ref[1 - down]),
        taper_plan(middle + jnp.where(down == 0, -PATCH, PATCH).astype(f32), inverse_ref[down]),
    ]
    anomalies = [rows_ref[near + i] for i in range(NEAR)]
    fields = [held_ref[k, pl.ds(near, NEAR), :] for k in range(2)]
    blank = jnp.zeros(total_ref.shape[1:], f32)
    totals = [accumulate(blank, plan, anomalies, *fields, near) for plan in plans]
    for start in range(NEAR, FAR, STEP):
        anomalies = [rows_ref[start + i] for i in range(STEP)]
        fields = [held_ref[k, start : start + STEP, :] for k in range(2)]
        totals[0] = accumulate(totals[0], plans[0], anomalies, *fields, jnp.int32(start))
    total_ref[1 - down] = totals[0]
    total_ref[down] = totals[1]
    message_ref[...] = message_of(*paired([total_ref[0], total_ref[1]], members, patch_cols))


def first_kernel(shares, *refs):
    parts, refs = refs[:shares], refs[shares:]
    sum_ref, field_ref, inverse_ref, rows_ref, held_ref, message_ref, flat_ref, total_ref = refs
    share_members, tile_rows, cols = parts[0].shape
    members = share_members * shares
    lag = lax.axis_index("lag")
    states = [part[...].astype(f32) for part in parts]
    mean = functools.reduce(jnp.add, [jnp.sum(state, axis=0) for state in states[1:]], sum_ref[...]) / members
    for k, state in enumerate(states):
        at = pl.multiple_of(lax.rem(lag + k, shares) * (share_members * tile_rows), 8)
        flat_ref[pl.ds(at, share_members * tile_rows), :] = (state - mean[None]).reshape(-1, cols)
    weight = field_ref[0]
    held_ref[0] = weight
    held_ref[1] = field_ref[1] - mean * weight
    for r in range(tile_rows):
        rows_ref[r] = flat_ref[pl.ds(r, members, stride=tile_rows), :].astype(bf16)
    outward(0, rows_ref, held_ref, inverse_ref, message_ref, total_ref)


def second_kernel(rows_ref, held_ref, inverse_ref, message_ref, total_ref):
    outward(1, rows_ref, held_ref, inverse_ref, message_ref, total_ref)


def own_kernel(rows_ref, held_ref, inverse_ref, out_ref):
    tile_rows, members, cols = rows_ref.shape
    patch_cols = cols // PATCH
    plans = [taper_plan(MIDDLE + a * PATCH, inverse_ref[a]) for a in range(tile_rows // PATCH)]
    totals = [jnp.zeros((patch_cols * members + PATCH, members), f32) for _ in plans]
    for start in range(0, tile_rows, STEP):
        anomalies = [rows_ref[start + i] for i in range(STEP)]
        fields = [held_ref[k, start : start + STEP, :] for k in range(2)]
        totals = [accumulate(total, plan, anomalies, *fields, jnp.int32(start)) for total, plan in zip(totals, plans)]
    out_ref[...] = jnp.concatenate(paired(totals, members, patch_cols), 0)


def finish_kernel(total_ref, first_ref, second_ref, lag_ref, mean_ref, out_ref, flat_ref):
    tile_rows, members, cols = lag_ref.shape
    degree = members - 1.0
    pair_count = total_ref.shape[0] // members
    grams_end = pair_count * members
    row = lax.broadcasted_iota(jnp.int32, (members, 2 * members), 0)
    lane = lax.broadcasted_iota(jnp.int32, (members, 2 * members), 1)
    identity = jnp.where(row == lane % members, 1.0, 0.0)
    left_mask = jnp.where(lane < members, 1.0, 0.0).astype(bf16)
    right_mask = jnp.where(lane < members, 0.0, 1.0).astype(bf16)

    def blocks(y):
        return jnp.concatenate([y * left_mask, y * right_mask], 0)

    def right(y):
        high, low = split(y)
        return blocks(high), blocks(low)

    def product(lefts, factor):
        high, low = factor
        rows = lefts[0][0].shape[0]
        first = mm(jnp.concatenate([part for pair in lefts for part in pair], 0), high)
        second = mm(jnp.concatenate([pair[0] for pair in lefts], 0), low)
        return [
            first[2 * k * rows : (2 * k + 1) * rows]
            + (first[(2 * k + 1) * rows : (2 * k + 2) * rows] + second[k * rows : (k + 1) * rows])
            for k in range(len(lefts))
        ]

    pairs = range(pair_count)
    total = total_ref[...]
    tile, tiles = lax.axis_index("dom"), lax.axis_size("dom")
    for turn, ref in enumerate((first_ref, second_ref)):
        down = half_of_lags() ^ turn
        there = jnp.where(down == 1, tile > 0, tile < tiles - 1)
        total = total + jnp.where(there, read_message(ref, pair_count), 0.0)
    grams = [total[p * members : (p + 1) * members] for p in pairs]
    sides = total[grams_end:]
    squares = jnp.concatenate([jnp.sum(gram * gram, axis=0, keepdims=True) for gram in grams], 0)
    at_left = lax.broadcasted_iota(jnp.int32, squares.shape, 1) < members
    norm_left = jnp.sum(jnp.where(at_left, squares, 0.0), axis=1, keepdims=True)
    norm_right = jnp.sum(jnp.where(at_left, 0.0, squares), axis=1, keepdims=True)
    bound = degree + jnp.sqrt(jnp.where(at_left, norm_left, norm_right))
    spread = jnp.sqrt(degree / bound)
    iterates = [(grams[p] + degree * identity) / bound[p : p + 1] for p in pairs]
    corrections = [1.5 * identity - 0.5 * iterates[p] for p in pairs]
    factors = [right(corrections[p]) for p in pairs]
    iterates = [product([split(iterates[p])], factors[p])[0] for p in pairs]
    roots = corrections
    for step in range(1, NS_STEPS):
        halves = [split(roots[p]) for p in pairs]
        corrections = [1.5 * identity - 0.5 * product([halves[p]], right(iterates[p]))[0] for p in pairs]
        factors = [right(corrections[p]) for p in pairs]
        if step < NS_STEPS - 1:
            both = [product([split(iterates[p]), halves[p]], factors[p]) for p in pairs]
            iterates = [pair[0] for pair in both]
            roots = [pair[1] for pair in both]
        else:
            roots = [product([halves[p]], factors[p])[0] for p in pairs]
    mixings = []
    for p in pairs:
        factor = right(roots[p])
        side = jnp.broadcast_to(sides[p : p + 1], (PATCH, cols))
        inner = product([split(side)], factor)[0]
        weights = product([split(inner)], factor)[0][:1] / bound[p : p + 1]
        mixings.append((spread[p : p + 1] * roots[p] + weights).astype(bf16))

    patch = lax.broadcasted_iota(jnp.int32, (members, cols), 1) // PATCH
    even = jnp.where(patch % 2 == 0, 1.0, 0.0).astype(bf16)
    odd = jnp.where(patch % 2 == 1, 1.0, 0.0).astype(bf16)
    per_row = cols // (2 * PATCH)
    for a in range(tile_rows // PATCH):
        mixing = jnp.concatenate(mixings[a * per_row : (a + 1) * per_row], 0)
        for r in range(a * PATCH, (a + 1) * PATCH, 2):
            state = jnp.concatenate(
                [jnp.concatenate([lag_ref[i] * even, lag_ref[i] * odd], 0) for i in (r, r + 1)], 1
            )
            spread_out = mm(mixing, state)
            for i in (0, 1):
                part = spread_out[:, i * cols : (i + 1) * cols]
                chosen = part[:members]
                for pair in range(1, per_row):
                    chosen = jnp.where(patch // 2 == pair, part[pair * members : (pair + 1) * members], chosen)
                flat_ref[pl.ds(r + i, members, stride=tile_rows), :] = chosen + mean_ref[r + i : r + i + 1, :]
    out_ref[...] = flat_ref[...].reshape(1, members, tile_rows, cols).astype(bf16)


def shards(history, forecast, spot, alive, levels, precision, radius):
    shares = lax.axis_size("lag")
    tiles = lax.axis_size("dom")
    share_members, tile_rows, cols = forecast.shape
    members = share_members * shares
    patch_cols = cols // PATCH
    def call(kernel, name, in_specs, out_shape, scratch=()):
        return pl.pallas_call(
            kernel,
            in_specs=in_specs,
            out_specs=jax.tree.map(lambda _: vmem, out_shape),
            out_shape=out_shape,
            scratch_shapes=scratch,
            compiler_params=pltpu.CompilerParams(vmem_limit_bytes=32 * 2**20),
            name=name,
        )

    shape = jax.ShapeDtypeStruct
    vmem = pl.BlockSpec(memory_space=pltpu.VMEM)
    parts = [forecast]
    for k in range(1, shares):
        parts.append(lax.ppermute(forecast, "lag", [((i + k) % shares, i) for i in range(shares)]))
    live = lax.broadcasted_iota(jnp.int32, spot.shape, 1) < alive[:, None]
    weights = jnp.where(live, precision, 0.0)
    kind = lax.broadcasted_iota(jnp.int32, (3, *spot.shape), 0)
    tables = jnp.where(kind == 0, weights[None], jnp.where(kind == 1, (weights * levels)[None], spot.astype(f32)[None]))
    inverse = jnp.broadcast_to(
        (1.0 / jnp.square(radius.astype(f32))).reshape(-1, patch_cols, 1), (tile_rows // PATCH, patch_cols, cols)
    )
    sent, tables = lax.optimization_barrier((inverse, tables))
    rings = [ring(tiles, shares, turn) for turn in range(2)]
    axes = ("dom", "lag")
    next_inverses = [lax.ppermute(sent, axes, [(t, s) for s, t in pairs]) for pairs in rings]
    fields, own_sum = call(
        functools.partial(fields_kernel, cols),
        "fields",
        [vmem, vmem],
        [shape((2, tile_rows, cols), f32), shape((tile_rows, cols), f32)],
    )(tables, forecast)
    pair_rows = patch_cols * members
    message_shape = shape((pair_rows + 2 * patch_cols, 2 * members), bf16)
    total_scratch = pltpu.VMEM((2, patch_cols * members + PATCH, members), f32)
    rows, held, message = call(
        functools.partial(first_kernel, shares),
        "first_gram",
        [vmem] * (shares + 3),
        [shape((tile_rows, members, cols), bf16), shape((2, tile_rows, cols), f32), message_shape],
        [pltpu.VMEM((members * tile_rows, cols), f32), total_scratch],
    )(*parts, own_sum, fields, next_inverses[0])
    first = lax.ppermute(message, axes, rings[0])
    message = call(second_kernel, "second_gram", [vmem] * 3, message_shape, [total_scratch])(rows, held, next_inverses[1])
    second = lax.ppermute(message, axes, rings[1])
    own = call(own_kernel, "own_gram", [vmem] * 3, shape((pair_rows + patch_cols, 2 * members), f32))(rows, held, inverse)
    lag_rows, lag_mean = call(
        state_kernel,
        "state",
        [vmem, vmem],
        [shape((tile_rows, members, cols), bf16), shape((tile_rows, cols), f32)],
        [pltpu.VMEM((members * tile_rows, cols), f32)],
    )(held, history[0])
    return call(
        finish_kernel,
        "finish",
        [vmem] * 5,
        shape((1, members, tile_rows, cols), bf16),
        [pltpu.VMEM((members * tile_rows, cols), f32)],
    )(own, first, second, lag_rows, lag_mean)


def solution(mesh):
    in_specs = (
        P("lag", None, "dom", None),
        P("lag", "dom", None),
        P("dom", None),
        P("dom"),
        P("dom", None),
        P("dom", None),
        P("dom"),
    )
    out_specs = P("lag", None, "dom", None)
    return jax.shard_map(shards, mesh=mesh, in_specs=in_specs, out_specs=out_specs, check_vma=False)
```

```python
import functools

import jax
import jax.numpy as jnp
from jax import lax
from jax.experimental import pallas as pl
from jax.experimental.pallas import tpu as pltpu
from jax.sharding import PartitionSpec as P

PATCH = 16
NS_STEPS = 4
RADIUS = 32
FAR = RADIUS - PATCH // 2
NEAR = FAR - PATCH
MIDDLE = (PATCH - 1) / 2

NT = (((1,), (1,)), ((), ()))
NN = (((1,), (0,)), ((), ()))
f32 = jnp.float32
bf16 = jnp.bfloat16


def mm(a, b, dims=NN):
    return lax.dot_general(a, b, dims, preferred_element_type=f32)


def split(x):
    high = x.astype(bf16)
    return high, (x - high.astype(f32)).astype(bf16)


def fields_kernel(cols, table_ref, part_ref, field_ref, sum_ref):
    sum_ref[...] = jnp.sum(part_ref[...].astype(f32), axis=0)
    patches, slots = table_ref.shape[1:]
    patch_cols = cols // PATCH
    patch_rows = patches // patch_cols
    spot = table_ref[2].astype(jnp.int32)
    row_in = spot // PATCH
    col_in = spot % PATCH
    iota_row = lax.broadcasted_iota(jnp.int32, (PATCH, slots), 0)
    iota_col = lax.broadcasted_iota(jnp.int32, (cols, slots), 0)
    for a in range(patch_rows):
        total = jnp.zeros((4 * PATCH, cols), f32)
        for b in range(patch_cols):
            p = a * patch_cols + b
            prec = table_ref[0, p : p + 1, :]
            level = table_ref[1, p : p + 1, :]
            prec_high = prec.astype(bf16).astype(f32)
            level_high = level.astype(bf16).astype(f32)
            on_row = row_in[p : p + 1, :] == iota_row
            pieces = [
                jnp.where(on_row, piece, 0.0).astype(bf16)
                for piece in (prec_high, prec - prec_high, level_high, level - level_high)
            ]
            on_col = jnp.where(col_in[p : p + 1, :] + b * PATCH == iota_col, 1.0, 0.0).astype(bf16)
            total = total + mm(jnp.concatenate(pieces, 0), on_col, NT)
        rows = slice(a * PATCH, (a + 1) * PATCH)
        field_ref[0, rows, :] = total[:PATCH] + total[PATCH : 2 * PATCH]
        field_ref[1, rows, :] = total[2 * PATCH : 3 * PATCH] + total[3 * PATCH :]


def state_kernel(after_ref, hist_ref, lag_ref, mean_ref, flat_ref):
    members, tile_rows, cols = hist_ref.shape
    state = hist_ref[...].astype(f32)
    mean = jnp.sum(state, axis=0) / members
    mean_ref[...] = mean
    flat_ref[...] = (state - mean[None]).reshape(members * tile_rows, cols)
    for r in range(tile_rows):
        lag_ref[r] = flat_ref[pl.ds(r, members, stride=tile_rows), :].astype(bf16)


def half_of_lags():
    return lax.axis_index("lag") // (lax.axis_size("lag") // 2)


def ring(tiles, shares, turn):
    half = shares // 2
    pairs = []
    for t in range(tiles):
        for l in range(shares):
            target = t + (1 if (l // half) ^ turn else -1)
            if 0 <= target < tiles:
                pairs.append((t * shares + l, target * shares + l))
            else:
                pairs.append((t * shares + l, t * shares + (l + half) % shares))
    return pairs


def taper_plan(centre_row, inverse_square):
    q_row = lax.broadcasted_iota(jnp.int32, inverse_square.shape, 0)
    col = lax.broadcasted_iota(jnp.int32, inverse_square.shape, 1)
    col_square = jnp.square(col.astype(f32) - (q_row.astype(f32) * PATCH + MIDDLE))
    return centre_row, col_square, inverse_square


def accumulate(total, plan, anomalies, weight, innovation, first_row):
    centre_row, col_square, inverse_square = plan
    patches, cols = col_square.shape
    lefts = []
    for i, anomaly in enumerate(anomalies):
        members = anomaly.shape[0]
        offset = (first_row + i).astype(f32) - centre_row
        taper = jnp.square(jnp.maximum(0.0, 1.0 - (offset * offset + col_square) * inverse_square))
        scale = taper * weight[i : i + 1]
        blocks = anomaly.reshape(members // PATCH, PATCH, cols)
        left = [
            (blocks * jnp.broadcast_to(scale[q : q + 1], (PATCH, cols)).astype(bf16)[None]).reshape(members, cols)
            for q in range(patches)
        ]
        tail = taper * innovation[i : i + 1]
        left.append(jnp.concatenate([tail, jnp.zeros((PATCH - patches, cols), f32)], 0).astype(bf16))
        lefts.append(jnp.concatenate(left, 0))
    return total + mm(jnp.concatenate(lefts, 1), jnp.concatenate(anomalies, 1), NT)


STEP = 8


def paired(totals, members, patch_cols):
    pairs = patch_cols // 2
    grams, sides = [], []
    for total in totals:
        for pair in range(pairs):
            at = 2 * pair * members
            grams.append(jnp.concatenate([total[at : at + members], total[at + members : at + 2 * members]], 1))
        for pair in range(pairs):
            at = patch_cols * members + 2 * pair
            sides.append(jnp.concatenate([total[at : at + 1], total[at + 1 : at + 2]], 1))
    return jnp.concatenate(grams, 0), jnp.concatenate(sides, 0)


def message_of(grams, sides):
    return jnp.concatenate([grams.astype(bf16), *split(sides)], 0)


def read_message(ref, side_count):
    at = ref.shape[0] - 2 * side_count
    high, low = ref[at : at + side_count, :].astype(f32), ref[at + side_count :, :].astype(f32)
    return jnp.concatenate([ref[:at, :].astype(f32), high + low], 0)


def outward(turn, rows_ref, held_ref, inverse_ref, message_ref, total_ref):
    tile_rows, members, cols = rows_ref.shape
    patch_cols = cols // PATCH
    down = half_of_lags() ^ turn
    near = pl.multiple_of(down * (tile_rows - NEAR), 8)
    middle = jnp.where(down == 0, MIDDLE - PATCH, MIDDLE + tile_rows)
    plans = [
        taper_plan(middle, inverse_ref[1 - down]),
        taper_plan(middle + jnp.where(down == 0, -PATCH, PATCH).astype(f32), inverse_ref[down]),
    ]
    anomalies = [rows_ref[near + i] for i in range(NEAR)]
    fields = [held_ref[k, pl.ds(near, NEAR), :] for k in range(2)]
    blank = jnp.zeros(total_ref.shape[1:], f32)
    totals = [accumulate(blank, plan, anomalies, *fields, near) for plan in plans]
    for start in range(NEAR, FAR, STEP):
        anomalies = [rows_ref[start + i] for i in range(STEP)]
        fields = [held_ref[k, start : start + STEP, :] for k in range(2)]
        totals[0] = accumulate(totals[0], plans[0], anomalies, *fields, jnp.int32(start))
    total_ref[1 - down] = totals[0]
    total_ref[down] = totals[1]
    message_ref[...] = message_of(*paired([total_ref[0], total_ref[1]], members, patch_cols))


def outward_kernel(shares, *refs):
    parts, refs = refs[:shares], refs[shares:]
    sum_ref, field_ref, inverses, rows_ref, held_ref, messages, flat_ref, total_ref = (
        *refs[:2], refs[2:4], *refs[4:6], refs[6:8], *refs[8:]
    )
    share_members, tile_rows, cols = parts[0].shape
    members = share_members * shares
    lag = lax.axis_index("lag")
    states = [part[...].astype(f32) for part in parts]
    mean = functools.reduce(jnp.add, [jnp.sum(state, axis=0) for state in states[1:]], sum_ref[...]) / members
    for k, state in enumerate(states):
        at = pl.multiple_of(lax.rem(lag + k, shares) * (share_members * tile_rows), 8)
        flat_ref[pl.ds(at, share_members * tile_rows), :] = (state - mean[None]).reshape(-1, cols)
    weight = field_ref[0]
    held_ref[0] = weight
    held_ref[1] = field_ref[1] - mean * weight
    for r in range(tile_rows):
        rows_ref[r] = flat_ref[pl.ds(r, members, stride=tile_rows), :].astype(bf16)
    for turn in range(2):
        outward(turn, rows_ref, held_ref, inverses[turn], messages[turn], total_ref.at[turn])


def own_kernel(rows_ref, held_ref, inverse_ref, out_ref):
    tile_rows, members, cols = rows_ref.shape
    patch_cols = cols // PATCH
    plans = [taper_plan(MIDDLE + a * PATCH, inverse_ref[a]) for a in range(tile_rows // PATCH)]
    totals = [jnp.zeros((patch_cols * members + PATCH, members), f32) for _ in plans]
    for start in range(0, tile_rows, STEP):
        anomalies = [rows_ref[start + i] for i in range(STEP)]
        fields = [held_ref[k, start : start + STEP, :] for k in range(2)]
        totals = [accumulate(total, plan, anomalies, *fields, jnp.int32(start)) for total, plan in zip(totals, plans)]
    out_ref[...] = jnp.concatenate(paired(totals, members, patch_cols), 0)


def finish_kernel(total_ref, first_ref, second_ref, lag_ref, mean_ref, out_ref, flat_ref):
    tile_rows, members, cols = lag_ref.shape
    degree = members - 1.0
    pair_count = total_ref.shape[0] // members
    grams_end = pair_count * members
    wide = 2 * cols
    row = lax.broadcasted_iota(jnp.int32, (members, wide), 0)
    lane = lax.broadcasted_iota(jnp.int32, (members, wide), 1)
    identity = jnp.where(row == lane % members, 1.0, 0.0)
    left_mask = jnp.where(lane[:, :cols] < members, 1.0, 0.0).astype(bf16)
    right_mask = jnp.where(lane[:, :cols] < members, 0.0, 1.0).astype(bf16)
    nothing = jnp.zeros((2 * members, cols), bf16)

    def blocks(y):
        upper, lower = (jnp.concatenate([half * left_mask, half * right_mask], 0) for half in (y[:, :cols], y[:, cols:]))
        return jnp.concatenate(
            [jnp.concatenate([upper, nothing], 1), jnp.concatenate([nothing, lower], 1)], 0
        )

    def right(y):
        high, low = split(y)
        return blocks(high), blocks(low)

    def product(lefts, factor):
        high, low = factor
        rows = lefts[0][0].shape[0]
        first = mm(jnp.concatenate([part for pair in lefts for part in pair], 0), high)
        second = mm(jnp.concatenate([pair[0] for pair in lefts], 0), low)
        return [
            first[2 * k * rows : (2 * k + 1) * rows]
            + (first[(2 * k + 1) * rows : (2 * k + 2) * rows] + second[k * rows : (k + 1) * rows])
            for k in range(len(lefts))
        ]

    total = total_ref[...]
    tile, tiles = lax.axis_index("dom"), lax.axis_size("dom")
    for turn, ref in enumerate((first_ref, second_ref)):
        down = half_of_lags() ^ turn
        there = jnp.where(down == 1, tile > 0, tile < tiles - 1)
        total = total + jnp.where(there, read_message(ref, pair_count), 0.0)
    grams = [total[p * members : (p + 1) * members] for p in range(pair_count)]
    squares = jnp.concatenate([jnp.sum(gram * gram, axis=0, keepdims=True) for gram in grams], 0)
    at_left = lax.broadcasted_iota(jnp.int32, squares.shape, 1) < members
    norm_left = jnp.sum(jnp.where(at_left, squares, 0.0), axis=1, keepdims=True)
    norm_right = jnp.sum(jnp.where(at_left, 0.0, squares), axis=1, keepdims=True)
    bounds = degree + jnp.sqrt(jnp.where(at_left, norm_left, norm_right))
    quads = range(pair_count // 2)

    def beside(parts, q):
        return jnp.concatenate([parts[2 * q], parts[2 * q + 1]], 1)

    def rows_of(table):
        return [table[p : p + 1] for p in range(pair_count)]

    bound = [beside(rows_of(bounds), q) for q in quads]
    sides = [beside(rows_of(total[grams_end:]), q) for q in quads]
    iterates = [(beside(grams, q) + degree * identity) / bound[q] for q in quads]
    corrections = [1.5 * identity - 0.5 * iterates[q] for q in quads]
    factors = [right(corrections[q]) for q in quads]
    iterates = [product([split(iterates[q])], factors[q])[0] for q in quads]
    roots = corrections
    for step in range(1, NS_STEPS):
        halves = [split(roots[q]) for q in quads]
        corrections = [1.5 * identity - 0.5 * product([halves[q]], right(iterates[q]))[0] for q in quads]
        factors = [right(corrections[q]) for q in quads]
        if step < NS_STEPS - 1:
            both = [product([split(iterates[q]), halves[q]], factors[q]) for q in quads]
            iterates = [pair[0] for pair in both]
            roots = [pair[1] for pair in both]
        else:
            roots = [product([halves[q]], factors[q])[0] for q in quads]
    mixings = []
    for q in quads:
        factor = right(roots[q])
        side = jnp.broadcast_to(sides[q], (PATCH, wide))
        inner = product([split(side)], factor)[0]
        weights = product([split(inner)], factor)[0][:1] / bound[q]
        mixing = (jnp.sqrt(degree / bound[q]) * roots[q] + weights).astype(bf16)
        mixings += [mixing[:, :cols], mixing[:, cols:]]

    patch = lax.broadcasted_iota(jnp.int32, (members, cols), 1) // PATCH
    even = jnp.where(patch % 2 == 0, 1.0, 0.0).astype(bf16)
    odd = jnp.where(patch % 2 == 1, 1.0, 0.0).astype(bf16)
    per_row = cols // (2 * PATCH)
    for a in range(tile_rows // PATCH):
        mixing = jnp.concatenate(mixings[a * per_row : (a + 1) * per_row], 0)
        for r in range(a * PATCH, (a + 1) * PATCH, 2):
            state = jnp.concatenate(
                [jnp.concatenate([lag_ref[i] * even, lag_ref[i] * odd], 0) for i in (r, r + 1)], 1
            )
            spread_out = mm(mixing, state)
            for i in (0, 1):
                part = spread_out[:, i * cols : (i + 1) * cols]
                chosen = part[:members]
                for pair in range(1, per_row):
                    chosen = jnp.where(patch // 2 == pair, part[pair * members : (pair + 1) * members], chosen)
                flat_ref[pl.ds(r + i, members, stride=tile_rows), :] = chosen + mean_ref[r + i : r + i + 1, :]
    out_ref[...] = flat_ref[...].reshape(1, members, tile_rows, cols).astype(bf16)


def shards(history, forecast, spot, alive, levels, precision, radius):
    shares = lax.axis_size("lag")
    tiles = lax.axis_size("dom")
    share_members, tile_rows, cols = forecast.shape
    members = share_members * shares
    patch_cols = cols // PATCH
    def call(kernel, name, in_specs, out_shape, scratch=()):
        return pl.pallas_call(
            kernel,
            in_specs=in_specs,
            out_specs=jax.tree.map(lambda _: vmem, out_shape),
            out_shape=out_shape,
            scratch_shapes=scratch,
            compiler_params=pltpu.CompilerParams(vmem_limit_bytes=32 * 2**20),
            name=name,
        )

    shape = jax.ShapeDtypeStruct
    vmem = pl.BlockSpec(memory_space=pltpu.VMEM)
    parts = [forecast]
    for k in range(1, shares):
        parts.append(lax.ppermute(forecast, "lag", [((i + k) % shares, i) for i in range(shares)]))
    live = lax.broadcasted_iota(jnp.int32, spot.shape, 1) < alive[:, None]
    weights = jnp.where(live, precision, 0.0)
    kind = lax.broadcasted_iota(jnp.int32, (3, *spot.shape), 0)
    tables = jnp.where(kind == 0, weights[None], jnp.where(kind == 1, (weights * levels)[None], spot.astype(f32)[None]))
    inverse = jnp.broadcast_to(
        (1.0 / jnp.square(radius.astype(f32))).reshape(-1, patch_cols, 1), (tile_rows // PATCH, patch_cols, cols)
    )
    sent, tables = lax.optimization_barrier((inverse, tables))
    rings = [ring(tiles, shares, turn) for turn in range(2)]
    axes = ("dom", "lag")
    next_inverses = [lax.ppermute(sent, axes, [(t, s) for s, t in pairs]) for pairs in rings]
    fields, own_sum = call(
        functools.partial(fields_kernel, cols),
        "fields",
        [vmem, vmem],
        [shape((2, tile_rows, cols), f32), shape((tile_rows, cols), f32)],
    )(tables, forecast)
    pair_rows = patch_cols * members
    message_shape = shape((pair_rows + 2 * patch_cols, 2 * members), bf16)
    total_scratch = pltpu.VMEM((2, 2, patch_cols * members + PATCH, members), f32)
    rows, held, *messages = call(
        functools.partial(outward_kernel, shares),
        "outward_gram",
        [vmem] * (shares + 4),
        [shape((tile_rows, members, cols), bf16), shape((2, tile_rows, cols), f32), message_shape, message_shape],
        [pltpu.VMEM((members * tile_rows, cols), f32), total_scratch],
    )(*parts, own_sum, fields, *next_inverses)
    first, second = (lax.ppermute(message, axes, pairs) for message, pairs in zip(messages, rings))
    own = call(own_kernel, "own_gram", [vmem] * 3, shape((pair_rows + patch_cols, 2 * members), f32))(rows, held, inverse)
    lag_rows, lag_mean = call(
        state_kernel,
        "state",
        [vmem, vmem],
        [shape((tile_rows, members, cols), bf16), shape((tile_rows, cols), f32)],
        [pltpu.VMEM((members * tile_rows, cols), f32)],
    )(held, history[0])
    return call(
        finish_kernel,
        "finish",
        [vmem] * 5,
        shape((1, members, tile_rows, cols), bf16),
        [pltpu.VMEM((members * tile_rows, cols), f32)],
    )(own, first, second, lag_rows, lag_mean)


def solution(mesh):
    in_specs = (
        P("lag", None, "dom", None),
        P("lag", "dom", None),
        P("dom", None),
        P("dom"),
        P("dom", None),
        P("dom", None),
        P("dom"),
    )
    out_specs = P("lag", None, "dom", None)
    return jax.shard_map(shards, mesh=mesh, in_specs=in_specs, out_specs=out_specs, check_vma=False)
```

```python
import functools

import jax
import jax.numpy as jnp
from jax import lax
from jax.experimental import pallas as pl
from jax.experimental.pallas import tpu as pltpu
from jax.sharding import PartitionSpec as P

PATCH = 16
NS_STEPS = 4
RADIUS = 32
FAR = RADIUS - PATCH // 2
NEAR = FAR - PATCH
MIDDLE = (PATCH - 1) / 2

NT = (((1,), (1,)), ((), ()))
NN = (((1,), (0,)), ((), ()))
f32 = jnp.float32
bf16 = jnp.bfloat16


def mm(a, b, dims=NN):
    return lax.dot_general(a, b, dims, preferred_element_type=f32)


def split(x):
    high = x.astype(bf16)
    return high, (x - high.astype(f32)).astype(bf16)


def fields_kernel(cols, table_ref, part_ref, field_ref, sum_ref):
    sum_ref[...] = jnp.sum(part_ref[...].astype(f32), axis=0)
    patches, slots = table_ref.shape[1:]
    patch_cols = cols // PATCH
    patch_rows = patches // patch_cols
    spot = table_ref[2].astype(jnp.int32)
    row_in = spot // PATCH
    col_in = spot % PATCH
    iota_row = lax.broadcasted_iota(jnp.int32, (PATCH, slots), 0)
    iota_col = lax.broadcasted_iota(jnp.int32, (cols, slots), 0)
    for a in range(patch_rows):
        total = jnp.zeros((4 * PATCH, cols), f32)
        for b in range(patch_cols):
            p = a * patch_cols + b
            prec = table_ref[0, p : p + 1, :]
            level = table_ref[1, p : p + 1, :]
            prec_high = prec.astype(bf16).astype(f32)
            level_high = level.astype(bf16).astype(f32)
            on_row = row_in[p : p + 1, :] == iota_row
            pieces = [
                jnp.where(on_row, piece, 0.0).astype(bf16)
                for piece in (prec_high, prec - prec_high, level_high, level - level_high)
            ]
            on_col = jnp.where(col_in[p : p + 1, :] + b * PATCH == iota_col, 1.0, 0.0).astype(bf16)
            total = total + mm(jnp.concatenate(pieces, 0), on_col, NT)
        rows = slice(a * PATCH, (a + 1) * PATCH)
        field_ref[0, rows, :] = total[:PATCH] + total[PATCH : 2 * PATCH]
        field_ref[1, rows, :] = total[2 * PATCH : 3 * PATCH] + total[3 * PATCH :]


def state_kernel(after_ref, hist_ref, lag_ref, mean_ref, flat_ref):
    members, tile_rows, cols = hist_ref.shape
    state = hist_ref[...].astype(f32)
    mean = jnp.sum(state, axis=0) / members
    mean_ref[...] = mean
    flat_ref[...] = (state - mean[None]).reshape(members * tile_rows, cols)
    for r in range(tile_rows):
        lag_ref[r] = flat_ref[pl.ds(r, members, stride=tile_rows), :].astype(bf16)


def half_of_lags():
    return lax.axis_index("lag") // (lax.axis_size("lag") // 2)


def neighbour_pairs(tiles, shares):
    half = shares // 2
    straight, cross = [], []
    for t in range(tiles):
        for l in range(shares):
            other = (l + half) % shares
            target = t + (1 if l >= half else -1)
            inside = 0 <= target < tiles
            straight.append((t * shares + l, target * shares + l if inside else t * shares + other))
            cross.append((t * shares + l, target * shares + other if inside else t * shares + l))
    return straight, cross


def taper_plan(centre_row, inverse_square):
    q_row = lax.broadcasted_iota(jnp.int32, inverse_square.shape, 0)
    col = lax.broadcasted_iota(jnp.int32, inverse_square.shape, 1)
    col_square = jnp.square(col.astype(f32) - (q_row.astype(f32) * PATCH + MIDDLE))
    return centre_row, col_square, inverse_square


def accumulate(total, plan, anomalies, weight, innovation, first_row):
    centre_row, col_square, inverse_square = plan
    patches, cols = col_square.shape
    lefts = []
    for i, anomaly in enumerate(anomalies):
        members = anomaly.shape[0]
        offset = (first_row + i).astype(f32) - centre_row
        taper = jnp.square(jnp.maximum(0.0, 1.0 - (offset * offset + col_square) * inverse_square))
        scale = taper * weight[i : i + 1]
        blocks = anomaly.reshape(members // PATCH, PATCH, cols)
        left = [
            (blocks * jnp.broadcast_to(scale[q : q + 1], (PATCH, cols)).astype(bf16)[None]).reshape(members, cols)
            for q in range(patches)
        ]
        tail = taper * innovation[i : i + 1]
        left.append(jnp.concatenate([tail, jnp.zeros((PATCH - patches, cols), f32)], 0).astype(bf16))
        lefts.append(jnp.concatenate(left, 0))
    return total + mm(jnp.concatenate(lefts, 1), jnp.concatenate(anomalies, 1), NT)


STEP = 8


def paired(totals, members, patch_cols):
    pairs = patch_cols // 2
    grams, sides = [], []
    for total in totals:
        for pair in range(pairs):
            at = 2 * pair * members
            grams.append(jnp.concatenate([total[at : at + members], total[at + members : at + 2 * members]], 1))
        for pair in range(pairs):
            at = patch_cols * members + 2 * pair
            sides.append(jnp.concatenate([total[at : at + 1], total[at + 1 : at + 2]], 1))
    return jnp.concatenate(grams, 0), jnp.concatenate(sides, 0)


def message_of(grams, sides):
    return jnp.concatenate([grams.astype(bf16), *split(sides)], 0)


def read_message(ref, side_count):
    at = ref.shape[0] - 2 * side_count
    high, low = ref[at : at + side_count, :].astype(f32), ref[at + side_count :, :].astype(f32)
    return jnp.concatenate([ref[:at, :].astype(f32), high + low], 0)


def outward(rows_ref, held_ref, inverse_ref, message_ref, total_ref):
    tile_rows, members, cols = rows_ref.shape
    patch_cols = cols // PATCH
    down = half_of_lags()
    near = pl.multiple_of(down * (tile_rows - NEAR), 8)
    middle = jnp.where(down == 0, MIDDLE - PATCH, MIDDLE + tile_rows)
    plans = [
        taper_plan(middle, inverse_ref[1 - down]),
        taper_plan(middle + jnp.where(down == 0, -PATCH, PATCH).astype(f32), inverse_ref[down]),
    ]
    anomalies = [rows_ref[near + i] for i in range(NEAR)]
    fields = [held_ref[k, pl.ds(near, NEAR), :] for k in range(2)]
    blank = jnp.zeros(total_ref.shape[1:], f32)
    totals = [accumulate(blank, plan, anomalies, *fields, near) for plan in plans]
    for start in range(NEAR, FAR, STEP):
        anomalies = [rows_ref[start + i] for i in range(STEP)]
        fields = [held_ref[k, start : start + STEP, :] for k in range(2)]
        totals[0] = accumulate(totals[0], plans[0], anomalies, *fields, jnp.int32(start))
    total_ref[1 - down] = totals[0]
    total_ref[down] = totals[1]
    message_ref[...] = message_of(*paired([total_ref[0], total_ref[1]], members, patch_cols))


def outward_kernel(shares, *refs):
    parts, refs = refs[:shares], refs[shares:]
    sum_ref, field_ref, inverse_ref, rows_ref, held_ref, message_ref, flat_ref, total_ref = refs
    share_members, tile_rows, cols = parts[0].shape
    members = share_members * shares
    lag = lax.axis_index("lag")
    states = [part[...].astype(f32) for part in parts]
    mean = functools.reduce(jnp.add, [jnp.sum(state, axis=0) for state in states[1:]], sum_ref[...]) / members
    for k, state in enumerate(states):
        at = pl.multiple_of(lax.rem(lag + k, shares) * (share_members * tile_rows), 8)
        flat_ref[pl.ds(at, share_members * tile_rows), :] = (state - mean[None]).reshape(-1, cols)
    weight = field_ref[0]
    held_ref[0] = weight
    held_ref[1] = field_ref[1] - mean * weight
    for r in range(tile_rows):
        rows_ref[r] = flat_ref[pl.ds(r, members, stride=tile_rows), :].astype(bf16)
    outward(rows_ref, held_ref, inverse_ref, message_ref, total_ref)


def own_kernel(rows_ref, held_ref, inverse_ref, out_ref):
    tile_rows, members, cols = rows_ref.shape
    patch_cols = cols // PATCH
    plans = [taper_plan(MIDDLE + a * PATCH, inverse_ref[a]) for a in range(tile_rows // PATCH)]
    totals = [jnp.zeros((patch_cols * members + PATCH, members), f32) for _ in plans]
    for start in range(0, tile_rows, STEP):
        anomalies = [rows_ref[start + i] for i in range(STEP)]
        fields = [held_ref[k, start : start + STEP, :] for k in range(2)]
        totals = [accumulate(total, plan, anomalies, *fields, jnp.int32(start)) for total, plan in zip(totals, plans)]
    out_ref[...] = jnp.concatenate(paired(totals, members, patch_cols), 0)


def finish_kernel(total_ref, first_ref, second_ref, lag_ref, mean_ref, out_ref, flat_ref):
    tile_rows, members, cols = lag_ref.shape
    degree = members - 1.0
    pair_count = total_ref.shape[0] // members
    grams_end = pair_count * members
    wide = 2 * cols
    row = lax.broadcasted_iota(jnp.int32, (members, wide), 0)
    lane = lax.broadcasted_iota(jnp.int32, (members, wide), 1)
    identity = jnp.where(row == lane % members, 1.0, 0.0)
    left_mask = jnp.where(lane[:, :cols] < members, 1.0, 0.0).astype(bf16)
    right_mask = jnp.where(lane[:, :cols] < members, 0.0, 1.0).astype(bf16)
    nothing = jnp.zeros((2 * members, cols), bf16)

    def blocks(y):
        upper, lower = (jnp.concatenate([half * left_mask, half * right_mask], 0) for half in (y[:, :cols], y[:, cols:]))
        return jnp.concatenate(
            [jnp.concatenate([upper, nothing], 1), jnp.concatenate([nothing, lower], 1)], 0
        )

    def right(y):
        high, low = split(y)
        return blocks(high), blocks(low)

    def product(lefts, factor):
        high, low = factor
        rows = lefts[0][0].shape[0]
        first = mm(jnp.concatenate([part for pair in lefts for part in pair], 0), high)
        second = mm(jnp.concatenate([pair[0] for pair in lefts], 0), low)
        return [
            first[2 * k * rows : (2 * k + 1) * rows]
            + (first[(2 * k + 1) * rows : (2 * k + 2) * rows] + second[k * rows : (k + 1) * rows])
            for k in range(len(lefts))
        ]

    total = total_ref[...]
    tile, tiles = lax.axis_index("dom"), lax.axis_size("dom")
    for turn, ref in enumerate((first_ref, second_ref)):
        down = half_of_lags() ^ turn
        there = jnp.where(down == 1, tile > 0, tile < tiles - 1)
        total = total + jnp.where(there, read_message(ref, pair_count), 0.0)
    grams = [total[p * members : (p + 1) * members] for p in range(pair_count)]
    squares = jnp.concatenate([jnp.sum(gram * gram, axis=0, keepdims=True) for gram in grams], 0)
    at_left = lax.broadcasted_iota(jnp.int32, squares.shape, 1) < members
    norm_left = jnp.sum(jnp.where(at_left, squares, 0.0), axis=1, keepdims=True)
    norm_right = jnp.sum(jnp.where(at_left, 0.0, squares), axis=1, keepdims=True)
    bounds = degree + jnp.sqrt(jnp.where(at_left, norm_left, norm_right))
    quads = range(pair_count // 2)

    def beside(parts, q):
        return jnp.concatenate([parts[2 * q], parts[2 * q + 1]], 1)

    def rows_of(table):
        return [table[p : p + 1] for p in range(pair_count)]

    bound = [beside(rows_of(bounds), q) for q in quads]
    sides = [beside(rows_of(total[grams_end:]), q) for q in quads]
    iterates = [(beside(grams, q) + degree * identity) / bound[q] for q in quads]
    corrections = [1.5 * identity - 0.5 * iterates[q] for q in quads]
    factors = [right(corrections[q]) for q in quads]
    iterates = [product([split(iterates[q])], factors[q])[0] for q in quads]
    roots = corrections
    for step in range(1, NS_STEPS):
        halves = [split(roots[q]) for q in quads]
        corrections = [1.5 * identity - 0.5 * product([halves[q]], right(iterates[q]))[0] for q in quads]
        factors = [right(corrections[q]) for q in quads]
        if step < NS_STEPS - 1:
            both = [product([split(iterates[q]), halves[q]], factors[q]) for q in quads]
            iterates = [pair[0] for pair in both]
            roots = [pair[1] for pair in both]
        else:
            roots = [product([halves[q]], factors[q])[0] for q in quads]
    mixings = []
    for q in quads:
        factor = right(roots[q])
        side = jnp.broadcast_to(sides[q], (PATCH, wide))
        inner = product([split(side)], factor)[0]
        weights = product([split(inner)], factor)[0][:1] / bound[q]
        mixing = (jnp.sqrt(degree / bound[q]) * roots[q] + weights).astype(bf16)
        mixings += [mixing[:, :cols], mixing[:, cols:]]

    patch = lax.broadcasted_iota(jnp.int32, (members, cols), 1) // PATCH
    even = jnp.where(patch % 2 == 0, 1.0, 0.0).astype(bf16)
    odd = jnp.where(patch % 2 == 1, 1.0, 0.0).astype(bf16)
    per_row = cols // (2 * PATCH)
    for a in range(tile_rows // PATCH):
        mixing = jnp.concatenate(mixings[a * per_row : (a + 1) * per_row], 0)
        for r in range(a * PATCH, (a + 1) * PATCH, 2):
            state = jnp.concatenate(
                [jnp.concatenate([lag_ref[i] * even, lag_ref[i] * odd], 0) for i in (r, r + 1)], 1
            )
            spread_out = mm(mixing, state)
            for i in (0, 1):
                part = spread_out[:, i * cols : (i + 1) * cols]
                chosen = part[:members]
                for pair in range(1, per_row):
                    chosen = jnp.where(patch // 2 == pair, part[pair * members : (pair + 1) * members], chosen)
                flat_ref[pl.ds(r + i, members, stride=tile_rows), :] = chosen + mean_ref[r + i : r + i + 1, :]
    out_ref[...] = flat_ref[...].reshape(1, members, tile_rows, cols).astype(bf16)


def shards(history, forecast, spot, alive, levels, precision, radius):
    shares = lax.axis_size("lag")
    tiles = lax.axis_size("dom")
    share_members, tile_rows, cols = forecast.shape
    members = share_members * shares
    patch_cols = cols // PATCH
    def call(kernel, name, in_specs, out_shape, scratch=()):
        return pl.pallas_call(
            kernel,
            in_specs=in_specs,
            out_specs=jax.tree.map(lambda _: vmem, out_shape),
            out_shape=out_shape,
            scratch_shapes=scratch,
            compiler_params=pltpu.CompilerParams(vmem_limit_bytes=32 * 2**20),
            name=name,
        )

    shape = jax.ShapeDtypeStruct
    vmem = pl.BlockSpec(memory_space=pltpu.VMEM)
    parts = [forecast]
    for k in range(1, shares):
        parts.append(lax.ppermute(forecast, "lag", [((i + k) % shares, i) for i in range(shares)]))
    live = lax.broadcasted_iota(jnp.int32, spot.shape, 1) < alive[:, None]
    weights = jnp.where(live, precision, 0.0)
    kind = lax.broadcasted_iota(jnp.int32, (3, *spot.shape), 0)
    tables = jnp.where(kind == 0, weights[None], jnp.where(kind == 1, (weights * levels)[None], spot.astype(f32)[None]))
    inverse = jnp.broadcast_to(
        (1.0 / jnp.square(radius.astype(f32))).reshape(-1, patch_cols, 1), (tile_rows // PATCH, patch_cols, cols)
    )
    sent, tables = lax.optimization_barrier((inverse, tables))
    straight, cross = neighbour_pairs(tiles, shares)
    axes = ("dom", "lag")
    next_inverse = lax.ppermute(sent, axes, [(t, s) for s, t in straight])
    fields, own_sum = call(
        functools.partial(fields_kernel, cols),
        "fields",
        [vmem, vmem],
        [shape((2, tile_rows, cols), f32), shape((tile_rows, cols), f32)],
    )(tables, forecast)
    pair_rows = patch_cols * members
    message_shape = shape((pair_rows + 2 * patch_cols, 2 * members), bf16)
    total_scratch = pltpu.VMEM((2, patch_cols * members + PATCH, members), f32)
    rows, held, message = call(
        functools.partial(outward_kernel, shares),
        "outward_gram",
        [vmem] * (shares + 3),
        [shape((tile_rows, members, cols), bf16), shape((2, tile_rows, cols), f32), message_shape],
        [pltpu.VMEM((members * tile_rows, cols), f32), total_scratch],
    )(*parts, own_sum, fields, next_inverse)
    first, second = (lax.ppermute(message, axes, pairs) for pairs in (straight, cross))
    own = call(own_kernel, "own_gram", [vmem] * 3, shape((pair_rows + patch_cols, 2 * members), f32))(rows, held, inverse)
    lag_rows, lag_mean = call(
        state_kernel,
        "state",
        [vmem, vmem],
        [shape((tile_rows, members, cols), bf16), shape((tile_rows, cols), f32)],
        [pltpu.VMEM((members * tile_rows, cols), f32)],
    )(held, history[0])
    return call(
        finish_kernel,
        "finish",
        [vmem] * 5,
        shape((1, members, tile_rows, cols), bf16),
        [pltpu.VMEM((members * tile_rows, cols), f32)],
    )(own, first, second, lag_rows, lag_mean)


def solution(mesh):
    in_specs = (
        P("lag", None, "dom", None),
        P("lag", "dom", None),
        P("dom", None),
        P("dom"),
        P("dom", None),
        P("dom", None),
        P("dom"),
    )
    out_specs = P("lag", None, "dom", None)
    return jax.shard_map(shards, mesh=mesh, in_specs=in_specs, out_specs=out_specs, check_vma=False)
```

```python
import functools

import jax
import jax.numpy as jnp
from jax import lax
from jax.experimental import pallas as pl
from jax.experimental.pallas import tpu as pltpu
from jax.sharding import PartitionSpec as P

PATCH = 16
NS_STEPS = 4
RADIUS = 32
FAR = RADIUS - PATCH // 2
NEAR = FAR - PATCH
MIDDLE = (PATCH - 1) / 2

NT = (((1,), (1,)), ((), ()))
NN = (((1,), (0,)), ((), ()))
f32 = jnp.float32
bf16 = jnp.bfloat16


def mm(a, b, dims=NN):
    return lax.dot_general(a, b, dims, preferred_element_type=f32)


def split(x):
    high = x.astype(bf16)
    return high, (x - high.astype(f32)).astype(bf16)


def fields_kernel(cols, table_ref, part_ref, field_ref, sum_ref):
    sum_ref[...] = jnp.sum(part_ref[...].astype(f32), axis=0)
    patches, slots = table_ref.shape[1:]
    patch_cols = cols // PATCH
    patch_rows = patches // patch_cols
    spot = table_ref[2].astype(jnp.int32)
    row_in = spot // PATCH
    col_in = spot % PATCH
    iota_row = lax.broadcasted_iota(jnp.int32, (PATCH, slots), 0)
    iota_col = lax.broadcasted_iota(jnp.int32, (cols, slots), 0)
    for a in range(patch_rows):
        total = jnp.zeros((4 * PATCH, cols), f32)
        for b in range(patch_cols):
            p = a * patch_cols + b
            prec = table_ref[0, p : p + 1, :]
            level = table_ref[1, p : p + 1, :]
            prec_high = prec.astype(bf16).astype(f32)
            level_high = level.astype(bf16).astype(f32)
            on_row = row_in[p : p + 1, :] == iota_row
            pieces = [
                jnp.where(on_row, piece, 0.0).astype(bf16)
                for piece in (prec_high, prec - prec_high, level_high, level - level_high)
            ]
            on_col = jnp.where(col_in[p : p + 1, :] + b * PATCH == iota_col, 1.0, 0.0).astype(bf16)
            total = total + mm(jnp.concatenate(pieces, 0), on_col, NT)
        rows = slice(a * PATCH, (a + 1) * PATCH)
        field_ref[0, rows, :] = total[:PATCH] + total[PATCH : 2 * PATCH]
        field_ref[1, rows, :] = total[2 * PATCH : 3 * PATCH] + total[3 * PATCH :]


def state_kernel(after_ref, hist_ref, lag_ref, mean_ref, flat_ref):
    members, tile_rows, cols = hist_ref.shape
    state = hist_ref[...].astype(f32)
    mean = jnp.sum(state, axis=0) / members
    mean_ref[...] = mean
    flat_ref[...] = (state - mean[None]).reshape(members * tile_rows, cols)
    for r in range(tile_rows):
        lag_ref[r] = flat_ref[pl.ds(r, members, stride=tile_rows), :].astype(bf16)


def half_of_lags():
    return lax.axis_index("lag") // (lax.axis_size("lag") // 2)


def ring(tiles, shares, turn):
    half = shares // 2
    pairs = []
    for t in range(tiles):
        for l in range(shares):
            target = t + (1 if (l // half) ^ turn else -1)
            if 0 <= target < tiles:
                pairs.append((t * shares + l, target * shares + l))
            else:
                pairs.append((t * shares + l, t * shares + (l + half) % shares))
    return pairs


def taper_plan(centre_row, inverse_square):
    q_row = lax.broadcasted_iota(jnp.int32, inverse_square.shape, 0)
    col = lax.broadcasted_iota(jnp.int32, inverse_square.shape, 1)
    col_square = jnp.square(col.astype(f32) - (q_row.astype(f32) * PATCH + MIDDLE))
    return centre_row, col_square, inverse_square


def accumulate(total, plan, anomalies, weight, innovation, first_row):
    centre_row, col_square, inverse_square = plan
    patches, cols = col_square.shape
    lefts = []
    for i, anomaly in enumerate(anomalies):
        members = anomaly.shape[0]
        offset = (first_row + i).astype(f32) - centre_row
        taper = jnp.square(jnp.maximum(0.0, 1.0 - (offset * offset + col_square) * inverse_square))
        scale = taper * weight[i : i + 1]
        blocks = anomaly.reshape(members // PATCH, PATCH, cols)
        left = [
            (blocks * jnp.broadcast_to(scale[q : q + 1], (PATCH, cols)).astype(bf16)[None]).reshape(members, cols)
            for q in range(patches)
        ]
        tail = taper * innovation[i : i + 1]
        left.append(jnp.concatenate([tail, jnp.zeros((PATCH - patches, cols), f32)], 0).astype(bf16))
        lefts.append(jnp.concatenate(left, 0))
    return total + mm(jnp.concatenate(lefts, 1), jnp.concatenate(anomalies, 1), NT)


STEP = 8


def paired(totals, members, patch_cols):
    pairs = patch_cols // 2
    grams, sides = [], []
    for total in totals:
        for pair in range(pairs):
            at = 2 * pair * members
            grams.append(jnp.concatenate([total[at : at + members], total[at + members : at + 2 * members]], 1))
        for pair in range(pairs):
            at = patch_cols * members + 2 * pair
            sides.append(jnp.concatenate([total[at : at + 1], total[at + 1 : at + 2]], 1))
    return jnp.concatenate(grams, 0), jnp.concatenate(sides, 0)


def message_of(grams, sides):
    return jnp.concatenate([grams.astype(bf16), *split(sides)], 0)


def read_message(ref, side_count):
    at = ref.shape[0] - 2 * side_count
    high, low = ref[at : at + side_count, :].astype(f32), ref[at + side_count :, :].astype(f32)
    return jnp.concatenate([ref[:at, :].astype(f32), high + low], 0)


def arrived(ref, turn, side_count):
    tile = lax.axis_index("dom")
    there = jnp.where(half_of_lags() ^ turn == 1, tile > 0, tile < lax.axis_size("dom") - 1)
    return jnp.where(there, read_message(ref, side_count), 0.0)


def outward(turn, rows_ref, held_ref, inverse_ref, message_ref, total_ref):
    tile_rows, members, cols = rows_ref.shape
    patch_cols = cols // PATCH
    down = half_of_lags() ^ turn
    near = pl.multiple_of(down * (tile_rows - NEAR), 8)
    middle = jnp.where(down == 0, MIDDLE - PATCH, MIDDLE + tile_rows)
    plans = [
        taper_plan(middle, inverse_ref[1 - down]),
        taper_plan(middle + jnp.where(down == 0, -PATCH, PATCH).astype(f32), inverse_ref[down]),
    ]
    anomalies = [rows_ref[near + i] for i in range(NEAR)]
    fields = [held_ref[k, pl.ds(near, NEAR), :] for k in range(2)]
    blank = jnp.zeros(total_ref.shape[1:], f32)
    totals = [accumulate(blank, plan, anomalies, *fields, near) for plan in plans]
    for start in range(NEAR, FAR, STEP):
        anomalies = [rows_ref[start + i] for i in range(STEP)]
        fields = [held_ref[k, start : start + STEP, :] for k in range(2)]
        totals[0] = accumulate(totals[0], plans[0], anomalies, *fields, jnp.int32(start))
    total_ref[1 - down] = totals[0]
    total_ref[down] = totals[1]
    message_ref[...] = message_of(*paired([total_ref[0], total_ref[1]], members, patch_cols))


def first_kernel(shares, *refs):
    parts, refs = refs[:shares], refs[shares:]
    sum_ref, field_ref, inverse_ref, rows_ref, held_ref, message_ref, flat_ref, total_ref = refs
    share_members, tile_rows, cols = parts[0].shape
    members = share_members * shares
    lag = lax.axis_index("lag")
    states = [part[...].astype(f32) for part in parts]
    mean = functools.reduce(jnp.add, [jnp.sum(state, axis=0) for state in states[1:]], sum_ref[...]) / members
    for k, state in enumerate(states):
        at = pl.multiple_of(lax.rem(lag + k, shares) * (share_members * tile_rows), 8)
        flat_ref[pl.ds(at, share_members * tile_rows), :] = (state - mean[None]).reshape(-1, cols)
    weight = field_ref[0]
    held_ref[0] = weight
    held_ref[1] = field_ref[1] - mean * weight
    for r in range(tile_rows):
        rows_ref[r] = flat_ref[pl.ds(r, members, stride=tile_rows), :].astype(bf16)
    outward(0, rows_ref, held_ref, inverse_ref, message_ref, total_ref)


def second_kernel(rows_ref, held_ref, inverse_ref, message_ref, total_ref):
    outward(1, rows_ref, held_ref, inverse_ref, message_ref, total_ref)


def own_kernel(after_ref, rows_ref, held_ref, inverse_ref, first_ref, out_ref):
    tile_rows, members, cols = rows_ref.shape
    patch_cols = cols // PATCH
    plans = [taper_plan(MIDDLE + a * PATCH, inverse_ref[a]) for a in range(tile_rows // PATCH)]
    totals = [jnp.zeros((patch_cols * members + PATCH, members), f32) for _ in plans]
    for start in range(0, tile_rows, STEP):
        anomalies = [rows_ref[start + i] for i in range(STEP)]
        fields = [held_ref[k, start : start + STEP, :] for k in range(2)]
        totals = [accumulate(total, plan, anomalies, *fields, jnp.int32(start)) for total, plan in zip(totals, plans)]
    sums = jnp.concatenate(paired(totals, members, patch_cols), 0)
    out_ref[...] = sums + arrived(first_ref, 0, patch_cols)


def finish_kernel(total_ref, second_ref, lag_ref, mean_ref, out_ref, flat_ref):
    tile_rows, members, cols = lag_ref.shape
    degree = members - 1.0
    pair_count = total_ref.shape[0] // members
    grams_end = pair_count * members
    wide = 2 * cols
    row = lax.broadcasted_iota(jnp.int32, (members, wide), 0)
    lane = lax.broadcasted_iota(jnp.int32, (members, wide), 1)
    identity = jnp.where(row == lane % members, 1.0, 0.0)
    left_mask = jnp.where(lane[:, :cols] < members, 1.0, 0.0).astype(bf16)
    right_mask = jnp.where(lane[:, :cols] < members, 0.0, 1.0).astype(bf16)
    nothing = jnp.zeros((2 * members, cols), bf16)

    def blocks(y):
        upper, lower = (jnp.concatenate([half * left_mask, half * right_mask], 0) for half in (y[:, :cols], y[:, cols:]))
        return jnp.concatenate(
            [jnp.concatenate([upper, nothing], 1), jnp.concatenate([nothing, lower], 1)], 0
        )

    def right(y):
        high, low = split(y)
        return blocks(high), blocks(low)

    def product(lefts, factor):
        high, low = factor
        rows = lefts[0][0].shape[0]
        first = mm(jnp.concatenate([part for pair in lefts for part in pair], 0), high)
        second = mm(jnp.concatenate([pair[0] for pair in lefts], 0), low)
        return [
            first[2 * k * rows : (2 * k + 1) * rows]
            + (first[(2 * k + 1) * rows : (2 * k + 2) * rows] + second[k * rows : (k + 1) * rows])
            for k in range(len(lefts))
        ]

    total = total_ref[...] + arrived(second_ref, 1, pair_count)
    grams = [total[p * members : (p + 1) * members] for p in range(pair_count)]
    squares = jnp.concatenate([jnp.sum(gram * gram, axis=0, keepdims=True) for gram in grams], 0)
    at_left = lax.broadcasted_iota(jnp.int32, squares.shape, 1) < members
    norm_left = jnp.sum(jnp.where(at_left, squares, 0.0), axis=1, keepdims=True)
    norm_right = jnp.sum(jnp.where(at_left, 0.0, squares), axis=1, keepdims=True)
    bounds = degree + jnp.sqrt(jnp.where(at_left, norm_left, norm_right))
    quads = range(pair_count // 2)

    def beside(parts, q):
        return jnp.concatenate([parts[2 * q], parts[2 * q + 1]], 1)

    def rows_of(table):
        return [table[p : p + 1] for p in range(pair_count)]

    bound = [beside(rows_of(bounds), q) for q in quads]
    sides = [beside(rows_of(total[grams_end:]), q) for q in quads]
    iterates = [(beside(grams, q) + degree * identity) / bound[q] for q in quads]
    corrections = [1.5 * identity - 0.5 * iterates[q] for q in quads]
    factors = [right(corrections[q]) for q in quads]
    iterates = [product([split(iterates[q])], factors[q])[0] for q in quads]
    roots = corrections
    for step in range(1, NS_STEPS):
        halves = [split(roots[q]) for q in quads]
        corrections = [1.5 * identity - 0.5 * product([halves[q]], right(iterates[q]))[0] for q in quads]
        factors = [right(corrections[q]) for q in quads]
        if step < NS_STEPS - 1:
            both = [product([split(iterates[q]), halves[q]], factors[q]) for q in quads]
            iterates = [pair[0] for pair in both]
            roots = [pair[1] for pair in both]
        else:
            roots = [product([halves[q]], factors[q])[0] for q in quads]
    mixings = []
    for q in quads:
        factor = right(roots[q])
        side = jnp.broadcast_to(sides[q], (PATCH, wide))
        inner = product([split(side)], factor)[0]
        weights = product([split(inner)], factor)[0][:1] / bound[q]
        mixing = (jnp.sqrt(degree / bound[q]) * roots[q] + weights).astype(bf16)
        mixings += [mixing[:, :cols], mixing[:, cols:]]

    patch = lax.broadcasted_iota(jnp.int32, (members, cols), 1) // PATCH
    even = jnp.where(patch % 2 == 0, 1.0, 0.0).astype(bf16)
    odd = jnp.where(patch % 2 == 1, 1.0, 0.0).astype(bf16)
    per_row = cols // (2 * PATCH)
    for a in range(tile_rows // PATCH):
        mixing = jnp.concatenate(mixings[a * per_row : (a + 1) * per_row], 0)
        for r in range(a * PATCH, (a + 1) * PATCH, 2):
            state = jnp.concatenate(
                [jnp.concatenate([lag_ref[i] * even, lag_ref[i] * odd], 0) for i in (r, r + 1)], 1
            )
            spread_out = mm(mixing, state)
            for i in (0, 1):
                part = spread_out[:, i * cols : (i + 1) * cols]
                chosen = part[:members]
                for pair in range(1, per_row):
                    chosen = jnp.where(patch // 2 == pair, part[pair * members : (pair + 1) * members], chosen)
                flat_ref[pl.ds(r + i, members, stride=tile_rows), :] = chosen + mean_ref[r + i : r + i + 1, :]
    out_ref[...] = flat_ref[...].reshape(1, members, tile_rows, cols).astype(bf16)


def shards(history, forecast, spot, alive, levels, precision, radius):
    shares = lax.axis_size("lag")
    tiles = lax.axis_size("dom")
    share_members, tile_rows, cols = forecast.shape
    members = share_members * shares
    patch_cols = cols // PATCH
    def call(kernel, name, in_specs, out_shape, scratch=()):
        return pl.pallas_call(
            kernel,
            in_specs=in_specs,
            out_specs=jax.tree.map(lambda _: vmem, out_shape),
            out_shape=out_shape,
            scratch_shapes=scratch,
            compiler_params=pltpu.CompilerParams(vmem_limit_bytes=32 * 2**20),
            name=name,
        )

    shape = jax.ShapeDtypeStruct
    vmem = pl.BlockSpec(memory_space=pltpu.VMEM)
    parts = [forecast]
    for k in range(1, shares):
        parts.append(lax.ppermute(forecast, "lag", [((i + k) % shares, i) for i in range(shares)]))
    live = lax.broadcasted_iota(jnp.int32, spot.shape, 1) < alive[:, None]
    weights = jnp.where(live, precision, 0.0)
    kind = lax.broadcasted_iota(jnp.int32, (3, *spot.shape), 0)
    tables = jnp.where(kind == 0, weights[None], jnp.where(kind == 1, (weights * levels)[None], spot.astype(f32)[None]))
    inverse = jnp.broadcast_to(
        (1.0 / jnp.square(radius.astype(f32))).reshape(-1, patch_cols, 1), (tile_rows // PATCH, patch_cols, cols)
    )
    sent, tables = lax.optimization_barrier((inverse, tables))
    rings = [ring(tiles, shares, turn) for turn in range(2)]
    axes = ("dom", "lag")
    next_inverses = [lax.ppermute(sent, axes, [(t, s) for s, t in pairs]) for pairs in rings]
    fields, own_sum = call(
        functools.partial(fields_kernel, cols),
        "fields",
        [vmem, vmem],
        [shape((2, tile_rows, cols), f32), shape((tile_rows, cols), f32)],
    )(tables, forecast)
    pair_rows = patch_cols * members
    message_shape = shape((pair_rows + 2 * patch_cols, 2 * members), bf16)
    total_scratch = pltpu.VMEM((2, patch_cols * members + PATCH, members), f32)
    rows, held, message = call(
        functools.partial(first_kernel, shares),
        "first_gram",
        [vmem] * (shares + 3),
        [shape((tile_rows, members, cols), bf16), shape((2, tile_rows, cols), f32), message_shape],
        [pltpu.VMEM((members * tile_rows, cols), f32), total_scratch],
    )(*parts, own_sum, fields, next_inverses[0])
    first = lax.ppermute(message, axes, rings[0])
    message = call(second_kernel, "second_gram", [vmem] * 3, message_shape, [total_scratch])(rows, held, next_inverses[1])
    second = lax.ppermute(message, axes, rings[1])
    lag_rows, lag_mean = call(
        state_kernel,
        "state",
        [vmem, vmem],
        [shape((tile_rows, members, cols), bf16), shape((tile_rows, cols), f32)],
        [pltpu.VMEM((members * tile_rows, cols), f32)],
    )(held, history[0])
    own_shape = shape((pair_rows + patch_cols, 2 * members), f32)
    own = call(own_kernel, "own_gram", [vmem] * 5, own_shape)(lag_mean, rows, held, inverse, first)
    return call(
        finish_kernel,
        "finish",
        [vmem] * 4,
        shape((1, members, tile_rows, cols), bf16),
        [pltpu.VMEM((members * tile_rows, cols), f32)],
    )(own, second, lag_rows, lag_mean)


def solution(mesh):
    in_specs = (
        P("lag", None, "dom", None),
        P("lag", "dom", None),
        P("dom", None),
        P("dom"),
        P("dom", None),
        P("dom", None),
        P("dom"),
    )
    out_specs = P("lag", None, "dom", None)
    return jax.shard_map(shards, mesh=mesh, in_specs=in_specs, out_specs=out_specs, check_vma=False)
```

```python
import functools

import jax
import jax.numpy as jnp
from jax import lax
from jax.experimental import pallas as pl
from jax.experimental.pallas import tpu as pltpu
from jax.sharding import PartitionSpec as P

PATCH = 16
NS_STEPS = 4
RADIUS = 32
FAR = RADIUS - PATCH // 2
NEAR = FAR - PATCH
MIDDLE = (PATCH - 1) / 2

NT = (((1,), (1,)), ((), ()))
NN = (((1,), (0,)), ((), ()))
f32 = jnp.float32
bf16 = jnp.bfloat16


def mm(a, b, dims=NN):
    return lax.dot_general(a, b, dims, preferred_element_type=f32)


def split(x):
    high = x.astype(bf16)
    return high, (x - high.astype(f32)).astype(bf16)


def fields_kernel(cols, table_ref, part_ref, field_ref, sum_ref):
    sum_ref[...] = jnp.sum(part_ref[...].astype(f32), axis=0)
    patches, slots = table_ref.shape[1:]
    patch_cols = cols // PATCH
    patch_rows = patches // patch_cols
    spot = table_ref[2].astype(jnp.int32)
    row_in = spot // PATCH
    col_in = spot % PATCH
    iota_row = lax.broadcasted_iota(jnp.int32, (PATCH, slots), 0)
    iota_col = lax.broadcasted_iota(jnp.int32, (cols, slots), 0)
    for a in range(patch_rows):
        total = jnp.zeros((4 * PATCH, cols), f32)
        for b in range(patch_cols):
            p = a * patch_cols + b
            prec = table_ref[0, p : p + 1, :]
            level = table_ref[1, p : p + 1, :]
            prec_high = prec.astype(bf16).astype(f32)
            level_high = level.astype(bf16).astype(f32)
            on_row = row_in[p : p + 1, :] == iota_row
            pieces = [
                jnp.where(on_row, piece, 0.0).astype(bf16)
                for piece in (prec_high, prec - prec_high, level_high, level - level_high)
            ]
            on_col = jnp.where(col_in[p : p + 1, :] + b * PATCH == iota_col, 1.0, 0.0).astype(bf16)
            total = total + mm(jnp.concatenate(pieces, 0), on_col, NT)
        rows = slice(a * PATCH, (a + 1) * PATCH)
        field_ref[0, rows, :] = total[:PATCH] + total[PATCH : 2 * PATCH]
        field_ref[1, rows, :] = total[2 * PATCH : 3 * PATCH] + total[3 * PATCH :]


def state_kernel(after_ref, hist_ref, lag_ref, mean_ref, flat_ref):
    members, tile_rows, cols = hist_ref.shape
    state = hist_ref[...].astype(f32)
    mean = jnp.sum(state, axis=0) / members
    mean_ref[...] = mean
    flat_ref[...] = (state - mean[None]).reshape(members * tile_rows, cols)
    for r in range(tile_rows):
        lag_ref[r] = flat_ref[pl.ds(r, members, stride=tile_rows), :].astype(bf16)


def half_of_lags():
    return lax.axis_index("lag") // (lax.axis_size("lag") // 2)


def ring(tiles, shares, turn):
    half = shares // 2
    pairs = []
    for t in range(tiles):
        for l in range(shares):
            target = t + (1 if (l // half) ^ turn else -1)
            if 0 <= target < tiles:
                pairs.append((t * shares + l, target * shares + l))
            else:
                pairs.append((t * shares + l, t * shares + (l + half) % shares))
    return pairs


def taper_plan(centre_row, inverse_square):
    q_row = lax.broadcasted_iota(jnp.int32, inverse_square.shape, 0)
    col = lax.broadcasted_iota(jnp.int32, inverse_square.shape, 1)
    col_square = jnp.square(col.astype(f32) - (q_row.astype(f32) * PATCH + MIDDLE))
    return centre_row, col_square, inverse_square


def accumulate(total, plan, anomalies, weight, innovation, first_row):
    centre_row, col_square, inverse_square = plan
    patches, cols = col_square.shape
    lefts = []
    for i, anomaly in enumerate(anomalies):
        members = anomaly.shape[0]
        offset = (first_row + i).astype(f32) - centre_row
        taper = jnp.square(jnp.maximum(0.0, 1.0 - (offset * offset + col_square) * inverse_square))
        scale = taper * weight[i : i + 1]
        blocks = anomaly.reshape(members // PATCH, PATCH, cols)
        left = [
            (blocks * jnp.broadcast_to(scale[q : q + 1], (PATCH, cols)).astype(bf16)[None]).reshape(members, cols)
            for q in range(patches)
        ]
        tail = taper * innovation[i : i + 1]
        left.append(jnp.concatenate([tail, jnp.zeros((PATCH - patches, cols), f32)], 0).astype(bf16))
        lefts.append(jnp.concatenate(left, 0))
    return total + mm(jnp.concatenate(lefts, 1), jnp.concatenate(anomalies, 1), NT)


STEP = 8


def paired(totals, members, patch_cols):
    pairs = patch_cols // 2
    grams, sides = [], []
    for total in totals:
        for pair in range(pairs):
            at = 2 * pair * members
            grams.append(jnp.concatenate([total[at : at + members], total[at + members : at + 2 * members]], 1))
        for pair in range(pairs):
            at = patch_cols * members + 2 * pair
            sides.append(jnp.concatenate([total[at : at + 1], total[at + 1 : at + 2]], 1))
    return jnp.concatenate(grams, 0), jnp.concatenate(sides, 0)


def message_of(grams, sides):
    return jnp.concatenate([grams.astype(bf16), *split(sides)], 0)


def read_message(ref, side_count):
    at = ref.shape[0] - 2 * side_count
    high, low = ref[at : at + side_count, :].astype(f32), ref[at + side_count :, :].astype(f32)
    return jnp.concatenate([ref[:at, :].astype(f32), high + low], 0)


def arrived(ref, turn, side_count):
    tile = lax.axis_index("dom")
    there = jnp.where(half_of_lags() ^ turn == 1, tile > 0, tile < lax.axis_size("dom") - 1)
    return jnp.where(there, read_message(ref, side_count), 0.0)


def outward(turn, rows_ref, held_ref, inverse_ref, message_ref, total_ref):
    tile_rows, members, cols = rows_ref.shape
    patch_cols = cols // PATCH
    down = half_of_lags() ^ turn
    near = pl.multiple_of(down * (tile_rows - NEAR), 8)
    middle = jnp.where(down == 0, MIDDLE - PATCH, MIDDLE + tile_rows)
    plans = [
        taper_plan(middle, inverse_ref[1 - down]),
        taper_plan(middle + jnp.where(down == 0, -PATCH, PATCH).astype(f32), inverse_ref[down]),
    ]
    anomalies = [rows_ref[near + i] for i in range(NEAR)]
    fields = [held_ref[k, pl.ds(near, NEAR), :] for k in range(2)]
    blank = jnp.zeros(total_ref.shape[1:], f32)
    totals = [accumulate(blank, plan, anomalies, *fields, near) for plan in plans]
    for start in range(NEAR, FAR, STEP):
        anomalies = [rows_ref[start + i] for i in range(STEP)]
        fields = [held_ref[k, start : start + STEP, :] for k in range(2)]
        totals[0] = accumulate(totals[0], plans[0], anomalies, *fields, jnp.int32(start))
    total_ref[1 - down] = totals[0]
    total_ref[down] = totals[1]
    message_ref[...] = message_of(*paired([total_ref[0], total_ref[1]], members, patch_cols))


def first_kernel(shares, *refs):
    parts, refs = refs[:shares], refs[shares:]
    sum_ref, field_ref, inverse_ref, rows_ref, held_ref, message_ref, flat_ref, total_ref = refs
    share_members, tile_rows, cols = parts[0].shape
    members = share_members * shares
    lag = lax.axis_index("lag")
    states = [part[...].astype(f32) for part in parts]
    mean = functools.reduce(jnp.add, [jnp.sum(state, axis=0) for state in states[1:]], sum_ref[...]) / members
    for k, state in enumerate(states):
        at = pl.multiple_of(lax.rem(lag + k, shares) * (share_members * tile_rows), 8)
        flat_ref[pl.ds(at, share_members * tile_rows), :] = (state - mean[None]).reshape(-1, cols)
    weight = field_ref[0]
    held_ref[0] = weight
    held_ref[1] = field_ref[1] - mean * weight
    for r in range(tile_rows):
        rows_ref[r] = flat_ref[pl.ds(r, members, stride=tile_rows), :].astype(bf16)
    outward(0, rows_ref, held_ref, inverse_ref, message_ref, total_ref)


def second_kernel(rows_ref, held_ref, inverse_ref, message_ref, total_ref):
    outward(1, rows_ref, held_ref, inverse_ref, message_ref, total_ref)


def own_kernel(after_ref, rows_ref, held_ref, inverse_ref, first_ref, out_ref):
    tile_rows, members, cols = rows_ref.shape
    patch_cols = cols // PATCH
    plans = [taper_plan(MIDDLE + a * PATCH, inverse_ref[a]) for a in range(tile_rows // PATCH)]
    totals = [jnp.zeros((patch_cols * members + PATCH, members), f32) for _ in plans]
    for start in range(0, tile_rows, STEP):
        anomalies = [rows_ref[start + i] for i in range(STEP)]
        fields = [held_ref[k, start : start + STEP, :] for k in range(2)]
        totals = [accumulate(total, plan, anomalies, *fields, jnp.int32(start)) for total, plan in zip(totals, plans)]
    sums = jnp.concatenate(paired(totals, members, patch_cols), 0)
    out_ref[...] = sums + arrived(first_ref, 0, patch_cols)


def finish_kernel(total_ref, second_ref, lag_ref, mean_ref, out_ref, flat_ref):
    tile_rows, members, cols = lag_ref.shape
    degree = members - 1.0
    pair_count = total_ref.shape[0] // members
    grams_end = pair_count * members
    row = lax.broadcasted_iota(jnp.int32, (members, cols), 0)
    lane = lax.broadcasted_iota(jnp.int32, (members, cols), 1)
    identity = jnp.where(row == lane % members, 1.0, 0.0)
    left_mask = jnp.where(lane < members, 1.0, 0.0).astype(bf16)
    right_mask = jnp.where(lane < members, 0.0, 1.0).astype(bf16)

    def right(y):
        halves = split(y)
        return jnp.concatenate(
            [jnp.concatenate([half * mask for half in halves], 1) for mask in (left_mask, right_mask)], 0
        )

    def product(lefts, factor):
        both = mm(jnp.concatenate([half for halves in lefts for half in halves], 0), factor)
        results, at = [], 0
        for high, low in lefts:
            rows = high.shape[0]
            upper, lower = both[at : at + rows], both[at + rows : at + 2 * rows]
            results.append(upper[:, :cols] + (upper[:, cols:] + lower[:, :cols]))
            at += 2 * rows
        return results

    total = total_ref[...] + arrived(second_ref, 1, pair_count)
    pairs = range(pair_count)
    grams = [total[p * members : (p + 1) * members] for p in pairs]
    squares = jnp.concatenate([jnp.sum(gram * gram, axis=0, keepdims=True) for gram in grams], 0)
    at_left = lax.broadcasted_iota(jnp.int32, squares.shape, 1) < members
    norm_left = jnp.sum(jnp.where(at_left, squares, 0.0), axis=1, keepdims=True)
    norm_right = jnp.sum(jnp.where(at_left, 0.0, squares), axis=1, keepdims=True)
    bounds = degree + jnp.sqrt(jnp.where(at_left, norm_left, norm_right))
    inverses = 1.0 / bounds
    spreads = jnp.sqrt(degree * inverses)
    sides = [jnp.broadcast_to(total[grams_end + p : grams_end + p + 1], (PATCH, cols)) for p in pairs]
    iterates = [(grams[p] + degree * identity) * inverses[p : p + 1] for p in pairs]
    roots = [None for _ in pairs]
    for step in range(NS_STEPS):
        for p in pairs:
            iterate = split(iterates[p])
            root = None if step == 0 else split(roots[p])
            ahead = iterates[p] if step == 0 else product([root], right(iterates[p]))[0]
            correction = 1.5 * identity - 0.5 * ahead
            lefts = [split(sides[p])]
            if step > 0:
                lefts.append(root)
            if step < NS_STEPS - 1:
                lefts.append(iterate)
            results = product(lefts, right(correction))
            sides[p] = results[0]
            roots[p] = correction if step == 0 else results[1]
            if step < NS_STEPS - 1:
                iterates[p] = results[-1]
    mixings = []
    for p in pairs:
        weights = product([split(sides[p])], right(roots[p]))[0][:1] * inverses[p : p + 1]
        mixings.append((spreads[p : p + 1] * roots[p] + weights).astype(bf16))

    patch = lax.broadcasted_iota(jnp.int32, (members, cols), 1) // PATCH
    masks = [jnp.where(patch % 4 == k, 1.0, 0.0).astype(bf16) for k in range(4)]
    quads = cols // (4 * PATCH)
    for a in range(tile_rows // PATCH):
        mixing = jnp.concatenate(
            [jnp.concatenate(mixings[2 * q : 2 * q + 2], 1) for q in range(a * quads, (a + 1) * quads)], 0
        )
        for r in range(a * PATCH, (a + 1) * PATCH, 2):
            state = jnp.concatenate(
                [jnp.concatenate([lag_ref[i] * mask for mask in masks], 0) for i in (r, r + 1)], 1
            )
            spread_out = mm(mixing, state)
            for i in (0, 1):
                part = spread_out[:, i * cols : (i + 1) * cols]
                chosen = part[:members]
                for q in range(1, quads):
                    chosen = jnp.where(patch // 4 == q, part[q * members : (q + 1) * members], chosen)
                flat_ref[pl.ds(r + i, members, stride=tile_rows), :] = chosen + mean_ref[r + i : r + i + 1, :]
    out_ref[...] = flat_ref[...].reshape(1, members, tile_rows, cols).astype(bf16)


def shards(history, forecast, spot, alive, levels, precision, radius):
    shares = lax.axis_size("lag")
    tiles = lax.axis_size("dom")
    share_members, tile_rows, cols = forecast.shape
    members = share_members * shares
    patch_cols = cols // PATCH
    def call(kernel, name, in_specs, out_shape, scratch=()):
        return pl.pallas_call(
            kernel,
            in_specs=in_specs,
            out_specs=jax.tree.map(lambda _: vmem, out_shape),
            out_shape=out_shape,
            scratch_shapes=scratch,
            compiler_params=pltpu.CompilerParams(vmem_limit_bytes=32 * 2**20),
            name=name,
        )

    shape = jax.ShapeDtypeStruct
    vmem = pl.BlockSpec(memory_space=pltpu.VMEM)
    parts = [forecast]
    for k in range(1, shares):
        parts.append(lax.ppermute(forecast, "lag", [((i + k) % shares, i) for i in range(shares)]))
    live = lax.broadcasted_iota(jnp.int32, spot.shape, 1) < alive[:, None]
    weights = jnp.where(live, precision, 0.0)
    kind = lax.broadcasted_iota(jnp.int32, (3, *spot.shape), 0)
    tables = jnp.where(kind == 0, weights[None], jnp.where(kind == 1, (weights * levels)[None], spot.astype(f32)[None]))
    inverse = jnp.broadcast_to(
        (1.0 / jnp.square(radius.astype(f32))).reshape(-1, patch_cols, 1), (tile_rows // PATCH, patch_cols, cols)
    )
    sent, tables = lax.optimization_barrier((inverse, tables))
    rings = [ring(tiles, shares, turn) for turn in range(2)]
    axes = ("dom", "lag")
    next_inverses = [lax.ppermute(sent, axes, [(t, s) for s, t in pairs]) for pairs in rings]
    fields, own_sum = call(
        functools.partial(fields_kernel, cols),
        "fields",
        [vmem, vmem],
        [shape((2, tile_rows, cols), f32), shape((tile_rows, cols), f32)],
    )(tables, forecast)
    pair_rows = patch_cols * members
    message_shape = shape((pair_rows + 2 * patch_cols, 2 * members), bf16)
    total_scratch = pltpu.VMEM((2, patch_cols * members + PATCH, members), f32)
    rows, held, message = call(
        functools.partial(first_kernel, shares),
        "first_gram",
        [vmem] * (shares + 3),
        [shape((tile_rows, members, cols), bf16), shape((2, tile_rows, cols), f32), message_shape],
        [pltpu.VMEM((members * tile_rows, cols), f32), total_scratch],
    )(*parts, own_sum, fields, next_inverses[0])
    first = lax.ppermute(message, axes, rings[0])
    message = call(second_kernel, "second_gram", [vmem] * 3, message_shape, [total_scratch])(rows, held, next_inverses[1])
    second = lax.ppermute(message, axes, rings[1])
    lag_rows, lag_mean = call(
        state_kernel,
        "state",
        [vmem, vmem],
        [shape((tile_rows, members, cols), bf16), shape((tile_rows, cols), f32)],
        [pltpu.VMEM((members * tile_rows, cols), f32)],
    )(held, history[0])
    own_shape = shape((pair_rows + patch_cols, 2 * members), f32)
    own = call(own_kernel, "own_gram", [vmem] * 5, own_shape)(lag_mean, rows, held, inverse, first)
    return call(
        finish_kernel,
        "finish",
        [vmem] * 4,
        shape((1, members, tile_rows, cols), bf16),
        [pltpu.VMEM((members * tile_rows, cols), f32)],
    )(own, second, lag_rows, lag_mean)


def solution(mesh):
    in_specs = (
        P("lag", None, "dom", None),
        P("lag", "dom", None),
        P("dom", None),
        P("dom"),
        P("dom", None),
        P("dom", None),
        P("dom"),
    )
    out_specs = P("lag", None, "dom", None)
    return jax.shard_map(shards, mesh=mesh, in_specs=in_specs, out_specs=out_specs, check_vma=False)
```

```python
import functools

import jax
import jax.numpy as jnp
from jax import lax
from jax.experimental import pallas as pl
from jax.experimental.pallas import tpu as pltpu
from jax.sharding import PartitionSpec as P

PATCH = 16
NS_STEPS = 4
RADIUS = 32
FAR = RADIUS - PATCH // 2
NEAR = FAR - PATCH
MIDDLE = (PATCH - 1) / 2

NT = (((1,), (1,)), ((), ()))
NN = (((1,), (0,)), ((), ()))
f32 = jnp.float32
bf16 = jnp.bfloat16


def mm(a, b, dims=NN):
    return lax.dot_general(a, b, dims, preferred_element_type=f32)


def split(x):
    high = x.astype(bf16)
    return high, (x - high.astype(f32)).astype(bf16)


def fields_kernel(cols, table_ref, part_ref, field_ref, sum_ref):
    sum_ref[...] = jnp.sum(part_ref[...].astype(f32), axis=0)
    patches, slots = table_ref.shape[1:]
    patch_cols = cols // PATCH
    patch_rows = patches // patch_cols
    spot = table_ref[2].astype(jnp.int32)
    row_in = spot // PATCH
    col_in = spot % PATCH
    iota_row = lax.broadcasted_iota(jnp.int32, (PATCH, slots), 0)
    iota_col = lax.broadcasted_iota(jnp.int32, (cols, slots), 0)
    for a in range(patch_rows):
        total = jnp.zeros((4 * PATCH, cols), f32)
        for b in range(patch_cols):
            p = a * patch_cols + b
            prec = table_ref[0, p : p + 1, :]
            level = table_ref[1, p : p + 1, :]
            prec_high = prec.astype(bf16).astype(f32)
            level_high = level.astype(bf16).astype(f32)
            on_row = row_in[p : p + 1, :] == iota_row
            pieces = [
                jnp.where(on_row, piece, 0.0).astype(bf16)
                for piece in (prec_high, prec - prec_high, level_high, level - level_high)
            ]
            on_col = jnp.where(col_in[p : p + 1, :] + b * PATCH == iota_col, 1.0, 0.0).astype(bf16)
            total = total + mm(jnp.concatenate(pieces, 0), on_col, NT)
        rows = slice(a * PATCH, (a + 1) * PATCH)
        field_ref[0, rows, :] = total[:PATCH] + total[PATCH : 2 * PATCH]
        field_ref[1, rows, :] = total[2 * PATCH : 3 * PATCH] + total[3 * PATCH :]


def state_kernel(after_ref, hist_ref, lag_ref, mean_ref, flat_ref):
    members, tile_rows, cols = hist_ref.shape
    state = hist_ref[...].astype(f32)
    mean = jnp.sum(state, axis=0) / members
    mean_ref[...] = mean
    flat_ref[...] = (state - mean[None]).reshape(members * tile_rows, cols)
    for r in range(tile_rows):
        lag_ref[r] = flat_ref[pl.ds(r, members, stride=tile_rows), :].astype(bf16)


def half_of_lags():
    return lax.axis_index("lag") // (lax.axis_size("lag") // 2)


def ring(tiles, shares, turn):
    half = shares // 2
    pairs = []
    for t in range(tiles):
        for l in range(shares):
            target = t + (1 if (l // half) ^ turn else -1)
            if 0 <= target < tiles:
                pairs.append((t * shares + l, target * shares + l))
            else:
                pairs.append((t * shares + l, t * shares + (l + half) % shares))
    return pairs


def taper_plan(centre_row, inverse_square):
    q_row = lax.broadcasted_iota(jnp.int32, inverse_square.shape, 0)
    col = lax.broadcasted_iota(jnp.int32, inverse_square.shape, 1)
    col_square = jnp.square(col.astype(f32) - (q_row.astype(f32) * PATCH + MIDDLE))
    return centre_row, col_square, inverse_square


def accumulate(total, plan, anomalies, weight, innovation, first_row):
    centre_row, col_square, inverse_square = plan
    patches, cols = col_square.shape
    lefts = []
    for i, anomaly in enumerate(anomalies):
        members = anomaly.shape[0]
        offset = (first_row + i).astype(f32) - centre_row
        taper = jnp.square(jnp.maximum(0.0, 1.0 - (offset * offset + col_square) * inverse_square))
        scale = taper * weight[i : i + 1]
        blocks = anomaly.reshape(members // PATCH, PATCH, cols)
        left = [
            (blocks * jnp.broadcast_to(scale[q : q + 1], (PATCH, cols)).astype(bf16)[None]).reshape(members, cols)
            for q in range(patches)
        ]
        tail = taper * innovation[i : i + 1]
        left.append(jnp.concatenate([tail, jnp.zeros((PATCH - patches, cols), f32)], 0).astype(bf16))
        lefts.append(jnp.concatenate(left, 0))
    return total + mm(jnp.concatenate(lefts, 1), jnp.concatenate(anomalies, 1), NT)


STEP = 8


def paired(totals, members, patch_cols):
    pairs = patch_cols // 2
    grams, sides = [], []
    for total in totals:
        for pair in range(pairs):
            at = 2 * pair * members
            grams.append(jnp.concatenate([total[at : at + members], total[at + members : at + 2 * members]], 1))
        for pair in range(pairs):
            at = patch_cols * members + 2 * pair
            sides.append(jnp.concatenate([total[at : at + 1], total[at + 1 : at + 2]], 1))
    return jnp.concatenate(grams, 0), jnp.concatenate(sides, 0)


def message_of(grams, sides):
    return jnp.concatenate([grams.astype(bf16), *split(sides)], 0)


def read_message(ref, side_count):
    at = ref.shape[0] - 2 * side_count
    high, low = ref[at : at + side_count, :].astype(f32), ref[at + side_count :, :].astype(f32)
    return jnp.concatenate([ref[:at, :].astype(f32), high + low], 0)


def arrived(ref, turn, side_count):
    tile = lax.axis_index("dom")
    there = jnp.where(half_of_lags() ^ turn == 1, tile > 0, tile < lax.axis_size("dom") - 1)
    return jnp.where(there, read_message(ref, side_count), 0.0)


def outward(turn, rows_ref, held_ref, inverse_ref, message_ref, total_ref):
    tile_rows, members, cols = rows_ref.shape
    patch_cols = cols // PATCH
    down = half_of_lags() ^ turn
    near = pl.multiple_of(down * (tile_rows - NEAR), 8)
    middle = jnp.where(down == 0, MIDDLE - PATCH, MIDDLE + tile_rows)
    plans = [
        taper_plan(middle, inverse_ref[1 - down]),
        taper_plan(middle + jnp.where(down == 0, -PATCH, PATCH).astype(f32), inverse_ref[down]),
    ]
    anomalies = [rows_ref[near + i] for i in range(NEAR)]
    fields = [held_ref[k, pl.ds(near, NEAR), :] for k in range(2)]
    blank = jnp.zeros(total_ref.shape[1:], f32)
    totals = [accumulate(blank, plan, anomalies, *fields, near) for plan in plans]
    for start in range(NEAR, FAR, STEP):
        anomalies = [rows_ref[start + i] for i in range(STEP)]
        fields = [held_ref[k, start : start + STEP, :] for k in range(2)]
        totals[0] = accumulate(totals[0], plans[0], anomalies, *fields, jnp.int32(start))
    total_ref[1 - down] = totals[0]
    total_ref[down] = totals[1]
    message_ref[...] = message_of(*paired([total_ref[0], total_ref[1]], members, patch_cols))


def first_kernel(shares, *refs):
    parts, refs = refs[:shares], refs[shares:]
    sum_ref, field_ref, inverse_ref, rows_ref, held_ref, message_ref, flat_ref, total_ref = refs
    share_members, tile_rows, cols = parts[0].shape
    members = share_members * shares
    lag = lax.axis_index("lag")
    states = [part[...].astype(f32) for part in parts]
    mean = functools.reduce(jnp.add, [jnp.sum(state, axis=0) for state in states[1:]], sum_ref[...]) / members
    for k, state in enumerate(states):
        at = pl.multiple_of(lax.rem(lag + k, shares) * (share_members * tile_rows), 8)
        flat_ref[pl.ds(at, share_members * tile_rows), :] = (state - mean[None]).reshape(-1, cols)
    weight = field_ref[0]
    held_ref[0] = weight
    held_ref[1] = field_ref[1] - mean * weight
    for r in range(tile_rows):
        rows_ref[r] = flat_ref[pl.ds(r, members, stride=tile_rows), :].astype(bf16)
    outward(0, rows_ref, held_ref, inverse_ref, message_ref, total_ref)


def second_kernel(rows_ref, held_ref, inverse_ref, message_ref, total_ref):
    outward(1, rows_ref, held_ref, inverse_ref, message_ref, total_ref)


def own_kernel(after_ref, rows_ref, held_ref, inverse_ref, first_ref, out_ref):
    tile_rows, members, cols = rows_ref.shape
    patch_cols = cols // PATCH
    plans = [taper_plan(MIDDLE + a * PATCH, inverse_ref[a]) for a in range(tile_rows // PATCH)]
    totals = [jnp.zeros((patch_cols * members + PATCH, members), f32) for _ in plans]
    for start in range(0, tile_rows, STEP):
        anomalies = [rows_ref[start + i] for i in range(STEP)]
        fields = [held_ref[k, start : start + STEP, :] for k in range(2)]
        totals = [accumulate(total, plan, anomalies, *fields, jnp.int32(start)) for total, plan in zip(totals, plans)]
    sums = jnp.concatenate(paired(totals, members, patch_cols), 0)
    out_ref[...] = sums + arrived(first_ref, 0, patch_cols)


def finish_kernel(total_ref, second_ref, lag_ref, mean_ref, out_ref, flat_ref):
    tile_rows, members, cols = lag_ref.shape
    degree = members - 1.0
    pair_count = total_ref.shape[0] // members
    grams_end = pair_count * members
    row = lax.broadcasted_iota(jnp.int32, (members, cols), 0)
    lane = lax.broadcasted_iota(jnp.int32, (members, cols), 1)
    identity = jnp.where(row == lane % members, 1.0, 0.0)
    left_mask = jnp.where(lane < members, 1.0, 0.0).astype(bf16)
    right_mask = jnp.where(lane < members, 0.0, 1.0).astype(bf16)

    def right(y):
        halves = split(y)
        return jnp.concatenate(
            [jnp.concatenate([half * mask for half in halves], 1) for mask in (left_mask, right_mask)], 0
        )

    def product(lefts, factor):
        both = mm(jnp.concatenate([half for halves in lefts for half in halves], 0), factor)
        results, at = [], 0
        for high, low in lefts:
            rows = high.shape[0]
            upper, lower = both[at : at + rows], both[at + rows : at + 2 * rows]
            results.append(upper[:, :cols] + (upper[:, cols:] + lower[:, :cols]))
            at += 2 * rows
        return results

    total = total_ref[...] + arrived(second_ref, 1, pair_count)
    pairs = range(pair_count)
    grams = [total[p * members : (p + 1) * members] for p in pairs]
    squares = jnp.concatenate([jnp.sum(gram * gram, axis=0, keepdims=True) for gram in grams], 0)
    at_left = lax.broadcasted_iota(jnp.int32, squares.shape, 1) < members
    norm_left = jnp.sum(jnp.where(at_left, squares, 0.0), axis=1, keepdims=True)
    norm_right = jnp.sum(jnp.where(at_left, 0.0, squares), axis=1, keepdims=True)
    bounds = degree + jnp.sqrt(jnp.where(at_left, norm_left, norm_right))
    inverses = 1.0 / bounds
    spreads = jnp.sqrt(degree * inverses)
    sides = [jnp.broadcast_to(total[grams_end + p : grams_end + p + 1], (PATCH, cols)) for p in pairs]
    iterates = [(grams[p] + degree * identity) * inverses[p : p + 1] for p in pairs]
    roots = [None for _ in pairs]
    for step in range(NS_STEPS):
        last = step == NS_STEPS - 1
        iterate_halves = [split(iterates[p]) for p in pairs]
        if step == 0:
            ahead = iterates
        else:
            root_halves = [split(roots[p]) for p in pairs]
            factors = [right(iterates[p]) for p in pairs]
            ahead = [product([root_halves[p]], factors[p])[0] for p in pairs]
        corrections = [1.5 * identity - 0.5 * ahead[p] for p in pairs]
        factors = [right(corrections[p]) for p in pairs]
        lefts = [
            [split(sides[p])] + ([] if step == 0 else [root_halves[p]]) + ([] if last else [iterate_halves[p]]) for p in pairs
        ]
        results = [product(lefts[p], factors[p]) for p in pairs]
        sides = [results[p][0] for p in pairs]
        roots = corrections if step == 0 else [results[p][1] for p in pairs]
        iterates = [results[p][-1] for p in pairs]
    factors = [right(roots[p]) for p in pairs]
    weights = [product([split(sides[p])], factors[p])[0][:1] * inverses[p : p + 1] for p in pairs]
    mixings = [(spreads[p : p + 1] * roots[p] + weights[p]).astype(bf16) for p in pairs]

    patch = lax.broadcasted_iota(jnp.int32, (members, cols), 1) // PATCH
    masks = [jnp.where(patch % 4 == k, 1.0, 0.0).astype(bf16) for k in range(4)]
    quads = cols // (4 * PATCH)
    for a in range(tile_rows // PATCH):
        mixing = jnp.concatenate(
            [jnp.concatenate(mixings[2 * q : 2 * q + 2], 1) for q in range(a * quads, (a + 1) * quads)], 0
        )
        for r in range(a * PATCH, (a + 1) * PATCH, 2):
            state = jnp.concatenate(
                [jnp.concatenate([lag_ref[i] * mask for mask in masks], 0) for i in (r, r + 1)], 1
            )
            spread_out = mm(mixing, state)
            for i in (0, 1):
                part = spread_out[:, i * cols : (i + 1) * cols]
                chosen = part[:members]
                for q in range(1, quads):
                    chosen = jnp.where(patch // 4 == q, part[q * members : (q + 1) * members], chosen)
                flat_ref[pl.ds(r + i, members, stride=tile_rows), :] = chosen + mean_ref[r + i : r + i + 1, :]
    out_ref[...] = flat_ref[...].reshape(1, members, tile_rows, cols).astype(bf16)


def shards(history, forecast, spot, alive, levels, precision, radius):
    shares = lax.axis_size("lag")
    tiles = lax.axis_size("dom")
    share_members, tile_rows, cols = forecast.shape
    members = share_members * shares
    patch_cols = cols // PATCH
    def call(kernel, name, in_specs, out_shape, scratch=()):
        return pl.pallas_call(
            kernel,
            in_specs=in_specs,
            out_specs=jax.tree.map(lambda _: vmem, out_shape),
            out_shape=out_shape,
            scratch_shapes=scratch,
            compiler_params=pltpu.CompilerParams(vmem_limit_bytes=32 * 2**20),
            name=name,
        )

    shape = jax.ShapeDtypeStruct
    vmem = pl.BlockSpec(memory_space=pltpu.VMEM)
    parts = [forecast]
    for k in range(1, shares):
        parts.append(lax.ppermute(forecast, "lag", [((i + k) % shares, i) for i in range(shares)]))
    live = lax.broadcasted_iota(jnp.int32, spot.shape, 1) < alive[:, None]
    weights = jnp.where(live, precision, 0.0)
    kind = lax.broadcasted_iota(jnp.int32, (3, *spot.shape), 0)
    tables = jnp.where(kind == 0, weights[None], jnp.where(kind == 1, (weights * levels)[None], spot.astype(f32)[None]))
    inverse = jnp.broadcast_to(
        (1.0 / jnp.square(radius.astype(f32))).reshape(-1, patch_cols, 1), (tile_rows // PATCH, patch_cols, cols)
    )
    sent, tables = lax.optimization_barrier((inverse, tables))
    rings = [ring(tiles, shares, turn) for turn in range(2)]
    axes = ("dom", "lag")
    next_inverses = [lax.ppermute(sent, axes, [(t, s) for s, t in pairs]) for pairs in rings]
    fields, own_sum = call(
        functools.partial(fields_kernel, cols),
        "fields",
        [vmem, vmem],
        [shape((2, tile_rows, cols), f32), shape((tile_rows, cols), f32)],
    )(tables, forecast)
    pair_rows = patch_cols * members
    message_shape = shape((pair_rows + 2 * patch_cols, 2 * members), bf16)
    total_scratch = pltpu.VMEM((2, patch_cols * members + PATCH, members), f32)
    rows, held, message = call(
        functools.partial(first_kernel, shares),
        "first_gram",
        [vmem] * (shares + 3),
        [shape((tile_rows, members, cols), bf16), shape((2, tile_rows, cols), f32), message_shape],
        [pltpu.VMEM((members * tile_rows, cols), f32), total_scratch],
    )(*parts, own_sum, fields, next_inverses[0])
    first = lax.ppermute(message, axes, rings[0])
    message = call(second_kernel, "second_gram", [vmem] * 3, message_shape, [total_scratch])(rows, held, next_inverses[1])
    second = lax.ppermute(message, axes, rings[1])
    lag_rows, lag_mean = call(
        state_kernel,
        "state",
        [vmem, vmem],
        [shape((tile_rows, members, cols), bf16), shape((tile_rows, cols), f32)],
        [pltpu.VMEM((members * tile_rows, cols), f32)],
    )(held, history[0])
    own_shape = shape((pair_rows + patch_cols, 2 * members), f32)
    own = call(own_kernel, "own_gram", [vmem] * 5, own_shape)(lag_mean, rows, held, inverse, first)
    return call(
        finish_kernel,
        "finish",
        [vmem] * 4,
        shape((1, members, tile_rows, cols), bf16),
        [pltpu.VMEM((members * tile_rows, cols), f32)],
    )(own, second, lag_rows, lag_mean)


def solution(mesh):
    in_specs = (
        P("lag", None, "dom", None),
        P("lag", "dom", None),
        P("dom", None),
        P("dom"),
        P("dom", None),
        P("dom", None),
        P("dom"),
    )
    out_specs = P("lag", None, "dom", None)
    return jax.shard_map(shards, mesh=mesh, in_specs=in_specs, out_specs=out_specs, check_vma=False)
```

```python
import functools

import jax
import jax.numpy as jnp
from jax import lax
from jax.experimental import pallas as pl
from jax.experimental.pallas import tpu as pltpu
from jax.sharding import PartitionSpec as P

PATCH = 16
NS_STEPS = 4
RADIUS = 32
FAR = RADIUS - PATCH // 2
NEAR = FAR - PATCH
MIDDLE = (PATCH - 1) / 2

NT = (((1,), (1,)), ((), ()))
NN = (((1,), (0,)), ((), ()))
f32 = jnp.float32
bf16 = jnp.bfloat16


def mm(a, b, dims=NN):
    return lax.dot_general(a, b, dims, preferred_element_type=f32)


def split(x):
    high = x.astype(bf16)
    return high, (x - high.astype(f32)).astype(bf16)


def fields_kernel(cols, table_ref, part_ref, field_ref, sum_ref):
    sum_ref[...] = jnp.sum(part_ref[...].astype(f32), axis=0)
    patches, slots = table_ref.shape[1:]
    patch_cols = cols // PATCH
    patch_rows = patches // patch_cols
    spot = table_ref[2].astype(jnp.int32)
    row_in = spot // PATCH
    col_in = spot % PATCH
    iota_row = lax.broadcasted_iota(jnp.int32, (PATCH, slots), 0)
    iota_col = lax.broadcasted_iota(jnp.int32, (cols, slots), 0)
    for a in range(patch_rows):
        total = jnp.zeros((4 * PATCH, cols), f32)
        for b in range(patch_cols):
            p = a * patch_cols + b
            prec = table_ref[0, p : p + 1, :]
            level = table_ref[1, p : p + 1, :]
            prec_high = prec.astype(bf16).astype(f32)
            level_high = level.astype(bf16).astype(f32)
            on_row = row_in[p : p + 1, :] == iota_row
            pieces = [
                jnp.where(on_row, piece, 0.0).astype(bf16)
                for piece in (prec_high, prec - prec_high, level_high, level - level_high)
            ]
            on_col = jnp.where(col_in[p : p + 1, :] + b * PATCH == iota_col, 1.0, 0.0).astype(bf16)
            total = total + mm(jnp.concatenate(pieces, 0), on_col, NT)
        rows = slice(a * PATCH, (a + 1) * PATCH)
        field_ref[0, rows, :] = total[:PATCH] + total[PATCH : 2 * PATCH]
        field_ref[1, rows, :] = total[2 * PATCH : 3 * PATCH] + total[3 * PATCH :]


def state_kernel(after_ref, hist_ref, lag_ref, mean_ref, flat_ref):
    members, tile_rows, cols = hist_ref.shape
    state = hist_ref[...].astype(f32)
    mean = jnp.sum(state, axis=0) / members
    mean_ref[...] = mean
    flat_ref[...] = (state - mean[None]).reshape(members * tile_rows, cols)
    for r in range(tile_rows):
        lag_ref[r] = flat_ref[pl.ds(r, members, stride=tile_rows), :].astype(bf16)


def half_of_lags():
    return lax.axis_index("lag") // (lax.axis_size("lag") // 2)


def ring(tiles, shares, turn):
    half = shares // 2
    pairs = []
    for t in range(tiles):
        for l in range(shares):
            target = t + (1 if (l // half) ^ turn else -1)
            if 0 <= target < tiles:
                pairs.append((t * shares + l, target * shares + l))
            else:
                pairs.append((t * shares + l, t * shares + (l + half) % shares))
    return pairs


def taper_plan(centre_row, inverse_square):
    q_row = lax.broadcasted_iota(jnp.int32, inverse_square.shape, 0)
    col = lax.broadcasted_iota(jnp.int32, inverse_square.shape, 1)
    col_square = jnp.square(col.astype(f32) - (q_row.astype(f32) * PATCH + MIDDLE))
    return centre_row, col_square, inverse_square


def accumulate(total, plan, anomalies, weight, innovation, first_row):
    centre_row, col_square, inverse_square = plan
    patches, cols = col_square.shape
    lefts = []
    for i, anomaly in enumerate(anomalies):
        members = anomaly.shape[0]
        offset = (first_row + i).astype(f32) - centre_row
        taper = jnp.square(jnp.maximum(0.0, 1.0 - (offset * offset + col_square) * inverse_square))
        scale = taper * weight[i : i + 1]
        blocks = anomaly.reshape(members // PATCH, PATCH, cols)
        left = [
            (blocks * jnp.broadcast_to(scale[q : q + 1], (PATCH, cols)).astype(bf16)[None]).reshape(members, cols)
            for q in range(patches)
        ]
        tail = taper * innovation[i : i + 1]
        left.append(jnp.concatenate([tail, jnp.zeros((PATCH - patches, cols), f32)], 0).astype(bf16))
        lefts.append(jnp.concatenate(left, 0))
    return total + mm(jnp.concatenate(lefts, 1), jnp.concatenate(anomalies, 1), NT)


STEP = 4


def paired(totals, members, patch_cols):
    pairs = patch_cols // 2
    grams, sides = [], []
    for total in totals:
        for pair in range(pairs):
            at = 2 * pair * members
            grams.append(jnp.concatenate([total[at : at + members], total[at + members : at + 2 * members]], 1))
        for pair in range(pairs):
            at = patch_cols * members + 2 * pair
            sides.append(jnp.concatenate([total[at : at + 1], total[at + 1 : at + 2]], 1))
    return jnp.concatenate(grams, 0), jnp.concatenate(sides, 0)


def message_of(grams, sides):
    return jnp.concatenate([grams.astype(bf16), *split(sides)], 0)


def read_message(ref, side_count):
    at = ref.shape[0] - 2 * side_count
    high, low = ref[at : at + side_count, :].astype(f32), ref[at + side_count :, :].astype(f32)
    return jnp.concatenate([ref[:at, :].astype(f32), high + low], 0)


def arrived(ref, turn, side_count):
    tile = lax.axis_index("dom")
    there = jnp.where(half_of_lags() ^ turn == 1, tile > 0, tile < lax.axis_size("dom") - 1)
    return jnp.where(there, read_message(ref, side_count), 0.0)


def outward(turn, rows_ref, held_ref, inverse_ref, message_ref, total_ref):
    tile_rows, members, cols = rows_ref.shape
    patch_cols = cols // PATCH
    down = half_of_lags() ^ turn
    near = pl.multiple_of(down * (tile_rows - NEAR), 8)
    middle = jnp.where(down == 0, MIDDLE - PATCH, MIDDLE + tile_rows)
    plans = [
        taper_plan(middle, inverse_ref[1 - down]),
        taper_plan(middle + jnp.where(down == 0, -PATCH, PATCH).astype(f32), inverse_ref[down]),
    ]
    totals = [jnp.zeros(total_ref.shape[1:], f32) for _ in plans]
    near_fields = [held_ref[k, pl.ds(near, NEAR), :] for k in range(2)]
    for start in range(0, NEAR, STEP):
        anomalies = [rows_ref[near + start + i] for i in range(STEP)]
        fields = [field[start : start + STEP] for field in near_fields]
        totals = [accumulate(total, plan, anomalies, *fields, near + start) for total, plan in zip(totals, plans)]
    for start in range(NEAR, FAR, STEP):
        anomalies = [rows_ref[start + i] for i in range(STEP)]
        fields = [held_ref[k, start : start + STEP, :] for k in range(2)]
        totals[0] = accumulate(totals[0], plans[0], anomalies, *fields, jnp.int32(start))
    total_ref[1 - down] = totals[0]
    total_ref[down] = totals[1]
    message_ref[...] = message_of(*paired([total_ref[0], total_ref[1]], members, patch_cols))


def first_kernel(shares, *refs):
    parts, refs = refs[:shares], refs[shares:]
    sum_ref, field_ref, inverse_ref, rows_ref, held_ref, message_ref, flat_ref, total_ref = refs
    share_members, tile_rows, cols = parts[0].shape
    members = share_members * shares
    lag = lax.axis_index("lag")
    states = [part[...].astype(f32) for part in parts]
    mean = functools.reduce(jnp.add, [jnp.sum(state, axis=0) for state in states[1:]], sum_ref[...]) / members
    for k, state in enumerate(states):
        at = pl.multiple_of(lax.rem(lag + k, shares) * (share_members * tile_rows), 8)
        flat_ref[pl.ds(at, share_members * tile_rows), :] = (state - mean[None]).reshape(-1, cols)
    weight = field_ref[0]
    held_ref[0] = weight
    held_ref[1] = field_ref[1] - mean * weight
    for r in range(tile_rows):
        rows_ref[r] = flat_ref[pl.ds(r, members, stride=tile_rows), :].astype(bf16)
    outward(0, rows_ref, held_ref, inverse_ref, message_ref, total_ref)


def second_kernel(rows_ref, held_ref, inverse_ref, message_ref, total_ref):
    outward(1, rows_ref, held_ref, inverse_ref, message_ref, total_ref)


def own_kernel(after_ref, rows_ref, held_ref, inverse_ref, first_ref, out_ref):
    tile_rows, members, cols = rows_ref.shape
    patch_cols = cols // PATCH
    plans = [taper_plan(MIDDLE + a * PATCH, inverse_ref[a]) for a in range(tile_rows // PATCH)]
    totals = [jnp.zeros((patch_cols * members + PATCH, members), f32) for _ in plans]
    for start in range(0, tile_rows, STEP):
        anomalies = [rows_ref[start + i] for i in range(STEP)]
        fields = [held_ref[k, start : start + STEP, :] for k in range(2)]
        totals = [accumulate(total, plan, anomalies, *fields, jnp.int32(start)) for total, plan in zip(totals, plans)]
    sums = jnp.concatenate(paired(totals, members, patch_cols), 0)
    out_ref[...] = sums + arrived(first_ref, 0, patch_cols)


def finish_kernel(total_ref, second_ref, lag_ref, mean_ref, out_ref, flat_ref):
    tile_rows, members, cols = lag_ref.shape
    degree = members - 1.0
    pair_count = total_ref.shape[0] // members
    grams_end = pair_count * members
    row = lax.broadcasted_iota(jnp.int32, (members, cols), 0)
    lane = lax.broadcasted_iota(jnp.int32, (members, cols), 1)
    identity = jnp.where(row == lane % members, 1.0, 0.0)
    left_mask = jnp.where(lane < members, 1.0, 0.0).astype(bf16)
    right_mask = jnp.where(lane < members, 0.0, 1.0).astype(bf16)

    def splits(parts):
        highs = [part.astype(bf16) for part in parts]
        rests = [part - high.astype(f32) for part, high in zip(parts, highs)]
        return list(zip(highs, [rest.astype(bf16) for rest in rests]))

    def rights(parts):
        return [
            jnp.concatenate(
                [jnp.concatenate([half * mask for half in halves], 1) for mask in (left_mask, right_mask)], 0
            )
            for halves in splits(parts)
        ]

    def products(lefts, factors):
        stacks = [jnp.concatenate([half for halves in left for half in halves], 0) for left in lefts]
        boths = [mm(stack, factor) for stack, factor in zip(stacks, factors)]
        results = []
        for left, both in zip(lefts, boths):
            parts, at = [], 0
            for high, low in left:
                rows = high.shape[0]
                upper, lower = both[at : at + rows], both[at + rows : at + 2 * rows]
                parts.append(upper[:, :cols] + (upper[:, cols:] + lower[:, :cols]))
                at += 2 * rows
            results.append(parts)
        return results

    total = total_ref[...] + arrived(second_ref, 1, pair_count)
    pairs = range(pair_count)
    grams = [total[p * members : (p + 1) * members] for p in pairs]
    squares = jnp.concatenate([jnp.sum(gram * gram, axis=0, keepdims=True) for gram in grams], 0)
    at_left = lax.broadcasted_iota(jnp.int32, squares.shape, 1) < members
    norm_left = jnp.sum(jnp.where(at_left, squares, 0.0), axis=1, keepdims=True)
    norm_right = jnp.sum(jnp.where(at_left, 0.0, squares), axis=1, keepdims=True)
    bounds = degree + jnp.sqrt(jnp.where(at_left, norm_left, norm_right))
    inverses = 1.0 / bounds
    spreads = jnp.sqrt(degree * inverses)
    sides = [jnp.broadcast_to(total[grams_end + p : grams_end + p + 1], (PATCH, cols)) for p in pairs]
    iterates = [(grams[p] + degree * identity) * inverses[p : p + 1] for p in pairs]
    roots = [None for _ in pairs]
    for step in range(NS_STEPS):
        lefts = [[halves] for halves in splits(sides)]
        if step == 0:
            ahead = iterates
        else:
            root_halves = splits(roots)
            lefts = [left + [halves] for left, halves in zip(lefts, root_halves)]
            ahead = [parts[0] for parts in products([[halves] for halves in root_halves], rights(iterates))]
        if step < NS_STEPS - 1:
            lefts = [left + [halves] for left, halves in zip(lefts, splits(iterates))]
        corrections = [1.5 * identity - 0.5 * product for product in ahead]
        results = products(lefts, rights(corrections))
        sides = [parts[0] for parts in results]
        roots = corrections if step == 0 else [parts[1] for parts in results]
        iterates = [parts[-1] for parts in results]
    weights = [parts[0][:1] for parts in products([[halves] for halves in splits(sides)], rights(roots))]
    weights = [weights[p] * inverses[p : p + 1] for p in pairs]
    mixings = [(spreads[p : p + 1] * roots[p] + weights[p]).astype(bf16) for p in pairs]

    patch = lax.broadcasted_iota(jnp.int32, (members, cols), 1) // PATCH
    masks = [jnp.where(patch % 4 == k, 1.0, 0.0).astype(bf16) for k in range(4)]
    quads = cols // (4 * PATCH)
    for a in range(tile_rows // PATCH):
        mixing = jnp.concatenate(
            [jnp.concatenate(mixings[2 * q : 2 * q + 2], 1) for q in range(a * quads, (a + 1) * quads)], 0
        )
        for r in range(a * PATCH, (a + 1) * PATCH, 2):
            state = jnp.concatenate(
                [jnp.concatenate([lag_ref[i] * mask for mask in masks], 0) for i in (r, r + 1)], 1
            )
            spread_out = mm(mixing, state)
            for i in (0, 1):
                part = spread_out[:, i * cols : (i + 1) * cols]
                chosen = part[:members]
                for q in range(1, quads):
                    chosen = jnp.where(patch // 4 == q, part[q * members : (q + 1) * members], chosen)
                flat_ref[pl.ds(r + i, members, stride=tile_rows), :] = chosen + mean_ref[r + i : r + i + 1, :]
    out_ref[...] = flat_ref[...].reshape(1, members, tile_rows, cols).astype(bf16)


def shards(history, forecast, spot, alive, levels, precision, radius):
    shares = lax.axis_size("lag")
    tiles = lax.axis_size("dom")
    share_members, tile_rows, cols = forecast.shape
    members = share_members * shares
    patch_cols = cols // PATCH
    def call(kernel, name, in_specs, out_shape, scratch=()):
        return pl.pallas_call(
            kernel,
            in_specs=in_specs,
            out_specs=jax.tree.map(lambda _: vmem, out_shape),
            out_shape=out_shape,
            scratch_shapes=scratch,
            compiler_params=pltpu.CompilerParams(vmem_limit_bytes=32 * 2**20),
            name=name,
        )

    shape = jax.ShapeDtypeStruct
    vmem = pl.BlockSpec(memory_space=pltpu.VMEM)
    parts = [forecast]
    for k in range(1, shares):
        parts.append(lax.ppermute(forecast, "lag", [((i + k) % shares, i) for i in range(shares)]))
    live = lax.broadcasted_iota(jnp.int32, spot.shape, 1) < alive[:, None]
    weights = jnp.where(live, precision, 0.0)
    kind = lax.broadcasted_iota(jnp.int32, (3, *spot.shape), 0)
    tables = jnp.where(kind == 0, weights[None], jnp.where(kind == 1, (weights * levels)[None], spot.astype(f32)[None]))
    inverse = jnp.broadcast_to(
        (1.0 / jnp.square(radius.astype(f32))).reshape(-1, patch_cols, 1), (tile_rows // PATCH, patch_cols, cols)
    )
    sent, tables = lax.optimization_barrier((inverse, tables))
    rings = [ring(tiles, shares, turn) for turn in range(2)]
    axes = ("dom", "lag")
    next_inverses = [lax.ppermute(sent, axes, [(t, s) for s, t in pairs]) for pairs in rings]
    fields, own_sum = call(
        functools.partial(fields_kernel, cols),
        "fields",
        [vmem, vmem],
        [shape((2, tile_rows, cols), f32), shape((tile_rows, cols), f32)],
    )(tables, forecast)
    pair_rows = patch_cols * members
    message_shape = shape((pair_rows + 2 * patch_cols, 2 * members), bf16)
    total_scratch = pltpu.VMEM((2, patch_cols * members + PATCH, members), f32)
    rows, held, message = call(
        functools.partial(first_kernel, shares),
        "first_gram",
        [vmem] * (shares + 3),
        [shape((tile_rows, members, cols), bf16), shape((2, tile_rows, cols), f32), message_shape],
        [pltpu.VMEM((members * tile_rows, cols), f32), total_scratch],
    )(*parts, own_sum, fields, next_inverses[0])
    first = lax.ppermute(message, axes, rings[0])
    message = call(second_kernel, "second_gram", [vmem] * 3, message_shape, [total_scratch])(rows, held, next_inverses[1])
    second = lax.ppermute(message, axes, rings[1])
    lag_rows, lag_mean = call(
        state_kernel,
        "state",
        [vmem, vmem],
        [shape((tile_rows, members, cols), bf16), shape((tile_rows, cols), f32)],
        [pltpu.VMEM((members * tile_rows, cols), f32)],
    )(held, history[0])
    own_shape = shape((pair_rows + patch_cols, 2 * members), f32)
    own = call(own_kernel, "own_gram", [vmem] * 5, own_shape)(lag_mean, rows, held, inverse, first)
    return call(
        finish_kernel,
        "finish",
        [vmem] * 4,
        shape((1, members, tile_rows, cols), bf16),
        [pltpu.VMEM((members * tile_rows, cols), f32)],
    )(own, second, lag_rows, lag_mean)


def solution(mesh):
    in_specs = (
        P("lag", None, "dom", None),
        P("lag", "dom", None),
        P("dom", None),
        P("dom"),
        P("dom", None),
        P("dom", None),
        P("dom"),
    )
    out_specs = P("lag", None, "dom", None)
    return jax.shard_map(shards, mesh=mesh, in_specs=in_specs, out_specs=out_specs, check_vma=False)
```

```python
import functools

import jax
import jax.numpy as jnp
from jax import lax
from jax.experimental import pallas as pl
from jax.experimental.pallas import tpu as pltpu
from jax.sharding import PartitionSpec as P

PATCH = 16
NS_STEPS = 4
RADIUS = 32
FAR = RADIUS - PATCH // 2
NEAR = FAR - PATCH
MIDDLE = (PATCH - 1) / 2

NT = (((1,), (1,)), ((), ()))
NN = (((1,), (0,)), ((), ()))
f32 = jnp.float32
bf16 = jnp.bfloat16


def mm(a, b, dims=NN):
    return lax.dot_general(a, b, dims, preferred_element_type=f32)


def split(x):
    high = x.astype(bf16)
    return high, (x - high.astype(f32)).astype(bf16)


def fields_kernel(cols, table_ref, part_ref, field_ref, sum_ref):
    sum_ref[...] = jnp.sum(part_ref[...].astype(f32), axis=0)
    patches, slots = table_ref.shape[1:]
    patch_cols = cols // PATCH
    patch_rows = patches // patch_cols
    spot = table_ref[2].astype(jnp.int32)
    row_in = spot // PATCH
    col_in = spot % PATCH
    iota_row = lax.broadcasted_iota(jnp.int32, (PATCH, slots), 0)
    iota_col = lax.broadcasted_iota(jnp.int32, (cols, slots), 0)
    for a in range(patch_rows):
        total = jnp.zeros((4 * PATCH, cols), f32)
        for b in range(patch_cols):
            p = a * patch_cols + b
            prec = table_ref[0, p : p + 1, :]
            level = table_ref[1, p : p + 1, :]
            prec_high = prec.astype(bf16).astype(f32)
            level_high = level.astype(bf16).astype(f32)
            on_row = row_in[p : p + 1, :] == iota_row
            pieces = [
                jnp.where(on_row, piece, 0.0).astype(bf16)
                for piece in (prec_high, prec - prec_high, level_high, level - level_high)
            ]
            on_col = jnp.where(col_in[p : p + 1, :] + b * PATCH == iota_col, 1.0, 0.0).astype(bf16)
            total = total + mm(jnp.concatenate(pieces, 0), on_col, NT)
        rows = slice(a * PATCH, (a + 1) * PATCH)
        field_ref[0, rows, :] = total[:PATCH] + total[PATCH : 2 * PATCH]
        field_ref[1, rows, :] = total[2 * PATCH : 3 * PATCH] + total[3 * PATCH :]


def state_kernel(after_ref, hist_ref, lag_ref, mean_ref, flat_ref):
    members, tile_rows, cols = hist_ref.shape
    state = hist_ref[...].astype(f32)
    mean = jnp.sum(state, axis=0) / members
    mean_ref[...] = mean
    flat_ref[...] = (state - mean[None]).reshape(members * tile_rows, cols)
    for r in range(tile_rows):
        lag_ref[r] = flat_ref[pl.ds(r, members, stride=tile_rows), :].astype(bf16)


def half_of_lags():
    return lax.axis_index("lag") // (lax.axis_size("lag") // 2)


def ring(tiles, shares, turn):
    half = shares // 2
    pairs = []
    for t in range(tiles):
        for l in range(shares):
            target = t + (1 if (l // half) ^ turn else -1)
            if 0 <= target < tiles:
                pairs.append((t * shares + l, target * shares + l))
            else:
                pairs.append((t * shares + l, t * shares + (l + half) % shares))
    return pairs


def taper_plan(centre_row, inverse_square):
    q_row = lax.broadcasted_iota(jnp.int32, inverse_square.shape, 0)
    col = lax.broadcasted_iota(jnp.int32, inverse_square.shape, 1)
    col_square = jnp.square(col.astype(f32) - (q_row.astype(f32) * PATCH + MIDDLE))
    return centre_row, col_square, inverse_square


def accumulate(total, plan, anomalies, weight, innovation, first_row):
    centre_row, col_square, inverse_square = plan
    patches, cols = col_square.shape
    lefts = []
    for i, anomaly in enumerate(anomalies):
        members = anomaly.shape[0]
        offset = (first_row + i).astype(f32) - centre_row
        taper = jnp.square(jnp.maximum(0.0, 1.0 - (offset * offset + col_square) * inverse_square))
        scale = taper * weight[i : i + 1]
        blocks = anomaly.reshape(members // PATCH, PATCH, cols)
        left = [
            (blocks * jnp.broadcast_to(scale[q : q + 1], (PATCH, cols)).astype(bf16)[None]).reshape(members, cols)
            for q in range(patches)
        ]
        tail = taper * innovation[i : i + 1]
        left.append(jnp.concatenate([tail, jnp.zeros((PATCH - patches, cols), f32)], 0).astype(bf16))
        lefts.append(jnp.concatenate(left, 0))
    return total + mm(jnp.concatenate(lefts, 1), jnp.concatenate(anomalies, 1), NT)


STEP = 8


def paired(totals, members, patch_cols):
    pairs = patch_cols // 2
    grams, sides = [], []
    for total in totals:
        for pair in range(pairs):
            at = 2 * pair * members
            grams.append(jnp.concatenate([total[at : at + members], total[at + members : at + 2 * members]], 1))
        for pair in range(pairs):
            at = patch_cols * members + 2 * pair
            sides.append(jnp.concatenate([total[at : at + 1], total[at + 1 : at + 2]], 1))
    return jnp.concatenate(grams, 0), jnp.concatenate(sides, 0)


def message_of(grams, sides):
    return jnp.concatenate([grams.astype(bf16), *split(sides)], 0)


def read_message(ref, side_count):
    at = ref.shape[0] - 2 * side_count
    high, low = ref[at : at + side_count, :].astype(f32), ref[at + side_count :, :].astype(f32)
    return jnp.concatenate([ref[:at, :].astype(f32), high + low], 0)


def arrived(ref, turn, side_count):
    tile = lax.axis_index("dom")
    there = jnp.where(half_of_lags() ^ turn == 1, tile > 0, tile < lax.axis_size("dom") - 1)
    return jnp.where(there, read_message(ref, side_count), 0.0)


def outward(down, near_rows, near_fields, far_rows, far_fields, tile_rows, inverse_ref, message_ref, total_ref):
    members, cols = near_rows[0].shape
    patch_cols = cols // PATCH
    middle = jnp.where(down == 0, MIDDLE - PATCH, MIDDLE + tile_rows)
    plans = [
        taper_plan(middle, inverse_ref[1 - down]),
        taper_plan(middle + jnp.where(down == 0, -PATCH, PATCH).astype(f32), inverse_ref[down]),
    ]
    blank = jnp.zeros(total_ref.shape[1:], f32)
    near = down * (tile_rows - NEAR)
    totals = [accumulate(blank, plan, near_rows, *near_fields, near) for plan in plans]
    for start in range(0, FAR - NEAR, STEP):
        rows = slice(start, start + STEP)
        totals[0] = accumulate(
            totals[0], plans[0], far_rows[rows], *[field[rows] for field in far_fields], jnp.int32(NEAR + start)
        )
    total_ref[1 - down] = totals[0]
    total_ref[down] = totals[1]
    message_ref[...] = message_of(*paired([total_ref[0], total_ref[1]], members, patch_cols))


def centre(first, parts, sum_ref, field_ref, held_ref, rows_ref, flat_ref):
    count, members, cols = rows_ref.shape
    tile_rows = parts[0].shape[1]
    shares = len(parts)
    share_members = members // shares
    lag = lax.axis_index("lag")
    late = tile_rows - count
    whole = parts[0][...].astype(f32)
    states = [jnp.where(first == 0, whole[:, :count], whole[:, late:])] + [part[...].astype(f32) for part in parts[1:]]
    run = pl.ds(pl.multiple_of(first, 8), count)
    mean = functools.reduce(jnp.add, [jnp.sum(state, axis=0) for state in states[1:]], sum_ref[run, :]) / members
    for k, state in enumerate(states):
        at = pl.multiple_of(lax.rem(lag + k, shares) * (share_members * count), 8)
        flat_ref[pl.ds(at, share_members * count), :] = (state - mean[None]).reshape(-1, cols)
    weight = field_ref[0, run, :]
    held_ref[0] = weight
    held_ref[1] = field_ref[1, run, :] - mean * weight
    for r in range(count):
        rows_ref[r] = flat_ref[pl.ds(r, members, stride=count), :].astype(bf16)


def far_run(down, rows_ref, held_ref):
    at = pl.multiple_of((1 - down) * NEAR, 8)
    rows = [rows_ref[at + i] for i in range(FAR - NEAR)]
    return rows, [held_ref[k, pl.ds(at, FAR - NEAR), :] for k in range(2)]


def first_kernel(shares, *refs):
    parts, refs = refs[:shares], refs[shares:]
    sum_ref, field_ref, inverse_ref, rows_ref, held_ref, message_ref, flat_ref, total_ref = refs
    down = half_of_lags()
    tile_rows = parts[0].shape[1]
    centre(down * (tile_rows - FAR), parts, sum_ref, field_ref, held_ref, rows_ref, flat_ref)
    at = pl.multiple_of(down * (FAR - NEAR), 8)
    near_rows = [rows_ref[at + i] for i in range(NEAR)]
    near_fields = [held_ref[k, pl.ds(at, NEAR), :] for k in range(2)]
    outward(
        down, near_rows, near_fields, *far_run(down, rows_ref, held_ref), tile_rows, inverse_ref, message_ref, total_ref
    )


def second_kernel(shares, *refs):
    parts, refs = refs[:shares], refs[shares:]
    sum_ref, field_ref, most_ref, most_held_ref, inverse_ref, rows_ref, held_ref, message_ref, flat_ref, total_ref = refs
    down = half_of_lags()
    tile_rows = parts[0].shape[1]
    centre((1 - down) * (tile_rows - NEAR), parts, sum_ref, field_ref, held_ref, rows_ref, flat_ref)
    near_rows = [rows_ref[i] for i in range(NEAR)]
    near_fields = [held_ref[k] for k in range(2)]
    outward(
        1 - down, near_rows, near_fields, *far_run(down, most_ref, most_held_ref), tile_rows, inverse_ref, message_ref, total_ref
    )


def own_kernel(after_ref, most_ref, most_held_ref, rest_ref, rest_held_ref, inverse_ref, first_ref, out_ref):
    members, cols = most_ref.shape[1:]
    patch_rows, patch_cols = inverse_ref.shape[:2]
    down = half_of_lags()
    plans = [taper_plan(MIDDLE + a * PATCH, inverse_ref[a]) for a in range(patch_rows)]
    totals = [jnp.zeros((patch_cols * members + PATCH, members), f32) for _ in plans]
    tile_rows = patch_rows * PATCH
    for first, rows_ref, held_ref in (
        (down * (tile_rows - FAR), most_ref, most_held_ref),
        ((1 - down) * (tile_rows - NEAR), rest_ref, rest_held_ref),
    ):
        for start in range(0, rows_ref.shape[0], STEP):
            anomalies = [rows_ref[start + i] for i in range(STEP)]
            fields = [held_ref[k, start : start + STEP, :] for k in range(2)]
            totals = [accumulate(total, plan, anomalies, *fields, first + start) for total, plan in zip(totals, plans)]
    sums = jnp.concatenate(paired(totals, members, patch_cols), 0)
    out_ref[...] = sums + arrived(first_ref, 0, patch_cols)


def finish_kernel(total_ref, second_ref, lag_ref, mean_ref, out_ref, flat_ref):
    tile_rows, members, cols = lag_ref.shape
    degree = members - 1.0
    pair_count = total_ref.shape[0] // members
    grams_end = pair_count * members
    row = lax.broadcasted_iota(jnp.int32, (members, cols), 0)
    lane = lax.broadcasted_iota(jnp.int32, (members, cols), 1)
    identity = jnp.where(row == lane % members, 1.0, 0.0)
    left_mask = jnp.where(lane < members, 1.0, 0.0).astype(bf16)
    right_mask = jnp.where(lane < members, 0.0, 1.0).astype(bf16)

    def splits(parts):
        highs = [part.astype(bf16) for part in parts]
        rests = [part - high.astype(f32) for part, high in zip(parts, highs)]
        return list(zip(highs, [rest.astype(bf16) for rest in rests]))

    def rights(parts):
        return [
            jnp.concatenate(
                [jnp.concatenate([half * mask for half in halves], 1) for mask in (left_mask, right_mask)], 0
            )
            for halves in splits(parts)
        ]

    def products(lefts, factors):
        stacks = [jnp.concatenate([half for halves in left for half in halves], 0) for left in lefts]
        boths = [mm(stack, factor) for stack, factor in zip(stacks, factors)]
        results = []
        for left, both in zip(lefts, boths):
            parts, at = [], 0
            for high, low in left:
                rows = high.shape[0]
                upper, lower = both[at : at + rows], both[at + rows : at + 2 * rows]
                parts.append(upper[:, :cols] + (upper[:, cols:] + lower[:, :cols]))
                at += 2 * rows
            results.append(parts)
        return results

    total = total_ref[...] + arrived(second_ref, 1, pair_count)
    pairs = range(pair_count)
    grams = [total[p * members : (p + 1) * members] for p in pairs]
    squares = jnp.concatenate([jnp.sum(gram * gram, axis=0, keepdims=True) for gram in grams], 0)
    at_left = lax.broadcasted_iota(jnp.int32, squares.shape, 1) < members
    norm_left = jnp.sum(jnp.where(at_left, squares, 0.0), axis=1, keepdims=True)
    norm_right = jnp.sum(jnp.where(at_left, 0.0, squares), axis=1, keepdims=True)
    bounds = degree + jnp.sqrt(jnp.where(at_left, norm_left, norm_right))
    inverses = 1.0 / bounds
    spreads = jnp.sqrt(degree * inverses)
    sides = [jnp.broadcast_to(total[grams_end + p : grams_end + p + 1], (PATCH, cols)) for p in pairs]
    iterates = [(grams[p] + degree * identity) * inverses[p : p + 1] for p in pairs]
    roots = [None for _ in pairs]
    for step in range(NS_STEPS):
        lefts = [[halves] for halves in splits(sides)]
        if step == 0:
            ahead = iterates
        else:
            root_halves = splits(roots)
            lefts = [left + [halves] for left, halves in zip(lefts, root_halves)]
            ahead = [parts[0] for parts in products([[halves] for halves in root_halves], rights(iterates))]
        if step < NS_STEPS - 1:
            lefts = [left + [halves] for left, halves in zip(lefts, splits(iterates))]
        corrections = [1.5 * identity - 0.5 * product for product in ahead]
        results = products(lefts, rights(corrections))
        sides = [parts[0] for parts in results]
        roots = corrections if step == 0 else [parts[1] for parts in results]
        iterates = [parts[-1] for parts in results]
    weights = [parts[0][:1] for parts in products([[halves] for halves in splits(sides)], rights(roots))]
    weights = [weights[p] * inverses[p : p + 1] for p in pairs]
    mixings = [(spreads[p : p + 1] * roots[p] + weights[p]).astype(bf16) for p in pairs]

    patch = lax.broadcasted_iota(jnp.int32, (members, cols), 1) // PATCH
    masks = [jnp.where(patch % 4 == k, 1.0, 0.0).astype(bf16) for k in range(4)]
    quads = cols // (4 * PATCH)
    for a in range(tile_rows // PATCH):
        mixing = jnp.concatenate(
            [jnp.concatenate(mixings[2 * q : 2 * q + 2], 1) for q in range(a * quads, (a + 1) * quads)], 0
        )
        for r in range(a * PATCH, (a + 1) * PATCH, 2):
            state = jnp.concatenate(
                [jnp.concatenate([lag_ref[i] * mask for mask in masks], 0) for i in (r, r + 1)], 1
            )
            spread_out = mm(mixing, state)
            for i in (0, 1):
                part = spread_out[:, i * cols : (i + 1) * cols]
                chosen = part[:members]
                for q in range(1, quads):
                    chosen = jnp.where(patch // 4 == q, part[q * members : (q + 1) * members], chosen)
                flat_ref[pl.ds(r + i, members, stride=tile_rows), :] = chosen + mean_ref[r + i : r + i + 1, :]
    out_ref[...] = flat_ref[...].reshape(1, members, tile_rows, cols).astype(bf16)


def shards(history, forecast, spot, alive, levels, precision, radius):
    shares = lax.axis_size("lag")
    tiles = lax.axis_size("dom")
    share_members, tile_rows, cols = forecast.shape
    members = share_members * shares
    patch_cols = cols // PATCH
    def call(kernel, name, in_specs, out_shape, scratch=()):
        return pl.pallas_call(
            kernel,
            in_specs=in_specs,
            out_specs=jax.tree.map(lambda _: vmem, out_shape),
            out_shape=out_shape,
            scratch_shapes=scratch,
            compiler_params=pltpu.CompilerParams(vmem_limit_bytes=32 * 2**20),
            name=name,
        )

    shape = jax.ShapeDtypeStruct
    vmem = pl.BlockSpec(memory_space=pltpu.VMEM)
    lag = lax.axis_index("lag")
    most_parts, rest_parts = [forecast], [forecast]
    for k in range(1, shares):
        half = lax.rem(lag + shares - k, shares) // (shares // 2)
        pairs = [((i + k) % shares, i) for i in range(shares)]
        most = lax.dynamic_slice_in_dim(forecast, half * (tile_rows - FAR), FAR, 1)
        most_parts.append(lax.ppermute(most, "lag", pairs))
    live = lax.broadcasted_iota(jnp.int32, spot.shape, 1) < alive[:, None]
    weights = jnp.where(live, precision, 0.0)
    kind = lax.broadcasted_iota(jnp.int32, (3, *spot.shape), 0)
    tables = jnp.where(kind == 0, weights[None], jnp.where(kind == 1, (weights * levels)[None], spot.astype(f32)[None]))
    inverse = jnp.broadcast_to(
        (1.0 / jnp.square(radius.astype(f32))).reshape(-1, patch_cols, 1), (tile_rows // PATCH, patch_cols, cols)
    )
    sent, tables = lax.optimization_barrier((inverse, tables))
    rings = [ring(tiles, shares, turn) for turn in range(2)]
    axes = ("dom", "lag")
    next_inverses = [lax.ppermute(sent, axes, [(t, s) for s, t in pairs]) for pairs in rings]
    fields, own_sum = call(
        functools.partial(fields_kernel, cols),
        "fields",
        [vmem, vmem],
        [shape((2, tile_rows, cols), f32), shape((tile_rows, cols), f32)],
    )(tables, forecast)
    fields, later = lax.optimization_barrier((fields, forecast))
    for k in range(1, shares):
        half = lax.rem(lag + shares - k, shares) // (shares // 2)
        rest = lax.dynamic_slice_in_dim(later, (1 - half) * FAR, tile_rows - FAR, 1)
        rest_parts.append(lax.ppermute(rest, "lag", [((i + k) % shares, i) for i in range(shares)]))
    pair_rows = patch_cols * members
    message_shape = shape((pair_rows + 2 * patch_cols, 2 * members), bf16)
    total_scratch = pltpu.VMEM((2, patch_cols * members + PATCH, members), f32)
    def run_shapes(count):
        return [shape((count, members, cols), bf16), shape((2, count, cols), f32), message_shape]

    def run_scratch(count):
        return [pltpu.VMEM((members * count, cols), f32), total_scratch]

    most, most_held, message = call(
        functools.partial(first_kernel, shares), "first_gram", [vmem] * (shares + 3), run_shapes(FAR), run_scratch(FAR)
    )(*most_parts, own_sum, fields, next_inverses[0])
    first = lax.ppermute(message, axes, rings[0])
    left = tile_rows - FAR
    rest, rest_held, message = call(
        functools.partial(second_kernel, shares), "second_gram", [vmem] * (shares + 5), run_shapes(left), run_scratch(left)
    )(*rest_parts, own_sum, fields, most, most_held, next_inverses[1])
    second = lax.ppermute(message, axes, rings[1])
    lag_rows, lag_mean = call(
        state_kernel,
        "state",
        [vmem, vmem],
        [shape((tile_rows, members, cols), bf16), shape((tile_rows, cols), f32)],
        [pltpu.VMEM((members * tile_rows, cols), f32)],
    )(most_held, history[0])
    own_shape = shape((pair_rows + patch_cols, 2 * members), f32)
    own = call(own_kernel, "own_gram", [vmem] * 7, own_shape)(
        lag_mean, most, most_held, rest, rest_held, inverse, first
    )
    return call(
        finish_kernel,
        "finish",
        [vmem] * 4,
        shape((1, members, tile_rows, cols), bf16),
        [pltpu.VMEM((members * tile_rows, cols), f32)],
    )(own, second, lag_rows, lag_mean)


def solution(mesh):
    in_specs = (
        P("lag", None, "dom", None),
        P("lag", "dom", None),
        P("dom", None),
        P("dom"),
        P("dom", None),
        P("dom", None),
        P("dom"),
    )
    out_specs = P("lag", None, "dom", None)
    return jax.shard_map(shards, mesh=mesh, in_specs=in_specs, out_specs=out_specs, check_vma=False)
```

```python
import functools

import jax
import jax.numpy as jnp
from jax import lax
from jax.experimental import pallas as pl
from jax.experimental.pallas import tpu as pltpu
from jax.sharding import PartitionSpec as P

PATCH = 16
NS_STEPS = 4
RADIUS = 32
FAR = RADIUS - PATCH // 2
NEAR = FAR - PATCH
MIDDLE = (PATCH - 1) / 2

NT = (((1,), (1,)), ((), ()))
NN = (((1,), (0,)), ((), ()))
f32 = jnp.float32
bf16 = jnp.bfloat16


def mm(a, b, dims=NN):
    return lax.dot_general(a, b, dims, preferred_element_type=f32)


def split(x):
    high = x.astype(bf16)
    return high, (x - high.astype(f32)).astype(bf16)


def fields_kernel(cols, table_ref, part_ref, field_ref, sum_ref):
    sum_ref[...] = jnp.sum(part_ref[...].astype(f32), axis=0)
    patches, slots = table_ref.shape[1:]
    patch_cols = cols // PATCH
    patch_rows = patches // patch_cols
    spot = table_ref[2].astype(jnp.int32)
    row_in = spot // PATCH
    col_in = spot % PATCH
    iota_row = lax.broadcasted_iota(jnp.int32, (PATCH, slots), 0)
    iota_col = lax.broadcasted_iota(jnp.int32, (cols, slots), 0)
    for a in range(patch_rows):
        total = jnp.zeros((4 * PATCH, cols), f32)
        for b in range(patch_cols):
            p = a * patch_cols + b
            prec = table_ref[0, p : p + 1, :]
            level = table_ref[1, p : p + 1, :]
            prec_high = prec.astype(bf16).astype(f32)
            level_high = level.astype(bf16).astype(f32)
            on_row = row_in[p : p + 1, :] == iota_row
            pieces = [
                jnp.where(on_row, piece, 0.0).astype(bf16)
                for piece in (prec_high, prec - prec_high, level_high, level - level_high)
            ]
            on_col = jnp.where(col_in[p : p + 1, :] + b * PATCH == iota_col, 1.0, 0.0).astype(bf16)
            total = total + mm(jnp.concatenate(pieces, 0), on_col, NT)
        rows = slice(a * PATCH, (a + 1) * PATCH)
        field_ref[0, rows, :] = total[:PATCH] + total[PATCH : 2 * PATCH]
        field_ref[1, rows, :] = total[2 * PATCH : 3 * PATCH] + total[3 * PATCH :]


def state_kernel(after_ref, hist_ref, lag_ref, mean_ref, flat_ref):
    members, tile_rows, cols = hist_ref.shape
    state = hist_ref[...].astype(f32)
    mean = jnp.sum(state, axis=0) / members
    mean_ref[...] = mean
    flat_ref[...] = (state - mean[None]).reshape(members * tile_rows, cols)
    for r in range(tile_rows):
        lag_ref[r] = flat_ref[pl.ds(r, members, stride=tile_rows), :].astype(bf16)


def half_of_lags():
    return lax.axis_index("lag") // (lax.axis_size("lag") // 2)


def ring(tiles, shares, turn):
    half = shares // 2
    pairs = []
    for t in range(tiles):
        for l in range(shares):
            target = t + (1 if (l // half) ^ turn else -1)
            if 0 <= target < tiles:
                pairs.append((t * shares + l, target * shares + l))
            else:
                pairs.append((t * shares + l, t * shares + (l + half) % shares))
    return pairs


def taper_plan(centre_row, inverse_square):
    q_row = lax.broadcasted_iota(jnp.int32, inverse_square.shape, 0)
    col = lax.broadcasted_iota(jnp.int32, inverse_square.shape, 1)
    col_square = jnp.square(col.astype(f32) - (q_row.astype(f32) * PATCH + MIDDLE))
    return centre_row, col_square, inverse_square


def accumulate(total, plan, anomalies, weight, innovation, first_row):
    centre_row, col_square, inverse_square = plan
    patches, cols = col_square.shape
    lefts = []
    for i, anomaly in enumerate(anomalies):
        members = anomaly.shape[0]
        offset = (first_row + i).astype(f32) - centre_row
        taper = jnp.square(jnp.maximum(0.0, 1.0 - (offset * offset + col_square) * inverse_square))
        scale = taper * weight[i : i + 1]
        blocks = anomaly.reshape(members // PATCH, PATCH, cols)
        left = [
            (blocks * jnp.broadcast_to(scale[q : q + 1], (PATCH, cols)).astype(bf16)[None]).reshape(members, cols)
            for q in range(patches)
        ]
        tail = taper * innovation[i : i + 1]
        left.append(jnp.concatenate([tail, jnp.zeros((PATCH - patches, cols), f32)], 0).astype(bf16))
        lefts.append(jnp.concatenate(left, 0))
    return total + mm(jnp.concatenate(lefts, 1), jnp.concatenate(anomalies, 1), NT)


STEP = 8


def paired(totals, members, patch_cols):
    pairs = patch_cols // 2
    grams, sides = [], []
    for total in totals:
        for pair in range(pairs):
            at = 2 * pair * members
            grams.append(jnp.concatenate([total[at : at + members], total[at + members : at + 2 * members]], 1))
        for pair in range(pairs):
            at = patch_cols * members + 2 * pair
            sides.append(jnp.concatenate([total[at : at + 1], total[at + 1 : at + 2]], 1))
    return jnp.concatenate(grams, 0), jnp.concatenate(sides, 0)


def message_of(grams, sides):
    return jnp.concatenate([grams.astype(bf16), *split(sides)], 0)


def read_message(ref, side_count):
    at = ref.shape[0] - 2 * side_count
    high, low = ref[at : at + side_count, :].astype(f32), ref[at + side_count :, :].astype(f32)
    return jnp.concatenate([ref[:at, :].astype(f32), high + low], 0)


def arrived(ref, turn, side_count):
    tile = lax.axis_index("dom")
    there = jnp.where(half_of_lags() ^ turn == 1, tile > 0, tile < lax.axis_size("dom") - 1)
    return jnp.where(there, read_message(ref, side_count), 0.0)


def outward(down, near_rows, near_fields, far_rows, far_fields, tile_rows, inverse_ref, message_ref, total_ref):
    members, cols = near_rows[0].shape
    patch_cols = cols // PATCH
    middle = jnp.where(down == 0, MIDDLE - PATCH, MIDDLE + tile_rows)
    plans = [
        taper_plan(middle, inverse_ref[1 - down]),
        taper_plan(middle + jnp.where(down == 0, -PATCH, PATCH).astype(f32), inverse_ref[down]),
    ]
    blank = jnp.zeros(total_ref.shape[1:], f32)
    near = down * (tile_rows - NEAR)
    totals = [accumulate(blank, plan, near_rows, *near_fields, near) for plan in plans]
    for start in range(0, FAR - NEAR, STEP):
        rows = slice(start, start + STEP)
        totals[0] = accumulate(
            totals[0], plans[0], far_rows[rows], *[field[rows] for field in far_fields], jnp.int32(NEAR + start)
        )
    total_ref[1 - down] = totals[0]
    total_ref[down] = totals[1]
    message_ref[...] = message_of(*paired([total_ref[0], total_ref[1]], members, patch_cols))


def centre(first, parts, sum_ref, field_ref, held_ref, rows_ref, flat_ref):
    count, members, cols = rows_ref.shape
    tile_rows = parts[0].shape[1]
    shares = len(parts)
    share_members = members // shares
    lag = lax.axis_index("lag")
    late = tile_rows - count
    whole = parts[0][...].astype(f32)
    states = [jnp.where(first == 0, whole[:, :count], whole[:, late:])] + [part[...].astype(f32) for part in parts[1:]]
    run = pl.ds(pl.multiple_of(first, 8), count)
    mean = functools.reduce(jnp.add, [jnp.sum(state, axis=0) for state in states[1:]], sum_ref[run, :]) / members
    for k, state in enumerate(states):
        at = pl.multiple_of(lax.rem(lag + k, shares) * (share_members * count), 8)
        flat_ref[pl.ds(at, share_members * count), :] = (state - mean[None]).reshape(-1, cols)
    weight = field_ref[0, run, :]
    held_ref[0] = weight
    held_ref[1] = field_ref[1, run, :] - mean * weight
    for r in range(count):
        rows_ref[r] = flat_ref[pl.ds(r, members, stride=count), :].astype(bf16)


def far_run(down, rows_ref, held_ref):
    at = pl.multiple_of((1 - down) * NEAR, 8)
    rows = [rows_ref[at + i] for i in range(FAR - NEAR)]
    return rows, [held_ref[k, pl.ds(at, FAR - NEAR), :] for k in range(2)]


def first_kernel(shares, *refs):
    parts, refs = refs[:shares], refs[shares:]
    sum_ref, field_ref, inverse_ref, rows_ref, held_ref, message_ref, flat_ref, total_ref = refs
    down = half_of_lags()
    tile_rows = parts[0].shape[1]
    centre(down * (tile_rows - FAR), parts, sum_ref, field_ref, held_ref, rows_ref, flat_ref)
    at = pl.multiple_of(down * (FAR - NEAR), 8)
    near_rows = [rows_ref[at + i] for i in range(NEAR)]
    near_fields = [held_ref[k, pl.ds(at, NEAR), :] for k in range(2)]
    outward(
        down, near_rows, near_fields, *far_run(down, rows_ref, held_ref), tile_rows, inverse_ref, message_ref, total_ref
    )


def second_kernel(shares, *refs):
    parts, refs = refs[:shares], refs[shares:]
    sum_ref, field_ref, most_ref, most_held_ref, inverse_ref, rows_ref, held_ref, message_ref, flat_ref, total_ref = refs
    down = half_of_lags()
    tile_rows = parts[0].shape[1]
    centre((1 - down) * (tile_rows - NEAR), parts, sum_ref, field_ref, held_ref, rows_ref, flat_ref)
    near_rows = [rows_ref[i] for i in range(NEAR)]
    near_fields = [held_ref[k] for k in range(2)]
    outward(
        1 - down, near_rows, near_fields, *far_run(down, most_ref, most_held_ref), tile_rows, inverse_ref, message_ref, total_ref
    )


def own_kernel(after_ref, most_ref, most_held_ref, rest_ref, rest_held_ref, inverse_ref, first_ref, out_ref):
    members, cols = most_ref.shape[1:]
    patch_rows, patch_cols = inverse_ref.shape[:2]
    down = half_of_lags()
    plans = [taper_plan(MIDDLE + a * PATCH, inverse_ref[a]) for a in range(patch_rows)]
    totals = [jnp.zeros((patch_cols * members + PATCH, members), f32) for _ in plans]
    tile_rows = patch_rows * PATCH
    for first, rows_ref, held_ref in (
        (down * (tile_rows - FAR), most_ref, most_held_ref),
        ((1 - down) * (tile_rows - NEAR), rest_ref, rest_held_ref),
    ):
        for start in range(0, rows_ref.shape[0], STEP):
            anomalies = [rows_ref[start + i] for i in range(STEP)]
            fields = [held_ref[k, start : start + STEP, :] for k in range(2)]
            totals = [accumulate(total, plan, anomalies, *fields, first + start) for total, plan in zip(totals, plans)]
    sums = jnp.concatenate(paired(totals, members, patch_cols), 0)
    out_ref[...] = sums + arrived(first_ref, 0, patch_cols)


def finish_kernel(total_ref, second_ref, lag_ref, mean_ref, out_ref, flat_ref):
    tile_rows, members, cols = lag_ref.shape
    degree = members - 1.0
    pair_count = total_ref.shape[0] // members
    grams_end = pair_count * members
    row = lax.broadcasted_iota(jnp.int32, (members, cols), 0)
    lane = lax.broadcasted_iota(jnp.int32, (members, cols), 1)
    identity = jnp.where(row == lane % members, 1.0, 0.0)
    left_mask = jnp.where(lane < members, 1.0, 0.0).astype(bf16)
    right_mask = jnp.where(lane < members, 0.0, 1.0).astype(bf16)

    def splits(parts):
        highs = [part.astype(bf16) for part in parts]
        rests = [part - high.astype(f32) for part, high in zip(parts, highs)]
        return list(zip(highs, [rest.astype(bf16) for rest in rests]))

    def rights(parts):
        return [
            jnp.concatenate(
                [jnp.concatenate([half * mask for half in halves], 1) for mask in (left_mask, right_mask)], 0
            )
            for halves in splits(parts)
        ]

    def products(lefts, factors):
        stacks = [jnp.concatenate([half for halves in left for half in halves], 0) for left in lefts]
        boths = [mm(stack, factor) for stack, factor in zip(stacks, factors)]
        results = []
        for left, both in zip(lefts, boths):
            parts, at = [], 0
            for high, low in left:
                rows = high.shape[0]
                upper, lower = both[at : at + rows], both[at + rows : at + 2 * rows]
                parts.append(upper[:, :cols] + (upper[:, cols:] + lower[:, :cols]))
                at += 2 * rows
            results.append(parts)
        return results

    total = total_ref[...] + arrived(second_ref, 1, pair_count)
    pairs = range(pair_count)
    grams = [total[p * members : (p + 1) * members] for p in pairs]
    squares = jnp.concatenate([jnp.sum(gram * gram, axis=0, keepdims=True) for gram in grams], 0)
    at_left = lax.broadcasted_iota(jnp.int32, squares.shape, 1) < members
    norm_left = jnp.sum(jnp.where(at_left, squares, 0.0), axis=1, keepdims=True)
    norm_right = jnp.sum(jnp.where(at_left, 0.0, squares), axis=1, keepdims=True)
    bounds = degree + jnp.sqrt(jnp.where(at_left, norm_left, norm_right))
    inverses = 1.0 / bounds
    spreads = jnp.sqrt(degree * inverses)
    sides = [jnp.broadcast_to(total[grams_end + p : grams_end + p + 1], (PATCH, cols)) for p in pairs]
    iterates = [(grams[p] + degree * identity) * inverses[p : p + 1] for p in pairs]
    roots = [None for _ in pairs]
    for step in range(NS_STEPS):
        lefts = [[halves] for halves in splits(sides)]
        if step == 0:
            ahead = iterates
        else:
            root_halves = splits(roots)
            lefts = [left + [halves] for left, halves in zip(lefts, root_halves)]
            ahead = [parts[0] for parts in products([[halves] for halves in root_halves], rights(iterates))]
        if step < NS_STEPS - 1:
            lefts = [left + [halves] for left, halves in zip(lefts, splits(iterates))]
        corrections = [1.5 * identity - 0.5 * product for product in ahead]
        results = products(lefts, rights(corrections))
        sides = [parts[0] for parts in results]
        roots = corrections if step == 0 else [parts[1] for parts in results]
        iterates = [parts[-1] for parts in results]
    weights = [parts[0][:1] for parts in products([[halves] for halves in splits(sides)], rights(roots))]
    weights = [weights[p] * inverses[p : p + 1] for p in pairs]
    mixings = [(spreads[p : p + 1] * roots[p] + weights[p]).astype(bf16) for p in pairs]

    patch = lax.broadcasted_iota(jnp.int32, (members, cols), 1) // PATCH
    masks = [jnp.where(patch % 4 == k, 1.0, 0.0).astype(bf16) for k in range(4)]
    quads = cols // (4 * PATCH)
    for a in range(tile_rows // PATCH):
        mixing = jnp.concatenate(
            [jnp.concatenate(mixings[2 * q : 2 * q + 2], 1) for q in range(a * quads, (a + 1) * quads)], 0
        )
        for r in range(a * PATCH, (a + 1) * PATCH, 2):
            state = jnp.concatenate(
                [jnp.concatenate([lag_ref[i] * mask for mask in masks], 0) for i in (r, r + 1)], 1
            )
            spread_out = mm(mixing, state)
            for i in (0, 1):
                part = spread_out[:, i * cols : (i + 1) * cols]
                chosen = part[:members]
                for q in range(1, quads):
                    chosen = jnp.where(patch // 4 == q, part[q * members : (q + 1) * members], chosen)
                flat_ref[pl.ds(r + i, members, stride=tile_rows), :] = chosen + mean_ref[r + i : r + i + 1, :]
    out_ref[...] = flat_ref[...].reshape(1, members, tile_rows, cols).astype(bf16)


def shards(history, forecast, spot, alive, levels, precision, radius):
    shares = lax.axis_size("lag")
    tiles = lax.axis_size("dom")
    share_members, tile_rows, cols = forecast.shape
    members = share_members * shares
    patch_cols = cols // PATCH
    def call(kernel, name, in_specs, out_shape, scratch=()):
        return pl.pallas_call(
            kernel,
            in_specs=in_specs,
            out_specs=jax.tree.map(lambda _: vmem, out_shape),
            out_shape=out_shape,
            scratch_shapes=scratch,
            compiler_params=pltpu.CompilerParams(vmem_limit_bytes=32 * 2**20),
            name=name,
        )

    shape = jax.ShapeDtypeStruct
    vmem = pl.BlockSpec(memory_space=pltpu.VMEM)
    lag = lax.axis_index("lag")
    most_parts, rest_parts = [forecast], [forecast]
    for k in range(1, shares):
        half = lax.rem(lag + shares - k, shares) // (shares // 2)
        pairs = [((i + k) % shares, i) for i in range(shares)]
        most = lax.dynamic_slice_in_dim(forecast, half * (tile_rows - FAR), FAR, 1)
        most_parts.append(lax.ppermute(most, "lag", pairs))
    live = lax.broadcasted_iota(jnp.int32, spot.shape, 1) < alive[:, None]
    weights = jnp.where(live, precision, 0.0)
    kind = lax.broadcasted_iota(jnp.int32, (3, *spot.shape), 0)
    tables = jnp.where(kind == 0, weights[None], jnp.where(kind == 1, (weights * levels)[None], spot.astype(f32)[None]))
    inverse = jnp.broadcast_to(
        (1.0 / jnp.square(radius.astype(f32))).reshape(-1, patch_cols, 1), (tile_rows // PATCH, patch_cols, cols)
    )
    sent, tables = lax.optimization_barrier((inverse, tables))
    rings = [ring(tiles, shares, turn) for turn in range(2)]
    axes = ("dom", "lag")
    next_inverses = [lax.ppermute(sent, axes, [(t, s) for s, t in pairs]) for pairs in rings]
    fields, own_sum = call(
        functools.partial(fields_kernel, cols),
        "fields",
        [vmem, vmem],
        [shape((2, tile_rows, cols), f32), shape((tile_rows, cols), f32)],
    )(tables, forecast)
    fields, later, next_inverses = lax.optimization_barrier((fields, forecast, next_inverses))
    for k in range(1, shares):
        half = lax.rem(lag + shares - k, shares) // (shares // 2)
        rest = lax.dynamic_slice_in_dim(later, (1 - half) * FAR, tile_rows - FAR, 1)
        rest_parts.append(lax.ppermute(rest, "lag", [((i + k) % shares, i) for i in range(shares)]))
    pair_rows = patch_cols * members
    message_shape = shape((pair_rows + 2 * patch_cols, 2 * members), bf16)
    total_scratch = pltpu.VMEM((2, patch_cols * members + PATCH, members), f32)
    def run_shapes(count):
        return [shape((count, members, cols), bf16), shape((2, count, cols), f32), message_shape]

    def run_scratch(count):
        return [pltpu.VMEM((members * count, cols), f32), total_scratch]

    most, most_held, message = call(
        functools.partial(first_kernel, shares), "first_gram", [vmem] * (shares + 3), run_shapes(FAR), run_scratch(FAR)
    )(*most_parts, own_sum, fields, next_inverses[0])
    first = lax.ppermute(message, axes, rings[0])
    left = tile_rows - FAR
    rest, rest_held, message = call(
        functools.partial(second_kernel, shares), "second_gram", [vmem] * (shares + 5), run_shapes(left), run_scratch(left)
    )(*rest_parts, own_sum, fields, most, most_held, next_inverses[1])
    second = lax.ppermute(message, axes, rings[1])
    lag_rows, lag_mean = call(
        state_kernel,
        "state",
        [vmem, vmem],
        [shape((tile_rows, members, cols), bf16), shape((tile_rows, cols), f32)],
        [pltpu.VMEM((members * tile_rows, cols), f32)],
    )(most_held, history[0])
    own_shape = shape((pair_rows + patch_cols, 2 * members), f32)
    own = call(own_kernel, "own_gram", [vmem] * 7, own_shape)(
        lag_mean, most, most_held, rest, rest_held, inverse, first
    )
    return call(
        finish_kernel,
        "finish",
        [vmem] * 4,
        shape((1, members, tile_rows, cols), bf16),
        [pltpu.VMEM((members * tile_rows, cols), f32)],
    )(own, second, lag_rows, lag_mean)


def solution(mesh):
    in_specs = (
        P("lag", None, "dom", None),
        P("lag", "dom", None),
        P("dom", None),
        P("dom"),
        P("dom", None),
        P("dom", None),
        P("dom"),
    )
    out_specs = P("lag", None, "dom", None)
    return jax.shard_map(shards, mesh=mesh, in_specs=in_specs, out_specs=out_specs, check_vma=False)
```

```python
import functools

import jax
import jax.numpy as jnp
from jax import lax
from jax.experimental import pallas as pl
from jax.experimental.pallas import tpu as pltpu
from jax.sharding import PartitionSpec as P

PATCH = 16
NS_STEPS = 4
RADIUS = 32
FAR = RADIUS - PATCH // 2
NEAR = FAR - PATCH
MIDDLE = (PATCH - 1) / 2

NT = (((1,), (1,)), ((), ()))
NN = (((1,), (0,)), ((), ()))
f32 = jnp.float32
bf16 = jnp.bfloat16


def mm(a, b, dims=NN):
    return lax.dot_general(a, b, dims, preferred_element_type=f32)


def split(x):
    high = x.astype(bf16)
    return high, (x - high.astype(f32)).astype(bf16)


def fields_kernel(cols, table_ref, part_ref, field_ref, sum_ref):
    sum_ref[...] = jnp.sum(part_ref[...].astype(f32), axis=0)
    patches, slots = table_ref.shape[1:]
    patch_cols = cols // PATCH
    patch_rows = patches // patch_cols
    spot = table_ref[2].astype(jnp.int32)
    row_in = spot // PATCH
    col_in = spot % PATCH
    iota_row = lax.broadcasted_iota(jnp.int32, (PATCH, slots), 0)
    iota_col = lax.broadcasted_iota(jnp.int32, (cols, slots), 0)
    for a in range(patch_rows):
        total = jnp.zeros((4 * PATCH, cols), f32)
        for b in range(patch_cols):
            p = a * patch_cols + b
            prec = table_ref[0, p : p + 1, :]
            level = table_ref[1, p : p + 1, :]
            prec_high = prec.astype(bf16).astype(f32)
            level_high = level.astype(bf16).astype(f32)
            on_row = row_in[p : p + 1, :] == iota_row
            pieces = [
                jnp.where(on_row, piece, 0.0).astype(bf16)
                for piece in (prec_high, prec - prec_high, level_high, level - level_high)
            ]
            on_col = jnp.where(col_in[p : p + 1, :] + b * PATCH == iota_col, 1.0, 0.0).astype(bf16)
            total = total + mm(jnp.concatenate(pieces, 0), on_col, NT)
        rows = slice(a * PATCH, (a + 1) * PATCH)
        field_ref[0, rows, :] = total[:PATCH] + total[PATCH : 2 * PATCH]
        field_ref[1, rows, :] = total[2 * PATCH : 3 * PATCH] + total[3 * PATCH :]


def state_kernel(after_ref, hist_ref, lag_ref, mean_ref, flat_ref):
    members, tile_rows, cols = hist_ref.shape
    state = hist_ref[...].astype(f32)
    mean = jnp.sum(state, axis=0) / members
    mean_ref[...] = mean
    flat_ref[...] = (state - mean[None]).reshape(members * tile_rows, cols)
    for r in range(tile_rows):
        lag_ref[r] = flat_ref[pl.ds(r, members, stride=tile_rows), :].astype(bf16)


def half_of_lags():
    return lax.axis_index("lag") // (lax.axis_size("lag") // 2)


def ring(tiles, shares, turn):
    half = shares // 2
    pairs = []
    for t in range(tiles):
        for l in range(shares):
            target = t + (1 if (l // half) ^ turn else -1)
            if 0 <= target < tiles:
                pairs.append((t * shares + l, target * shares + l))
            else:
                pairs.append((t * shares + l, t * shares + (l + half) % shares))
    return pairs


def taper_plan(centre_row, inverse_square):
    q_row = lax.broadcasted_iota(jnp.int32, inverse_square.shape, 0)
    col = lax.broadcasted_iota(jnp.int32, inverse_square.shape, 1)
    col_square = jnp.square(col.astype(f32) - (q_row.astype(f32) * PATCH + MIDDLE))
    return centre_row, col_square, inverse_square


def accumulate(total, plan, anomalies, weight, innovation, first_row):
    centre_row, col_square, inverse_square = plan
    patches, cols = col_square.shape
    lefts = []
    for i, anomaly in enumerate(anomalies):
        members = anomaly.shape[0]
        offset = (first_row + i).astype(f32) - centre_row
        taper = jnp.square(jnp.maximum(0.0, 1.0 - (offset * offset + col_square) * inverse_square))
        scale = taper * weight[i : i + 1]
        blocks = anomaly.reshape(members // PATCH, PATCH, cols)
        left = [
            (blocks * jnp.broadcast_to(scale[q : q + 1], (PATCH, cols)).astype(bf16)[None]).reshape(members, cols)
            for q in range(patches)
        ]
        tail = taper * innovation[i : i + 1]
        left.append(jnp.concatenate([tail, jnp.zeros((PATCH - patches, cols), f32)], 0).astype(bf16))
        lefts.append(jnp.concatenate(left, 0))
    return total + mm(jnp.concatenate(lefts, 1), jnp.concatenate(anomalies, 1), NT)


STEP = 8


def packed(totals, members, patch_cols):
    pairs = patch_cols // 2
    half = members // 2
    grams, sides = [], []
    for total in totals:
        for pair in range(pairs):
            at = 2 * pair * members
            grams.append(jnp.concatenate([total[at : at + members], total[at + members : at + 2 * members]], 1))
        for pair in range(pairs):
            at = patch_cols * members + 2 * pair
            sides.append(jnp.concatenate([total[at : at + 1], total[at + 1 : at + 2]], 1))
    lane = lax.broadcasted_iota(jnp.int32, (half, 2 * members), 1)
    tops = [gram[:half] for gram in grams]
    ends = [
        jnp.where(lane % members < half, pltpu.roll(a[half:], 2 * members - half, 1), b[half:])
        for a, b in zip(grams[::2], grams[1::2])
    ]
    return jnp.concatenate(tops + ends, 0), jnp.concatenate(sides, 0)


def unpacked(rows, members):
    half = members // 2
    wide = 2 * members
    count = rows.shape[0] * 2 // (3 * half)
    lane = lax.broadcasted_iota(jnp.int32, (half, wide), 1)
    tops = [rows[p * half : (p + 1) * half] for p in range(count)]
    ends = [rows[(count + k) * half : (count + k + 1) * half] for k in range(count // 2)]
    per_square = wide // half
    turned = [
        jnp.transpose(jnp.concatenate(tops[p : p + per_square], 0)) for p in range(0, count, per_square)
    ]
    grams = []
    for p in range(count):
        square, at = turned[p // per_square], (p % per_square) * half
        first = pltpu.roll(square[half:members], (wide - at) % wide, 1)
        second = pltpu.roll(square[members + half :], (members + wide - at) % wide, 1)
        corner = ends[p // 2] if p % 2 else pltpu.roll(ends[p // 2], half, 1)
        bottom = jnp.where(lane % members < half, jnp.where(lane < members, first, second), corner)
        grams.append(jnp.concatenate([tops[p], bottom], 0))
    return grams


def message_of(grams, sides):
    return jnp.concatenate([grams.astype(bf16), *split(sides)], 0)


def read_message(ref, side_count):
    at = ref.shape[0] - 2 * side_count
    high, low = ref[at : at + side_count, :].astype(f32), ref[at + side_count :, :].astype(f32)
    return jnp.concatenate([ref[:at, :].astype(f32), high + low], 0)


def arrived(ref, turn, side_count):
    tile = lax.axis_index("dom")
    there = jnp.where(half_of_lags() ^ turn == 1, tile > 0, tile < lax.axis_size("dom") - 1)
    return jnp.where(there, read_message(ref, side_count), 0.0)


def outward(turn, rows_ref, held_ref, inverse_ref, message_ref, total_ref):
    tile_rows, members, cols = rows_ref.shape
    patch_cols = cols // PATCH
    down = half_of_lags() ^ turn
    near = pl.multiple_of(down * (tile_rows - NEAR), 8)
    middle = jnp.where(down == 0, MIDDLE - PATCH, MIDDLE + tile_rows)
    plans = [
        taper_plan(middle, inverse_ref[1 - down]),
        taper_plan(middle + jnp.where(down == 0, -PATCH, PATCH).astype(f32), inverse_ref[down]),
    ]
    anomalies = [rows_ref[near + i] for i in range(NEAR)]
    fields = [held_ref[k, pl.ds(near, NEAR), :] for k in range(2)]
    blank = jnp.zeros(total_ref.shape[1:], f32)
    totals = [accumulate(blank, plan, anomalies, *fields, near) for plan in plans]
    for start in range(NEAR, FAR, STEP):
        anomalies = [rows_ref[start + i] for i in range(STEP)]
        fields = [held_ref[k, start : start + STEP, :] for k in range(2)]
        totals[0] = accumulate(totals[0], plans[0], anomalies, *fields, jnp.int32(start))
    total_ref[1 - down] = totals[0]
    total_ref[down] = totals[1]
    message_ref[...] = message_of(*packed([total_ref[0], total_ref[1]], members, patch_cols))


def first_kernel(shares, *refs):
    parts, refs = refs[:shares], refs[shares:]
    sum_ref, field_ref, inverse_ref, rows_ref, held_ref, message_ref, flat_ref, total_ref = refs
    share_members, tile_rows, cols = parts[0].shape
    members = share_members * shares
    lag = lax.axis_index("lag")
    states = [part[...].astype(f32) for part in parts]
    mean = functools.reduce(jnp.add, [jnp.sum(state, axis=0) for state in states[1:]], sum_ref[...]) / members
    for k, state in enumerate(states):
        at = pl.multiple_of(lax.rem(lag + k, shares) * (share_members * tile_rows), 8)
        flat_ref[pl.ds(at, share_members * tile_rows), :] = (state - mean[None]).reshape(-1, cols)
    weight = field_ref[0]
    held_ref[0] = weight
    held_ref[1] = field_ref[1] - mean * weight
    for r in range(tile_rows):
        rows_ref[r] = flat_ref[pl.ds(r, members, stride=tile_rows), :].astype(bf16)
    outward(0, rows_ref, held_ref, inverse_ref, message_ref, total_ref)


def second_kernel(rows_ref, held_ref, inverse_ref, message_ref, total_ref):
    outward(1, rows_ref, held_ref, inverse_ref, message_ref, total_ref)


def own_kernel(after_ref, rows_ref, held_ref, inverse_ref, first_ref, out_ref):
    tile_rows, members, cols = rows_ref.shape
    patch_cols = cols // PATCH
    plans = [taper_plan(MIDDLE + a * PATCH, inverse_ref[a]) for a in range(tile_rows // PATCH)]
    totals = [jnp.zeros((patch_cols * members + PATCH, members), f32) for _ in plans]
    for start in range(0, tile_rows, STEP):
        anomalies = [rows_ref[start + i] for i in range(STEP)]
        fields = [held_ref[k, start : start + STEP, :] for k in range(2)]
        totals = [accumulate(total, plan, anomalies, *fields, jnp.int32(start)) for total, plan in zip(totals, plans)]
    sums = jnp.concatenate(packed(totals, members, patch_cols), 0)
    out_ref[...] = sums + arrived(first_ref, 0, patch_cols)


def finish_kernel(total_ref, second_ref, lag_ref, mean_ref, out_ref, flat_ref):
    tile_rows, members, cols = lag_ref.shape
    degree = members - 1.0
    pair_count = (tile_rows // PATCH) * (cols // PATCH) // 2
    grams_end = total_ref.shape[0] - pair_count
    row = lax.broadcasted_iota(jnp.int32, (members, cols), 0)
    lane = lax.broadcasted_iota(jnp.int32, (members, cols), 1)
    identity = jnp.where(row == lane % members, 1.0, 0.0)
    left_mask = jnp.where(lane < members, 1.0, 0.0).astype(bf16)
    right_mask = jnp.where(lane < members, 0.0, 1.0).astype(bf16)

    def splits(parts):
        highs = [part.astype(bf16) for part in parts]
        rests = [part - high.astype(f32) for part, high in zip(parts, highs)]
        return list(zip(highs, [rest.astype(bf16) for rest in rests]))

    def rights(parts):
        return [
            jnp.concatenate(
                [jnp.concatenate([half * mask for half in halves], 1) for mask in (left_mask, right_mask)], 0
            )
            for halves in splits(parts)
        ]

    def products(lefts, factors):
        stacks = [jnp.concatenate([half for halves in left for half in halves], 0) for left in lefts]
        boths = [mm(stack, factor) for stack, factor in zip(stacks, factors)]
        results = []
        for left, both in zip(lefts, boths):
            parts, at = [], 0
            for high, low in left:
                rows = high.shape[0]
                upper, lower = both[at : at + rows], both[at + rows : at + 2 * rows]
                parts.append(upper[:, :cols] + (upper[:, cols:] + lower[:, :cols]))
                at += 2 * rows
            results.append(parts)
        return results

    total = total_ref[...] + arrived(second_ref, 1, pair_count)
    pairs = range(pair_count)
    grams = unpacked(total[:grams_end], members)
    squares = jnp.concatenate([jnp.sum(gram * gram, axis=0, keepdims=True) for gram in grams], 0)
    at_left = lax.broadcasted_iota(jnp.int32, squares.shape, 1) < members
    norm_left = jnp.sum(jnp.where(at_left, squares, 0.0), axis=1, keepdims=True)
    norm_right = jnp.sum(jnp.where(at_left, 0.0, squares), axis=1, keepdims=True)
    bounds = degree + jnp.sqrt(jnp.where(at_left, norm_left, norm_right))
    inverses = 1.0 / bounds
    spreads = jnp.sqrt(degree * inverses)
    sides = [jnp.broadcast_to(total[grams_end + p : grams_end + p + 1], (PATCH, cols)) for p in pairs]
    iterates = [(grams[p] + degree * identity) * inverses[p : p + 1] for p in pairs]
    roots = [None for _ in pairs]
    for step in range(NS_STEPS):
        lefts = [[halves] for halves in splits(sides)]
        if step == 0:
            ahead = iterates
        else:
            root_halves = splits(roots)
            lefts = [left + [halves] for left, halves in zip(lefts, root_halves)]
            ahead = [parts[0] for parts in products([[halves] for halves in root_halves], rights(iterates))]
        if step < NS_STEPS - 1:
            lefts = [left + [halves] for left, halves in zip(lefts, splits(iterates))]
        corrections = [1.5 * identity - 0.5 * product for product in ahead]
        results = products(lefts, rights(corrections))
        sides = [parts[0] for parts in results]
        roots = corrections if step == 0 else [parts[1] for parts in results]
        iterates = [parts[-1] for parts in results]
    weights = [parts[0][:1] for parts in products([[halves] for halves in splits(sides)], rights(roots))]
    weights = [weights[p] * inverses[p : p + 1] for p in pairs]
    mixings = [(spreads[p : p + 1] * roots[p] + weights[p]).astype(bf16) for p in pairs]

    patch = lax.broadcasted_iota(jnp.int32, (members, cols), 1) // PATCH
    masks = [jnp.where(patch % 4 == k, 1.0, 0.0).astype(bf16) for k in range(4)]
    quads = cols // (4 * PATCH)
    for a in range(tile_rows // PATCH):
        mixing = jnp.concatenate(
            [jnp.concatenate(mixings[2 * q : 2 * q + 2], 1) for q in range(a * quads, (a + 1) * quads)], 0
        )
        for r in range(a * PATCH, (a + 1) * PATCH, 2):
            state = jnp.concatenate(
                [jnp.concatenate([lag_ref[i] * mask for mask in masks], 0) for i in (r, r + 1)], 1
            )
            spread_out = mm(mixing, state)
            for i in (0, 1):
                part = spread_out[:, i * cols : (i + 1) * cols]
                chosen = part[:members]
                for q in range(1, quads):
                    chosen = jnp.where(patch // 4 == q, part[q * members : (q + 1) * members], chosen)
                flat_ref[pl.ds(r + i, members, stride=tile_rows), :] = chosen + mean_ref[r + i : r + i + 1, :]
    out_ref[...] = flat_ref[...].reshape(1, members, tile_rows, cols).astype(bf16)


def shards(history, forecast, spot, alive, levels, precision, radius):
    shares = lax.axis_size("lag")
    tiles = lax.axis_size("dom")
    share_members, tile_rows, cols = forecast.shape
    members = share_members * shares
    patch_cols = cols // PATCH
    def call(kernel, name, in_specs, out_shape, scratch=()):
        return pl.pallas_call(
            kernel,
            in_specs=in_specs,
            out_specs=jax.tree.map(lambda _: vmem, out_shape),
            out_shape=out_shape,
            scratch_shapes=scratch,
            compiler_params=pltpu.CompilerParams(vmem_limit_bytes=32 * 2**20),
            name=name,
        )

    shape = jax.ShapeDtypeStruct
    vmem = pl.BlockSpec(memory_space=pltpu.VMEM)
    parts = [forecast]
    for k in range(1, shares):
        parts.append(lax.ppermute(forecast, "lag", [((i + k) % shares, i) for i in range(shares)]))
    live = lax.broadcasted_iota(jnp.int32, spot.shape, 1) < alive[:, None]
    weights = jnp.where(live, precision, 0.0)
    kind = lax.broadcasted_iota(jnp.int32, (3, *spot.shape), 0)
    tables = jnp.where(kind == 0, weights[None], jnp.where(kind == 1, (weights * levels)[None], spot.astype(f32)[None]))
    inverse = jnp.broadcast_to(
        (1.0 / jnp.square(radius.astype(f32))).reshape(-1, patch_cols, 1), (tile_rows // PATCH, patch_cols, cols)
    )
    sent, tables = lax.optimization_barrier((inverse, tables))
    rings = [ring(tiles, shares, turn) for turn in range(2)]
    axes = ("dom", "lag")
    next_inverses = [lax.ppermute(sent, axes, [(t, s) for s, t in pairs]) for pairs in rings]
    fields, own_sum = call(
        functools.partial(fields_kernel, cols),
        "fields",
        [vmem, vmem],
        [shape((2, tile_rows, cols), f32), shape((tile_rows, cols), f32)],
    )(tables, forecast)
    packed_rows = patch_cols * members * 3 // 4
    message_shape = shape((packed_rows + 2 * patch_cols, 2 * members), bf16)
    total_scratch = pltpu.VMEM((2, patch_cols * members + PATCH, members), f32)
    rows, held, message = call(
        functools.partial(first_kernel, shares),
        "first_gram",
        [vmem] * (shares + 3),
        [shape((tile_rows, members, cols), bf16), shape((2, tile_rows, cols), f32), message_shape],
        [pltpu.VMEM((members * tile_rows, cols), f32), total_scratch],
    )(*parts, own_sum, fields, next_inverses[0])
    first = lax.ppermute(message, axes, rings[0])
    message = call(second_kernel, "second_gram", [vmem] * 3, message_shape, [total_scratch])(rows, held, next_inverses[1])
    second = lax.ppermute(message, axes, rings[1])
    lag_rows, lag_mean = call(
        state_kernel,
        "state",
        [vmem, vmem],
        [shape((tile_rows, members, cols), bf16), shape((tile_rows, cols), f32)],
        [pltpu.VMEM((members * tile_rows, cols), f32)],
    )(held, history[0])
    own_shape = shape((packed_rows + patch_cols, 2 * members), f32)
    own = call(own_kernel, "own_gram", [vmem] * 5, own_shape)(lag_mean, rows, held, inverse, first)
    return call(
        finish_kernel,
        "finish",
        [vmem] * 4,
        shape((1, members, tile_rows, cols), bf16),
        [pltpu.VMEM((members * tile_rows, cols), f32)],
    )(own, second, lag_rows, lag_mean)


def solution(mesh):
    in_specs = (
        P("lag", None, "dom", None),
        P("lag", "dom", None),
        P("dom", None),
        P("dom"),
        P("dom", None),
        P("dom", None),
        P("dom"),
    )
    out_specs = P("lag", None, "dom", None)
    return jax.shard_map(shards, mesh=mesh, in_specs=in_specs, out_specs=out_specs, check_vma=False)
```

```python
import functools

import jax
import jax.numpy as jnp
from jax import lax
from jax.experimental import pallas as pl
from jax.experimental.pallas import tpu as pltpu
from jax.sharding import PartitionSpec as P

PATCH = 16
NS_STEPS = 4
RADIUS = 32
FAR = RADIUS - PATCH // 2
NEAR = FAR - PATCH
MIDDLE = (PATCH - 1) / 2

NT = (((1,), (1,)), ((), ()))
NN = (((1,), (0,)), ((), ()))
f32 = jnp.float32
bf16 = jnp.bfloat16


def mm(a, b, dims=NN):
    return lax.dot_general(a, b, dims, preferred_element_type=f32)


def split(x):
    high = x.astype(bf16)
    return high, (x - high.astype(f32)).astype(bf16)


def fields_kernel(cols, table_ref, part_ref, field_ref, sum_ref):
    sum_ref[...] = jnp.sum(part_ref[...].astype(f32), axis=0)
    patches, slots = table_ref.shape[1:]
    patch_cols = cols // PATCH
    patch_rows = patches // patch_cols
    spot = table_ref[2].astype(jnp.int32)
    row_in = spot // PATCH
    col_in = spot % PATCH
    iota_row = lax.broadcasted_iota(jnp.int32, (PATCH, slots), 0)
    iota_col = lax.broadcasted_iota(jnp.int32, (cols, slots), 0)
    for a in range(patch_rows):
        total = jnp.zeros((4 * PATCH, cols), f32)
        for b in range(patch_cols):
            p = a * patch_cols + b
            prec = table_ref[0, p : p + 1, :]
            level = table_ref[1, p : p + 1, :]
            prec_high = prec.astype(bf16).astype(f32)
            level_high = level.astype(bf16).astype(f32)
            on_row = row_in[p : p + 1, :] == iota_row
            pieces = [
                jnp.where(on_row, piece, 0.0).astype(bf16)
                for piece in (prec_high, prec - prec_high, level_high, level - level_high)
            ]
            on_col = jnp.where(col_in[p : p + 1, :] + b * PATCH == iota_col, 1.0, 0.0).astype(bf16)
            total = total + mm(jnp.concatenate(pieces, 0), on_col, NT)
        rows = slice(a * PATCH, (a + 1) * PATCH)
        field_ref[0, rows, :] = total[:PATCH] + total[PATCH : 2 * PATCH]
        field_ref[1, rows, :] = total[2 * PATCH : 3 * PATCH] + total[3 * PATCH :]


def state_kernel(after_ref, hist_ref, lag_ref, mean_ref, flat_ref):
    members, tile_rows, cols = hist_ref.shape
    state = hist_ref[...].astype(f32)
    mean = jnp.sum(state, axis=0) / members
    mean_ref[...] = mean
    flat_ref[...] = (state - mean[None]).reshape(members * tile_rows, cols)
    for r in range(tile_rows):
        lag_ref[r] = flat_ref[pl.ds(r, members, stride=tile_rows), :].astype(bf16)


def down_first():
    return 1 - lax.axis_index("lag") // (lax.axis_size("lag") // 2)


def ring(tiles, shares, turn):
    half = shares // 2
    pairs = []
    for t in range(tiles):
        for l in range(shares):
            target = t + (-1 if (l // half) ^ turn else 1)
            if 0 <= target < tiles:
                pairs.append((t * shares + l, target * shares + l))
            else:
                pairs.append((t * shares + l, t * shares + (l + half) % shares))
    return pairs


def taper_plan(centre_row, inverse_square):
    q_row = lax.broadcasted_iota(jnp.int32, inverse_square.shape, 0)
    col = lax.broadcasted_iota(jnp.int32, inverse_square.shape, 1)
    col_square = jnp.square(col.astype(f32) - (q_row.astype(f32) * PATCH + MIDDLE))
    return centre_row, col_square, inverse_square


def accumulate(total, plan, anomalies, weight, innovation, first_row):
    centre_row, col_square, inverse_square = plan
    patches, cols = col_square.shape
    lefts = []
    for i, anomaly in enumerate(anomalies):
        members = anomaly.shape[0]
        offset = (first_row + i).astype(f32) - centre_row
        taper = jnp.square(jnp.maximum(0.0, 1.0 - (offset * offset + col_square) * inverse_square))
        scale = taper * weight[i : i + 1]
        blocks = anomaly.reshape(members // PATCH, PATCH, cols)
        left = [
            (blocks * jnp.broadcast_to(scale[q : q + 1], (PATCH, cols)).astype(bf16)[None]).reshape(members, cols)
            for q in range(patches)
        ]
        tail = taper * innovation[i : i + 1]
        left.append(jnp.concatenate([tail, jnp.zeros((PATCH - patches, cols), f32)], 0).astype(bf16))
        lefts.append(jnp.concatenate(left, 0))
    return total + mm(jnp.concatenate(lefts, 1), jnp.concatenate(anomalies, 1), NT)


STEP = 8


def packed(totals, members, patch_cols):
    pairs = patch_cols // 2
    half = members // 2
    grams, sides = [], []
    for total in totals:
        for pair in range(pairs):
            at = 2 * pair * members
            grams.append(jnp.concatenate([total[at : at + members], total[at + members : at + 2 * members]], 1))
        for pair in range(pairs):
            at = patch_cols * members + 2 * pair
            sides.append(jnp.concatenate([total[at : at + 1], total[at + 1 : at + 2]], 1))
    lane = lax.broadcasted_iota(jnp.int32, (half, 2 * members), 1)
    tops = [gram[:half] for gram in grams]
    ends = [
        jnp.where(lane % members < half, pltpu.roll(a[half:], 2 * members - half, 1), b[half:])
        for a, b in zip(grams[::2], grams[1::2])
    ]
    return jnp.concatenate(tops + ends, 0), jnp.concatenate(sides, 0)


def unpacked(rows, members):
    half = members // 2
    wide = 2 * members
    count = rows.shape[0] * 2 // (3 * half)
    lane = lax.broadcasted_iota(jnp.int32, (half, wide), 1)
    tops = [rows[p * half : (p + 1) * half] for p in range(count)]
    ends = [rows[(count + k) * half : (count + k + 1) * half] for k in range(count // 2)]
    per_square = wide // half
    turned = [
        jnp.transpose(jnp.concatenate(tops[p : p + per_square], 0)) for p in range(0, count, per_square)
    ]
    grams = []
    for p in range(count):
        square, at = turned[p // per_square], (p % per_square) * half
        first = pltpu.roll(square[half:members], (wide - at) % wide, 1)
        second = pltpu.roll(square[members + half :], (members + wide - at) % wide, 1)
        corner = ends[p // 2] if p % 2 else pltpu.roll(ends[p // 2], half, 1)
        bottom = jnp.where(lane % members < half, jnp.where(lane < members, first, second), corner)
        grams.append(jnp.concatenate([tops[p], bottom], 0))
    return grams


def message_of(grams, sides):
    return jnp.concatenate([grams.astype(bf16), *split(sides)], 0)


def read_message(ref, side_count):
    at = ref.shape[0] - 2 * side_count
    high, low = ref[at : at + side_count, :].astype(f32), ref[at + side_count :, :].astype(f32)
    return jnp.concatenate([ref[:at, :].astype(f32), high + low], 0)


def arrived(ref, turn, side_count):
    tile = lax.axis_index("dom")
    there = jnp.where(down_first() ^ turn == 1, tile > 0, tile < lax.axis_size("dom") - 1)
    return jnp.where(there, read_message(ref, side_count), 0.0)


def outward(turn, rows_ref, held_ref, inverse_ref, message_ref, total_ref):
    tile_rows, members, cols = rows_ref.shape
    patch_cols = cols // PATCH
    down = down_first() ^ turn
    near = pl.multiple_of(down * (tile_rows - NEAR), 8)
    middle = jnp.where(down == 0, MIDDLE - PATCH, MIDDLE + tile_rows)
    plans = [
        taper_plan(middle, inverse_ref[1 - down]),
        taper_plan(middle + jnp.where(down == 0, -PATCH, PATCH).astype(f32), inverse_ref[down]),
    ]
    anomalies = [rows_ref[near + i] for i in range(NEAR)]
    fields = [held_ref[k, pl.ds(near, NEAR), :] for k in range(2)]
    blank = jnp.zeros(total_ref.shape[1:], f32)
    totals = [accumulate(blank, plan, anomalies, *fields, near) for plan in plans]
    for start in range(NEAR, FAR, STEP):
        anomalies = [rows_ref[start + i] for i in range(STEP)]
        fields = [held_ref[k, start : start + STEP, :] for k in range(2)]
        totals[0] = accumulate(totals[0], plans[0], anomalies, *fields, jnp.int32(start))
    total_ref[1 - down] = totals[0]
    total_ref[down] = totals[1]
    message_ref[...] = message_of(*packed([total_ref[0], total_ref[1]], members, patch_cols))


def first_kernel(shares, *refs):
    parts, refs = refs[:shares], refs[shares:]
    sum_ref, field_ref, inverse_ref, rows_ref, held_ref, message_ref, flat_ref, total_ref = refs
    share_members, tile_rows, cols = parts[0].shape
    members = share_members * shares
    lag = lax.axis_index("lag")
    states = [part[...].astype(f32) for part in parts]
    mean = functools.reduce(jnp.add, [jnp.sum(state, axis=0) for state in states[1:]], sum_ref[...]) / members
    for k, state in enumerate(states):
        at = pl.multiple_of(lax.rem(lag + k, shares) * (share_members * tile_rows), 8)
        flat_ref[pl.ds(at, share_members * tile_rows), :] = (state - mean[None]).reshape(-1, cols)
    weight = field_ref[0]
    held_ref[0] = weight
    held_ref[1] = field_ref[1] - mean * weight
    for r in range(tile_rows):
        rows_ref[r] = flat_ref[pl.ds(r, members, stride=tile_rows), :].astype(bf16)
    outward(0, rows_ref, held_ref, inverse_ref, message_ref, total_ref)


def second_kernel(rows_ref, held_ref, inverse_ref, message_ref, total_ref):
    outward(1, rows_ref, held_ref, inverse_ref, message_ref, total_ref)


def own_kernel(after_ref, rows_ref, held_ref, inverse_ref, first_ref, out_ref):
    tile_rows, members, cols = rows_ref.shape
    patch_cols = cols // PATCH
    plans = [taper_plan(MIDDLE + a * PATCH, inverse_ref[a]) for a in range(tile_rows // PATCH)]
    totals = [jnp.zeros((patch_cols * members + PATCH, members), f32) for _ in plans]
    for start in range(0, tile_rows, STEP):
        anomalies = [rows_ref[start + i] for i in range(STEP)]
        fields = [held_ref[k, start : start + STEP, :] for k in range(2)]
        totals = [accumulate(total, plan, anomalies, *fields, jnp.int32(start)) for total, plan in zip(totals, plans)]
    sums = jnp.concatenate(packed(totals, members, patch_cols), 0)
    out_ref[...] = sums + arrived(first_ref, 0, patch_cols)


def finish_kernel(total_ref, second_ref, lag_ref, mean_ref, out_ref, flat_ref):
    tile_rows, members, cols = lag_ref.shape
    degree = members - 1.0
    pair_count = (tile_rows // PATCH) * (cols // PATCH) // 2
    grams_end = total_ref.shape[0] - pair_count
    row = lax.broadcasted_iota(jnp.int32, (members, cols), 0)
    lane = lax.broadcasted_iota(jnp.int32, (members, cols), 1)
    identity = jnp.where(row == lane % members, 1.0, 0.0)
    left_mask = jnp.where(lane < members, 1.0, 0.0).astype(bf16)
    right_mask = jnp.where(lane < members, 0.0, 1.0).astype(bf16)

    def splits(parts):
        highs = [part.astype(bf16) for part in parts]
        rests = [part - high.astype(f32) for part, high in zip(parts, highs)]
        return list(zip(highs, [rest.astype(bf16) for rest in rests]))

    def rights(parts):
        return [
            jnp.concatenate(
                [jnp.concatenate([half * mask for half in halves], 1) for mask in (left_mask, right_mask)], 0
            )
            for halves in splits(parts)
        ]

    def products(lefts, factors):
        stacks = [jnp.concatenate([half for halves in left for half in halves], 0) for left in lefts]
        boths = [mm(stack, factor) for stack, factor in zip(stacks, factors)]
        results = []
        for left, both in zip(lefts, boths):
            parts, at = [], 0
            for high, low in left:
                rows = high.shape[0]
                upper, lower = both[at : at + rows], both[at + rows : at + 2 * rows]
                parts.append(upper[:, :cols] + (upper[:, cols:] + lower[:, :cols]))
                at += 2 * rows
            results.append(parts)
        return results

    total = total_ref[...] + arrived(second_ref, 1, pair_count)
    pairs = range(pair_count)
    grams = unpacked(total[:grams_end], members)
    squares = jnp.concatenate([jnp.sum(gram * gram, axis=0, keepdims=True) for gram in grams], 0)
    at_left = lax.broadcasted_iota(jnp.int32, squares.shape, 1) < members
    norm_left = jnp.sum(jnp.where(at_left, squares, 0.0), axis=1, keepdims=True)
    norm_right = jnp.sum(jnp.where(at_left, 0.0, squares), axis=1, keepdims=True)
    bounds = degree + jnp.sqrt(jnp.where(at_left, norm_left, norm_right))
    inverses = 1.0 / bounds
    spreads = jnp.sqrt(degree * inverses)
    sides = [jnp.broadcast_to(total[grams_end + p : grams_end + p + 1], (PATCH, cols)) for p in pairs]
    iterates = [(grams[p] + degree * identity) * inverses[p : p + 1] for p in pairs]
    roots = [None for _ in pairs]
    for step in range(NS_STEPS):
        lefts = [[halves] for halves in splits(sides)]
        if step == 0:
            ahead = iterates
        else:
            root_halves = splits(roots)
            lefts = [left + [halves] for left, halves in zip(lefts, root_halves)]
            ahead = [parts[0] for parts in products([[halves] for halves in root_halves], rights(iterates))]
        if step < NS_STEPS - 1:
            lefts = [left + [halves] for left, halves in zip(lefts, splits(iterates))]
        corrections = [1.5 * identity - 0.5 * product for product in ahead]
        results = products(lefts, rights(corrections))
        sides = [parts[0] for parts in results]
        roots = corrections if step == 0 else [parts[1] for parts in results]
        iterates = [parts[-1] for parts in results]
    weights = [parts[0][:1] for parts in products([[halves] for halves in splits(sides)], rights(roots))]
    weights = [weights[p] * inverses[p : p + 1] for p in pairs]
    mixings = [(spreads[p : p + 1] * roots[p] + weights[p]).astype(bf16) for p in pairs]

    patch = lax.broadcasted_iota(jnp.int32, (members, cols), 1) // PATCH
    masks = [jnp.where(patch % 4 == k, 1.0, 0.0).astype(bf16) for k in range(4)]
    quads = cols // (4 * PATCH)
    for a in range(tile_rows // PATCH):
        mixing = jnp.concatenate(
            [jnp.concatenate(mixings[2 * q : 2 * q + 2], 1) for q in range(a * quads, (a + 1) * quads)], 0
        )
        for r in range(a * PATCH, (a + 1) * PATCH, 2):
            state = jnp.concatenate(
                [jnp.concatenate([lag_ref[i] * mask for mask in masks], 0) for i in (r, r + 1)], 1
            )
            spread_out = mm(mixing, state)
            for i in (0, 1):
                part = spread_out[:, i * cols : (i + 1) * cols]
                chosen = part[:members]
                for q in range(1, quads):
                    chosen = jnp.where(patch // 4 == q, part[q * members : (q + 1) * members], chosen)
                flat_ref[pl.ds(r + i, members, stride=tile_rows), :] = chosen + mean_ref[r + i : r + i + 1, :]
    out_ref[...] = flat_ref[...].reshape(1, members, tile_rows, cols).astype(bf16)


def shards(history, forecast, spot, alive, levels, precision, radius):
    shares = lax.axis_size("lag")
    tiles = lax.axis_size("dom")
    share_members, tile_rows, cols = forecast.shape
    members = share_members * shares
    patch_cols = cols // PATCH
    def call(kernel, name, in_specs, out_shape, scratch=()):
        return pl.pallas_call(
            kernel,
            in_specs=in_specs,
            out_specs=jax.tree.map(lambda _: vmem, out_shape),
            out_shape=out_shape,
            scratch_shapes=scratch,
            compiler_params=pltpu.CompilerParams(vmem_limit_bytes=32 * 2**20),
            name=name,
        )

    shape = jax.ShapeDtypeStruct
    vmem = pl.BlockSpec(memory_space=pltpu.VMEM)
    parts = [forecast]
    for k in range(1, shares):
        parts.append(lax.ppermute(forecast, "lag", [((i + k) % shares, i) for i in range(shares)]))
    live = lax.broadcasted_iota(jnp.int32, spot.shape, 1) < alive[:, None]
    weights = jnp.where(live, precision, 0.0)
    kind = lax.broadcasted_iota(jnp.int32, (3, *spot.shape), 0)
    tables = jnp.where(kind == 0, weights[None], jnp.where(kind == 1, (weights * levels)[None], spot.astype(f32)[None]))
    inverse = jnp.broadcast_to(
        (1.0 / jnp.square(radius.astype(f32))).reshape(-1, patch_cols, 1), (tile_rows // PATCH, patch_cols, cols)
    )
    sent, tables = lax.optimization_barrier((inverse, tables))
    rings = [ring(tiles, shares, turn) for turn in range(2)]
    axes = ("dom", "lag")
    next_inverses = [lax.ppermute(sent, axes, [(t, s) for s, t in pairs]) for pairs in rings]
    fields, own_sum = call(
        functools.partial(fields_kernel, cols),
        "fields",
        [vmem, vmem],
        [shape((2, tile_rows, cols), f32), shape((tile_rows, cols), f32)],
    )(tables, forecast)
    packed_rows = patch_cols * members * 3 // 4
    message_shape = shape((packed_rows + 2 * patch_cols, 2 * members), bf16)
    total_scratch = pltpu.VMEM((2, patch_cols * members + PATCH, members), f32)
    rows, held, message = call(
        functools.partial(first_kernel, shares),
        "first_gram",
        [vmem] * (shares + 3),
        [shape((tile_rows, members, cols), bf16), shape((2, tile_rows, cols), f32), message_shape],
        [pltpu.VMEM((members * tile_rows, cols), f32), total_scratch],
    )(*parts, own_sum, fields, next_inverses[0])
    first = lax.ppermute(message, axes, rings[0])
    message = call(second_kernel, "second_gram", [vmem] * 3, message_shape, [total_scratch])(rows, held, next_inverses[1])
    second = lax.ppermute(message, axes, rings[1])
    lag_rows, lag_mean = call(
        state_kernel,
        "state",
        [vmem, vmem],
        [shape((tile_rows, members, cols), bf16), shape((tile_rows, cols), f32)],
        [pltpu.VMEM((members * tile_rows, cols), f32)],
    )(held, history[0])
    own_shape = shape((packed_rows + patch_cols, 2 * members), f32)
    own = call(own_kernel, "own_gram", [vmem] * 5, own_shape)(lag_mean, rows, held, inverse, first)
    return call(
        finish_kernel,
        "finish",
        [vmem] * 4,
        shape((1, members, tile_rows, cols), bf16),
        [pltpu.VMEM((members * tile_rows, cols), f32)],
    )(own, second, lag_rows, lag_mean)


def solution(mesh):
    in_specs = (
        P("lag", None, "dom", None),
        P("lag", "dom", None),
        P("dom", None),
        P("dom"),
        P("dom", None),
        P("dom", None),
        P("dom"),
    )
    out_specs = P("lag", None, "dom", None)
    return jax.shard_map(shards, mesh=mesh, in_specs=in_specs, out_specs=out_specs, check_vma=False)
```

```python
import functools

import jax
import jax.numpy as jnp
from jax import lax
from jax.experimental import pallas as pl
from jax.experimental.pallas import tpu as pltpu
from jax.sharding import PartitionSpec as P

PATCH = 16
NS_STEPS = 4
RADIUS = 32
FAR = RADIUS - PATCH // 2
NEAR = FAR - PATCH
MIDDLE = (PATCH - 1) / 2

NT = (((1,), (1,)), ((), ()))
NN = (((1,), (0,)), ((), ()))
f32 = jnp.float32
bf16 = jnp.bfloat16


def mm(a, b, dims=NN):
    return lax.dot_general(a, b, dims, preferred_element_type=f32)


def split(x):
    high = x.astype(bf16)
    return high, (x - high.astype(f32)).astype(bf16)


def fields_kernel(cols, table_ref, part_ref, field_ref, sum_ref):
    sum_ref[...] = jnp.sum(part_ref[...].astype(f32), axis=0)
    patches, slots = table_ref.shape[1:]
    patch_cols = cols // PATCH
    patch_rows = patches // patch_cols
    spot = table_ref[2].astype(jnp.int32)
    row_in = spot // PATCH
    col_in = spot % PATCH
    iota_row = lax.broadcasted_iota(jnp.int32, (PATCH, slots), 0)
    iota_col = lax.broadcasted_iota(jnp.int32, (cols, slots), 0)
    for a in range(patch_rows):
        total = jnp.zeros((4 * PATCH, cols), f32)
        for b in range(patch_cols):
            p = a * patch_cols + b
            prec = table_ref[0, p : p + 1, :]
            level = table_ref[1, p : p + 1, :]
            prec_high = prec.astype(bf16).astype(f32)
            level_high = level.astype(bf16).astype(f32)
            on_row = row_in[p : p + 1, :] == iota_row
            pieces = [
                jnp.where(on_row, piece, 0.0).astype(bf16)
                for piece in (prec_high, prec - prec_high, level_high, level - level_high)
            ]
            on_col = jnp.where(col_in[p : p + 1, :] + b * PATCH == iota_col, 1.0, 0.0).astype(bf16)
            total = total + mm(jnp.concatenate(pieces, 0), on_col, NT)
        rows = slice(a * PATCH, (a + 1) * PATCH)
        field_ref[0, rows, :] = total[:PATCH] + total[PATCH : 2 * PATCH]
        field_ref[1, rows, :] = total[2 * PATCH : 3 * PATCH] + total[3 * PATCH :]


def state_kernel(after_ref, hist_ref, lag_ref, mean_ref, flat_ref):
    members, tile_rows, cols = hist_ref.shape
    state = hist_ref[...].astype(f32)
    mean = jnp.sum(state, axis=0) / members
    mean_ref[...] = mean
    flat_ref[...] = (state - mean[None]).reshape(members * tile_rows, cols)
    for r in range(tile_rows):
        lag_ref[r] = flat_ref[pl.ds(r, members, stride=tile_rows), :].astype(bf16)


def down_first():
    return 1 - lax.axis_index("lag") // (lax.axis_size("lag") // 2)


def ring(tiles, shares, turn):
    half = shares // 2
    pairs = []
    for t in range(tiles):
        for l in range(shares):
            target = t + (-1 if (l // half) ^ turn else 1)
            if 0 <= target < tiles:
                pairs.append((t * shares + l, target * shares + l))
            else:
                pairs.append((t * shares + l, t * shares + (l + half) % shares))
    return pairs


def taper_plan(centre_row, inverse_square):
    q_row = lax.broadcasted_iota(jnp.int32, inverse_square.shape, 0)
    col = lax.broadcasted_iota(jnp.int32, inverse_square.shape, 1)
    col_square = jnp.square(col.astype(f32) - (q_row.astype(f32) * PATCH + MIDDLE))
    return centre_row, col_square, inverse_square


def accumulate(total, plan, anomalies, weight, innovation, first_row):
    centre_row, col_square, inverse_square = plan
    patches, cols = col_square.shape
    lefts = []
    for i, anomaly in enumerate(anomalies):
        members = anomaly.shape[0]
        offset = (first_row + i).astype(f32) - centre_row
        taper = jnp.square(jnp.maximum(0.0, 1.0 - (offset * offset + col_square) * inverse_square))
        scale = taper * weight[i : i + 1]
        blocks = anomaly.reshape(members // PATCH, PATCH, cols)
        left = [
            (blocks * jnp.broadcast_to(scale[q : q + 1], (PATCH, cols)).astype(bf16)[None]).reshape(members, cols)
            for q in range(patches)
        ]
        tail = taper * innovation[i : i + 1]
        left.append(jnp.concatenate([tail, jnp.zeros((PATCH - patches, cols), f32)], 0).astype(bf16))
        lefts.append(jnp.concatenate(left, 0))
    return total + mm(jnp.concatenate(lefts, 1), jnp.concatenate(anomalies, 1), NT)


STEP = 16
SMOOTH_STEP = 4


def packed(totals, members, patch_cols):
    pairs = patch_cols // 2
    half = members // 2
    grams, sides = [], []
    for total in totals:
        for pair in range(pairs):
            at = 2 * pair * members
            grams.append(jnp.concatenate([total[at : at + members], total[at + members : at + 2 * members]], 1))
        for pair in range(pairs):
            at = patch_cols * members + 2 * pair
            sides.append(jnp.concatenate([total[at : at + 1], total[at + 1 : at + 2]], 1))
    lane = lax.broadcasted_iota(jnp.int32, (half, 2 * members), 1)
    tops = [gram[:half] for gram in grams]
    ends = [
        jnp.where(lane % members < half, pltpu.roll(a[half:], 2 * members - half, 1), b[half:])
        for a, b in zip(grams[::2], grams[1::2])
    ]
    return jnp.concatenate(tops + ends, 0), jnp.concatenate(sides, 0)


def unpacked(rows, members):
    half = members // 2
    wide = 2 * members
    count = rows.shape[0] * 2 // (3 * half)
    lane = lax.broadcasted_iota(jnp.int32, (half, wide), 1)
    tops = [rows[p * half : (p + 1) * half] for p in range(count)]
    ends = [rows[(count + k) * half : (count + k + 1) * half] for k in range(count // 2)]
    per_square = wide // half
    turned = [
        jnp.transpose(jnp.concatenate(tops[p : p + per_square], 0)) for p in range(0, count, per_square)
    ]
    grams = []
    for p in range(count):
        square, at = turned[p // per_square], (p % per_square) * half
        first = pltpu.roll(square[half:members], (wide - at) % wide, 1)
        second = pltpu.roll(square[members + half :], (members + wide - at) % wide, 1)
        corner = ends[p // 2] if p % 2 else pltpu.roll(ends[p // 2], half, 1)
        bottom = jnp.where(lane % members < half, jnp.where(lane < members, first, second), corner)
        grams.append(jnp.concatenate([tops[p], bottom], 0))
    return grams


def message_of(grams, sides):
    return jnp.concatenate([grams.astype(bf16), *split(sides)], 0)


def read_message(ref, side_count):
    at = ref.shape[0] - 2 * side_count
    high, low = ref[at : at + side_count, :].astype(f32), ref[at + side_count :, :].astype(f32)
    return jnp.concatenate([ref[:at, :].astype(f32), high + low], 0)


def arrived(ref, turn, side_count):
    tile = lax.axis_index("dom")
    there = jnp.where(down_first() ^ turn == 1, tile > 0, tile < lax.axis_size("dom") - 1)
    return jnp.where(there, read_message(ref, side_count), 0.0)


def outward(turn, rows_ref, held_ref, inverse_ref, message_ref, total_ref):
    tile_rows, members, cols = rows_ref.shape
    patch_cols = cols // PATCH
    down = down_first() ^ turn
    near = pl.multiple_of(down * (tile_rows - NEAR), 8)
    middle = jnp.where(down == 0, MIDDLE - PATCH, MIDDLE + tile_rows)
    plans = [
        taper_plan(middle, inverse_ref[1 - down]),
        taper_plan(middle + jnp.where(down == 0, -PATCH, PATCH).astype(f32), inverse_ref[down]),
    ]
    anomalies = [rows_ref[near + i] for i in range(NEAR)]
    fields = [held_ref[k, pl.ds(near, NEAR), :] for k in range(2)]
    blank = jnp.zeros(total_ref.shape[1:], f32)
    totals = [accumulate(blank, plan, anomalies, *fields, near) for plan in plans]
    for start in range(NEAR, FAR, STEP):
        anomalies = [rows_ref[start + i] for i in range(STEP)]
        fields = [held_ref[k, start : start + STEP, :] for k in range(2)]
        totals[0] = accumulate(totals[0], plans[0], anomalies, *fields, jnp.int32(start))
    total_ref[1 - down] = totals[0]
    total_ref[down] = totals[1]
    message_ref[...] = message_of(*packed([total_ref[0], total_ref[1]], members, patch_cols))


def first_kernel(shares, *refs):
    parts, refs = refs[:shares], refs[shares:]
    sum_ref, field_ref, inverse_ref, rows_ref, held_ref, message_ref, flat_ref, total_ref = refs
    share_members, tile_rows, cols = parts[0].shape
    members = share_members * shares
    lag = lax.axis_index("lag")
    states = [part[...].astype(f32) for part in parts]
    mean = functools.reduce(jnp.add, [jnp.sum(state, axis=0) for state in states[1:]], sum_ref[...]) / members
    for k, state in enumerate(states):
        at = pl.multiple_of(lax.rem(lag + k, shares) * (share_members * tile_rows), 8)
        flat_ref[pl.ds(at, share_members * tile_rows), :] = (state - mean[None]).reshape(-1, cols)
    weight = field_ref[0]
    held_ref[0] = weight
    held_ref[1] = field_ref[1] - mean * weight
    for r in range(tile_rows):
        rows_ref[r] = flat_ref[pl.ds(r, members, stride=tile_rows), :].astype(bf16)
    outward(0, rows_ref, held_ref, inverse_ref, message_ref, total_ref)


def second_kernel(rows_ref, held_ref, inverse_ref, message_ref, total_ref):
    outward(1, rows_ref, held_ref, inverse_ref, message_ref, total_ref)


def own_kernel(after_ref, rows_ref, held_ref, inverse_ref, first_ref, out_ref):
    tile_rows, members, cols = rows_ref.shape
    patch_cols = cols // PATCH
    plans = [taper_plan(MIDDLE + a * PATCH, inverse_ref[a]) for a in range(tile_rows // PATCH)]
    totals = [jnp.zeros((patch_cols * members + PATCH, members), f32) for _ in plans]
    for start in range(0, tile_rows, STEP):
        anomalies = [rows_ref[start + i] for i in range(STEP)]
        fields = [held_ref[k, start : start + STEP, :] for k in range(2)]
        totals = [accumulate(total, plan, anomalies, *fields, jnp.int32(start)) for total, plan in zip(totals, plans)]
    sums = jnp.concatenate(packed(totals, members, patch_cols), 0)
    out_ref[...] = sums + arrived(first_ref, 0, patch_cols)


def finish_kernel(total_ref, second_ref, lag_ref, mean_ref, out_ref, flat_ref):
    tile_rows, members, cols = lag_ref.shape
    degree = members - 1.0
    pair_count = (tile_rows // PATCH) * (cols // PATCH) // 2
    grams_end = total_ref.shape[0] - pair_count
    row = lax.broadcasted_iota(jnp.int32, (members, cols), 0)
    lane = lax.broadcasted_iota(jnp.int32, (members, cols), 1)
    identity = jnp.where(row == lane % members, 1.0, 0.0)
    left_mask = jnp.where(lane < members, 1.0, 0.0).astype(bf16)
    right_mask = jnp.where(lane < members, 0.0, 1.0).astype(bf16)

    def splits(parts):
        highs = [part.astype(bf16) for part in parts]
        rests = [part - high.astype(f32) for part, high in zip(parts, highs)]
        return list(zip(highs, [rest.astype(bf16) for rest in rests]))

    def rights(parts):
        return [
            jnp.concatenate(
                [jnp.concatenate([half * mask for half in halves], 1) for mask in (left_mask, right_mask)], 0
            )
            for halves in splits(parts)
        ]

    def products(lefts, factors):
        stacks = [jnp.concatenate([half for halves in left for half in halves], 0) for left in lefts]
        boths = [mm(stack, factor) for stack, factor in zip(stacks, factors)]
        results = []
        for left, both in zip(lefts, boths):
            parts, at = [], 0
            for high, low in left:
                rows = high.shape[0]
                upper, lower = both[at : at + rows], both[at + rows : at + 2 * rows]
                parts.append(upper[:, :cols] + (upper[:, cols:] + lower[:, :cols]))
                at += 2 * rows
            results.append(parts)
        return results

    total = total_ref[...] + arrived(second_ref, 1, pair_count)
    pairs = range(pair_count)
    grams = unpacked(total[:grams_end], members)
    squares = jnp.concatenate([jnp.sum(gram * gram, axis=0, keepdims=True) for gram in grams], 0)
    at_left = lax.broadcasted_iota(jnp.int32, squares.shape, 1) < members
    norm_left = jnp.sum(jnp.where(at_left, squares, 0.0), axis=1, keepdims=True)
    norm_right = jnp.sum(jnp.where(at_left, 0.0, squares), axis=1, keepdims=True)
    bounds = degree + jnp.sqrt(jnp.where(at_left, norm_left, norm_right))
    inverses = 1.0 / bounds
    spreads = jnp.sqrt(degree * inverses)
    sides = [jnp.broadcast_to(total[grams_end + p : grams_end + p + 1], (PATCH, cols)) for p in pairs]
    iterates = [(grams[p] + degree * identity) * inverses[p : p + 1] for p in pairs]
    roots = [None for _ in pairs]
    for step in range(NS_STEPS):
        lefts = [[halves] for halves in splits(sides)]
        if step == 0:
            ahead = iterates
        else:
            root_halves = splits(roots)
            lefts = [left + [halves] for left, halves in zip(lefts, root_halves)]
            ahead = [parts[0] for parts in products([[halves] for halves in root_halves], rights(iterates))]
        if step < NS_STEPS - 1:
            lefts = [left + [halves] for left, halves in zip(lefts, splits(iterates))]
        corrections = [1.5 * identity - 0.5 * product for product in ahead]
        results = products(lefts, rights(corrections))
        sides = [parts[0] for parts in results]
        roots = corrections if step == 0 else [parts[1] for parts in results]
        iterates = [parts[-1] for parts in results]
    weights = [parts[0][:1] for parts in products([[halves] for halves in splits(sides)], rights(roots))]
    weights = [weights[p] * inverses[p : p + 1] for p in pairs]
    mixings = [(spreads[p : p + 1] * roots[p] + weights[p]).astype(bf16) for p in pairs]

    patch = lax.broadcasted_iota(jnp.int32, (members, cols), 1) // PATCH
    masks = [jnp.where(patch % 4 == k, 1.0, 0.0).astype(bf16) for k in range(4)]
    quads = cols // (4 * PATCH)
    for a in range(tile_rows // PATCH):
        mixing = jnp.concatenate(
            [jnp.concatenate(mixings[2 * q : 2 * q + 2], 1) for q in range(a * quads, (a + 1) * quads)], 0
        )
        for r in range(a * PATCH, (a + 1) * PATCH, SMOOTH_STEP):
            state = jnp.concatenate(
                [jnp.concatenate([lag_ref[i] * mask for mask in masks], 0) for i in range(r, r + SMOOTH_STEP)], 1
            )
            spread_out = mm(mixing, state)
            for i in range(SMOOTH_STEP):
                part = spread_out[:, i * cols : (i + 1) * cols]
                chosen = part[:members]
                for q in range(1, quads):
                    chosen = jnp.where(patch // 4 == q, part[q * members : (q + 1) * members], chosen)
                flat_ref[pl.ds(r + i, members, stride=tile_rows), :] = chosen + mean_ref[r + i : r + i + 1, :]
    out_ref[...] = flat_ref[...].reshape(1, members, tile_rows, cols).astype(bf16)


def shards(history, forecast, spot, alive, levels, precision, radius):
    shares = lax.axis_size("lag")
    tiles = lax.axis_size("dom")
    share_members, tile_rows, cols = forecast.shape
    members = share_members * shares
    patch_cols = cols // PATCH
    def call(kernel, name, in_specs, out_shape, scratch=()):
        return pl.pallas_call(
            kernel,
            in_specs=in_specs,
            out_specs=jax.tree.map(lambda _: vmem, out_shape),
            out_shape=out_shape,
            scratch_shapes=scratch,
            compiler_params=pltpu.CompilerParams(vmem_limit_bytes=32 * 2**20),
            name=name,
        )

    shape = jax.ShapeDtypeStruct
    vmem = pl.BlockSpec(memory_space=pltpu.VMEM)
    parts = [forecast]
    for k in range(1, shares):
        parts.append(lax.ppermute(forecast, "lag", [((i + k) % shares, i) for i in range(shares)]))
    live = lax.broadcasted_iota(jnp.int32, spot.shape, 1) < alive[:, None]
    weights = jnp.where(live, precision, 0.0)
    kind = lax.broadcasted_iota(jnp.int32, (3, *spot.shape), 0)
    tables = jnp.where(kind == 0, weights[None], jnp.where(kind == 1, (weights * levels)[None], spot.astype(f32)[None]))
    inverse = jnp.broadcast_to(
        (1.0 / jnp.square(radius.astype(f32))).reshape(-1, patch_cols, 1), (tile_rows // PATCH, patch_cols, cols)
    )
    sent, tables = lax.optimization_barrier((inverse, tables))
    rings = [ring(tiles, shares, turn) for turn in range(2)]
    axes = ("dom", "lag")
    next_inverses = [lax.ppermute(sent, axes, [(t, s) for s, t in pairs]) for pairs in rings]
    fields, own_sum = call(
        functools.partial(fields_kernel, cols),
        "fields",
        [vmem, vmem],
        [shape((2, tile_rows, cols), f32), shape((tile_rows, cols), f32)],
    )(tables, forecast)
    packed_rows = patch_cols * members * 3 // 4
    message_shape = shape((packed_rows + 2 * patch_cols, 2 * members), bf16)
    total_scratch = pltpu.VMEM((2, patch_cols * members + PATCH, members), f32)
    rows, held, message = call(
        functools.partial(first_kernel, shares),
        "first_gram",
        [vmem] * (shares + 3),
        [shape((tile_rows, members, cols), bf16), shape((2, tile_rows, cols), f32), message_shape],
        [pltpu.VMEM((members * tile_rows, cols), f32), total_scratch],
    )(*parts, own_sum, fields, next_inverses[0])
    first = lax.ppermute(message, axes, rings[0])
    message = call(second_kernel, "second_gram", [vmem] * 3, message_shape, [total_scratch])(rows, held, next_inverses[1])
    second = lax.ppermute(message, axes, rings[1])
    lag_rows, lag_mean = call(
        state_kernel,
        "state",
        [vmem, vmem],
        [shape((tile_rows, members, cols), bf16), shape((tile_rows, cols), f32)],
        [pltpu.VMEM((members * tile_rows, cols), f32)],
    )(held, history[0])
    own_shape = shape((packed_rows + patch_cols, 2 * members), f32)
    own = call(own_kernel, "own_gram", [vmem] * 5, own_shape)(lag_mean, rows, held, inverse, first)
    return call(
        finish_kernel,
        "finish",
        [vmem] * 4,
        shape((1, members, tile_rows, cols), bf16),
        [pltpu.VMEM((members * tile_rows, cols), f32)],
    )(own, second, lag_rows, lag_mean)


def solution(mesh):
    in_specs = (
        P("lag", None, "dom", None),
        P("lag", "dom", None),
        P("dom", None),
        P("dom"),
        P("dom", None),
        P("dom", None),
        P("dom"),
    )
    out_specs = P("lag", None, "dom", None)
    return jax.shard_map(shards, mesh=mesh, in_specs=in_specs, out_specs=out_specs, check_vma=False)
```

```python
import functools

import jax
import jax.numpy as jnp
from jax import lax
from jax.experimental import pallas as pl
from jax.experimental.pallas import tpu as pltpu
from jax.sharding import PartitionSpec as P

PATCH = 16
NS_STEPS = 4
RADIUS = 32
FAR = RADIUS - PATCH // 2
NEAR = FAR - PATCH
MIDDLE = (PATCH - 1) / 2

NT = (((1,), (1,)), ((), ()))
NN = (((1,), (0,)), ((), ()))
f32 = jnp.float32
bf16 = jnp.bfloat16


def mm(a, b, dims=NN):
    return lax.dot_general(a, b, dims, preferred_element_type=f32)


def split(x):
    high = x.astype(bf16)
    return high, (x - high.astype(f32)).astype(bf16)


def fields_kernel(cols, table_ref, part_ref, field_ref, sum_ref):
    sum_ref[...] = jnp.sum(part_ref[...].astype(f32), axis=0)
    patches, slots = table_ref.shape[1:]
    patch_cols = cols // PATCH
    patch_rows = patches // patch_cols
    spot = table_ref[2].astype(jnp.int32)
    row_in = spot // PATCH
    col_in = spot % PATCH
    iota_row = lax.broadcasted_iota(jnp.int32, (PATCH, slots), 0)
    iota_col = lax.broadcasted_iota(jnp.int32, (cols, slots), 0)
    for a in range(patch_rows):
        total = jnp.zeros((4 * PATCH, cols), f32)
        for b in range(patch_cols):
            p = a * patch_cols + b
            prec = table_ref[0, p : p + 1, :]
            level = table_ref[1, p : p + 1, :]
            prec_high = prec.astype(bf16).astype(f32)
            level_high = level.astype(bf16).astype(f32)
            on_row = row_in[p : p + 1, :] == iota_row
            pieces = [
                jnp.where(on_row, piece, 0.0).astype(bf16)
                for piece in (prec_high, prec - prec_high, level_high, level - level_high)
            ]
            on_col = jnp.where(col_in[p : p + 1, :] + b * PATCH == iota_col, 1.0, 0.0).astype(bf16)
            total = total + mm(jnp.concatenate(pieces, 0), on_col, NT)
        rows = slice(a * PATCH, (a + 1) * PATCH)
        field_ref[0, rows, :] = total[:PATCH] + total[PATCH : 2 * PATCH]
        field_ref[1, rows, :] = total[2 * PATCH : 3 * PATCH] + total[3 * PATCH :]


def state_kernel(hist_ref, lag_ref, mean_ref, flat_ref):
    members, tile_rows, cols = hist_ref.shape
    state = hist_ref[...].astype(f32)
    mean = jnp.sum(state, axis=0) / members
    mean_ref[...] = mean
    flat_ref[...] = (state - mean[None]).reshape(members * tile_rows, cols)
    for r in range(tile_rows):
        lag_ref[r] = flat_ref[pl.ds(r, members, stride=tile_rows), :].astype(bf16)


def down_first():
    return 1 - lax.axis_index("lag") // (lax.axis_size("lag") // 2)


def ring(tiles, shares, turn):
    half = shares // 2
    pairs = []
    for t in range(tiles):
        for l in range(shares):
            target = t + (-1 if (l // half) ^ turn else 1)
            if 0 <= target < tiles:
                pairs.append((t * shares + l, target * shares + l))
            else:
                pairs.append((t * shares + l, t * shares + (l + half) % shares))
    return pairs


def taper_plan(centre_row, inverse_square):
    q_row = lax.broadcasted_iota(jnp.int32, inverse_square.shape, 0)
    col = lax.broadcasted_iota(jnp.int32, inverse_square.shape, 1)
    col_square = jnp.square(col.astype(f32) - (q_row.astype(f32) * PATCH + MIDDLE))
    return centre_row, col_square, inverse_square


def accumulate(total, plan, anomalies, weight, innovation, first_row):
    centre_row, col_square, inverse_square = plan
    patches, cols = col_square.shape
    lefts = []
    for i, anomaly in enumerate(anomalies):
        members = anomaly.shape[0]
        offset = (first_row + i).astype(f32) - centre_row
        taper = jnp.square(jnp.maximum(0.0, 1.0 - (offset * offset + col_square) * inverse_square))
        scale = taper * weight[i : i + 1]
        blocks = anomaly.reshape(members // PATCH, PATCH, cols)
        left = [
            (blocks * jnp.broadcast_to(scale[q : q + 1], (PATCH, cols)).astype(bf16)[None]).reshape(members, cols)
            for q in range(patches)
        ]
        tail = taper * innovation[i : i + 1]
        left.append(jnp.concatenate([tail, jnp.zeros((PATCH - patches, cols), f32)], 0).astype(bf16))
        lefts.append(jnp.concatenate(left, 0))
    return total + mm(jnp.concatenate(lefts, 1), jnp.concatenate(anomalies, 1), NT)


STEP = 8


def packed(totals, members, patch_cols):
    pairs = patch_cols // 2
    half = members // 2
    grams, sides = [], []
    for total in totals:
        for pair in range(pairs):
            at = 2 * pair * members
            grams.append(jnp.concatenate([total[at : at + members], total[at + members : at + 2 * members]], 1))
        for pair in range(pairs):
            at = patch_cols * members + 2 * pair
            sides.append(jnp.concatenate([total[at : at + 1], total[at + 1 : at + 2]], 1))
    lane = lax.broadcasted_iota(jnp.int32, (half, 2 * members), 1)
    tops = [gram[:half] for gram in grams]
    ends = [
        jnp.where(lane % members < half, pltpu.roll(a[half:], 2 * members - half, 1), b[half:])
        for a, b in zip(grams[::2], grams[1::2])
    ]
    return jnp.concatenate(tops + ends, 0), jnp.concatenate(sides, 0)


def unpacked(rows, members):
    half = members // 2
    wide = 2 * members
    count = rows.shape[0] * 2 // (3 * half)
    lane = lax.broadcasted_iota(jnp.int32, (half, wide), 1)
    tops = [rows[p * half : (p + 1) * half] for p in range(count)]
    ends = [rows[(count + k) * half : (count + k + 1) * half] for k in range(count // 2)]
    per_square = wide // half
    turned = [
        jnp.transpose(jnp.concatenate(tops[p : p + per_square], 0)) for p in range(0, count, per_square)
    ]
    grams = []
    for p in range(count):
        square, at = turned[p // per_square], (p % per_square) * half
        first = pltpu.roll(square[half:members], (wide - at) % wide, 1)
        second = pltpu.roll(square[members + half :], (members + wide - at) % wide, 1)
        corner = ends[p // 2] if p % 2 else pltpu.roll(ends[p // 2], half, 1)
        bottom = jnp.where(lane % members < half, jnp.where(lane < members, first, second), corner)
        grams.append(jnp.concatenate([tops[p], bottom], 0))
    return grams


def message_of(grams, sides):
    return jnp.concatenate([grams.astype(bf16), *split(sides)], 0)


def read_message(ref, side_count):
    at = ref.shape[0] - 2 * side_count
    high, low = ref[at : at + side_count, :].astype(f32), ref[at + side_count :, :].astype(f32)
    return jnp.concatenate([ref[:at, :].astype(f32), high + low], 0)


def arrived(ref, turn, side_count):
    tile = lax.axis_index("dom")
    there = jnp.where(down_first() ^ turn == 1, tile > 0, tile < lax.axis_size("dom") - 1)
    return jnp.where(there, read_message(ref, side_count), 0.0)


def outward(turn, rows_ref, held_ref, inverse_ref, message_ref, total_ref):
    tile_rows, members, cols = rows_ref.shape
    patch_cols = cols // PATCH
    down = down_first() ^ turn
    near = pl.multiple_of(down * (tile_rows - NEAR), 8)
    middle = jnp.where(down == 0, MIDDLE - PATCH, MIDDLE + tile_rows)
    plans = [
        taper_plan(middle, inverse_ref[1 - down]),
        taper_plan(middle + jnp.where(down == 0, -PATCH, PATCH).astype(f32), inverse_ref[down]),
    ]
    anomalies = [rows_ref[near + i] for i in range(NEAR)]
    fields = [held_ref[k, pl.ds(near, NEAR), :] for k in range(2)]
    blank = jnp.zeros(total_ref.shape[1:], f32)
    totals = [accumulate(blank, plan, anomalies, *fields, near) for plan in plans]
    for start in range(NEAR, FAR, STEP):
        anomalies = [rows_ref[start + i] for i in range(STEP)]
        fields = [held_ref[k, start : start + STEP, :] for k in range(2)]
        totals[0] = accumulate(totals[0], plans[0], anomalies, *fields, jnp.int32(start))
    total_ref[1 - down] = totals[0]
    total_ref[down] = totals[1]
    message_ref[...] = message_of(*packed([total_ref[0], total_ref[1]], members, patch_cols))


def first_kernel(shares, *refs):
    parts, refs = refs[:shares], refs[shares:]
    sum_ref, field_ref, inverse_ref, _, rows_ref, held_ref, message_ref, flat_ref, total_ref = refs
    share_members, tile_rows, cols = parts[0].shape
    members = share_members * shares
    lag = lax.axis_index("lag")
    states = [part[...].astype(f32) for part in parts]
    mean = functools.reduce(jnp.add, [jnp.sum(state, axis=0) for state in states[1:]], sum_ref[...]) / members
    for k, state in enumerate(states):
        at = pl.multiple_of(lax.rem(lag + k, shares) * (share_members * tile_rows), 8)
        flat_ref[pl.ds(at, share_members * tile_rows), :] = (state - mean[None]).reshape(-1, cols)
    weight = field_ref[0]
    held_ref[0] = weight
    held_ref[1] = field_ref[1] - mean * weight
    for r in range(tile_rows):
        rows_ref[r] = flat_ref[pl.ds(r, members, stride=tile_rows), :].astype(bf16)
    outward(0, rows_ref, held_ref, inverse_ref, message_ref, total_ref)


def second_kernel(rows_ref, held_ref, inverse_ref, message_ref, total_ref):
    outward(1, rows_ref, held_ref, inverse_ref, message_ref, total_ref)


def own_sums(rows, rows_ref, held_ref, inverse_ref):
    members, cols = rows_ref.shape[1:]
    patch_rows, patch_cols = inverse_ref.shape[:2]
    plans = [taper_plan(MIDDLE + a * PATCH, inverse_ref[a]) for a in range(patch_rows)]
    totals = [jnp.zeros((patch_cols * members + PATCH, members), f32) for _ in plans]
    for start in range(rows.start, rows.stop, STEP):
        anomalies = [rows_ref[start + i] for i in range(STEP)]
        fields = [held_ref[k, start : start + STEP, :] for k in range(2)]
        totals = [accumulate(total, plan, anomalies, *fields, jnp.int32(start)) for total, plan in zip(totals, plans)]
    return jnp.concatenate(packed(totals, members, patch_cols), 0)


def upper_kernel(rows_ref, held_ref, inverse_ref, out_ref):
    out_ref[...] = own_sums(slice(0, rows_ref.shape[0] // 2), rows_ref, held_ref, inverse_ref)


def lower_kernel(upper_ref, rows_ref, held_ref, inverse_ref, first_ref, out_ref):
    tile_rows = rows_ref.shape[0]
    sums = own_sums(slice(tile_rows // 2, tile_rows), rows_ref, held_ref, inverse_ref)
    out_ref[...] = upper_ref[...] + sums + arrived(first_ref, 0, inverse_ref.shape[1])


def finish_kernel(total_ref, second_ref, lag_ref, mean_ref, out_ref, flat_ref):
    tile_rows, members, cols = lag_ref.shape
    degree = members - 1.0
    pair_count = (tile_rows // PATCH) * (cols // PATCH) // 2
    grams_end = total_ref.shape[0] - pair_count
    row = lax.broadcasted_iota(jnp.int32, (members, cols), 0)
    lane = lax.broadcasted_iota(jnp.int32, (members, cols), 1)
    identity = jnp.where(row == lane % members, 1.0, 0.0)
    left_mask = jnp.where(lane < members, 1.0, 0.0).astype(bf16)
    right_mask = jnp.where(lane < members, 0.0, 1.0).astype(bf16)

    def splits(parts):
        highs = [part.astype(bf16) for part in parts]
        rests = [part - high.astype(f32) for part, high in zip(parts, highs)]
        return list(zip(highs, [rest.astype(bf16) for rest in rests]))

    def rights(parts):
        return [
            jnp.concatenate(
                [jnp.concatenate([half * mask for half in halves], 1) for mask in (left_mask, right_mask)], 0
            )
            for halves in splits(parts)
        ]

    def products(lefts, factors):
        stacks = [jnp.concatenate([half for halves in left for half in halves], 0) for left in lefts]
        boths = [mm(stack, factor) for stack, factor in zip(stacks, factors)]
        results = []
        for left, both in zip(lefts, boths):
            parts, at = [], 0
            for high, low in left:
                rows = high.shape[0]
                upper, lower = both[at : at + rows], both[at + rows : at + 2 * rows]
                parts.append(upper[:, :cols] + (upper[:, cols:] + lower[:, :cols]))
                at += 2 * rows
            results.append(parts)
        return results

    total = total_ref[...] + arrived(second_ref, 1, pair_count)
    pairs = range(pair_count)
    grams = unpacked(total[:grams_end], members)
    squares = jnp.concatenate([jnp.sum(gram * gram, axis=0, keepdims=True) for gram in grams], 0)
    at_left = lax.broadcasted_iota(jnp.int32, squares.shape, 1) < members
    norm_left = jnp.sum(jnp.where(at_left, squares, 0.0), axis=1, keepdims=True)
    norm_right = jnp.sum(jnp.where(at_left, 0.0, squares), axis=1, keepdims=True)
    bounds = degree + jnp.sqrt(jnp.where(at_left, norm_left, norm_right))
    inverses = 1.0 / bounds
    spreads = jnp.sqrt(degree * inverses)
    sides = [jnp.broadcast_to(total[grams_end + p : grams_end + p + 1], (PATCH, cols)) for p in pairs]
    iterates = [(grams[p] + degree * identity) * inverses[p : p + 1] for p in pairs]
    roots = [None for _ in pairs]
    for step in range(NS_STEPS):
        lefts = [[halves] for halves in splits(sides)]
        if step == 0:
            ahead = iterates
        else:
            root_halves = splits(roots)
            lefts = [left + [halves] for left, halves in zip(lefts, root_halves)]
            ahead = [parts[0] for parts in products([[halves] for halves in root_halves], rights(iterates))]
        if step < NS_STEPS - 1:
            lefts = [left + [halves] for left, halves in zip(lefts, splits(iterates))]
        corrections = [1.5 * identity - 0.5 * product for product in ahead]
        results = products(lefts, rights(corrections))
        sides = [parts[0] for parts in results]
        roots = corrections if step == 0 else [parts[1] for parts in results]
        iterates = [parts[-1] for parts in results]
    weights = [parts[0][:1] for parts in products([[halves] for halves in splits(sides)], rights(roots))]
    weights = [weights[p] * inverses[p : p + 1] for p in pairs]
    mixings = [(spreads[p : p + 1] * roots[p] + weights[p]).astype(bf16) for p in pairs]

    patch = lax.broadcasted_iota(jnp.int32, (members, cols), 1) // PATCH
    masks = [jnp.where(patch % 4 == k, 1.0, 0.0).astype(bf16) for k in range(4)]
    quads = cols // (4 * PATCH)
    for a in range(tile_rows // PATCH):
        mixing = jnp.concatenate(
            [jnp.concatenate(mixings[2 * q : 2 * q + 2], 1) for q in range(a * quads, (a + 1) * quads)], 0
        )
        for r in range(a * PATCH, (a + 1) * PATCH, 2):
            state = jnp.concatenate(
                [jnp.concatenate([lag_ref[i] * mask for mask in masks], 0) for i in (r, r + 1)], 1
            )
            spread_out = mm(mixing, state)
            for i in (0, 1):
                part = spread_out[:, i * cols : (i + 1) * cols]
                chosen = part[:members]
                for q in range(1, quads):
                    chosen = jnp.where(patch // 4 == q, part[q * members : (q + 1) * members], chosen)
                flat_ref[pl.ds(r + i, members, stride=tile_rows), :] = chosen + mean_ref[r + i : r + i + 1, :]
    out_ref[...] = flat_ref[...].reshape(1, members, tile_rows, cols).astype(bf16)


def shards(history, forecast, spot, alive, levels, precision, radius):
    shares = lax.axis_size("lag")
    tiles = lax.axis_size("dom")
    share_members, tile_rows, cols = forecast.shape
    members = share_members * shares
    patch_cols = cols // PATCH
    def call(kernel, name, in_specs, out_shape, scratch=()):
        return pl.pallas_call(
            kernel,
            in_specs=in_specs,
            out_specs=jax.tree.map(lambda _: vmem, out_shape),
            out_shape=out_shape,
            scratch_shapes=scratch,
            compiler_params=pltpu.CompilerParams(vmem_limit_bytes=32 * 2**20),
            name=name,
        )

    shape = jax.ShapeDtypeStruct
    vmem = pl.BlockSpec(memory_space=pltpu.VMEM)
    parts = [forecast]
    for k in range(1, shares):
        parts.append(lax.ppermute(forecast, "lag", [((i + k) % shares, i) for i in range(shares)]))
    live = lax.broadcasted_iota(jnp.int32, spot.shape, 1) < alive[:, None]
    weights = jnp.where(live, precision, 0.0)
    kind = lax.broadcasted_iota(jnp.int32, (3, *spot.shape), 0)
    tables = jnp.where(kind == 0, weights[None], jnp.where(kind == 1, (weights * levels)[None], spot.astype(f32)[None]))
    inverse = jnp.broadcast_to(
        (1.0 / jnp.square(radius.astype(f32))).reshape(-1, patch_cols, 1), (tile_rows // PATCH, patch_cols, cols)
    )
    sent, tables = lax.optimization_barrier((inverse, tables))
    rings = [ring(tiles, shares, turn) for turn in range(2)]
    axes = ("dom", "lag")
    next_inverses = [lax.ppermute(sent, axes, [(t, s) for s, t in pairs]) for pairs in rings]
    fields, own_sum = call(
        functools.partial(fields_kernel, cols),
        "fields",
        [vmem, vmem],
        [shape((2, tile_rows, cols), f32), shape((tile_rows, cols), f32)],
    )(tables, forecast)
    packed_rows = patch_cols * members * 3 // 4
    message_shape = shape((packed_rows + 2 * patch_cols, 2 * members), bf16)
    total_scratch = pltpu.VMEM((2, patch_cols * members + PATCH, members), f32)
    lag_rows, lag_mean = call(
        state_kernel,
        "state",
        [vmem],
        [shape((tile_rows, members, cols), bf16), shape((tile_rows, cols), f32)],
        [pltpu.VMEM((members * tile_rows, cols), f32)],
    )(history[0])
    rows, held, message = call(
        functools.partial(first_kernel, shares),
        "first_gram",
        [vmem] * (shares + 4),
        [shape((tile_rows, members, cols), bf16), shape((2, tile_rows, cols), f32), message_shape],
        [pltpu.VMEM((members * tile_rows, cols), f32), total_scratch],
    )(*parts, own_sum, fields, next_inverses[0], lag_mean)
    first = lax.ppermute(message, axes, rings[0])
    message = call(second_kernel, "second_gram", [vmem] * 3, message_shape, [total_scratch])(rows, held, next_inverses[1])
    second = lax.ppermute(message, axes, rings[1])
    own_shape = shape((packed_rows + patch_cols, 2 * members), f32)
    upper = call(upper_kernel, "upper_gram", [vmem] * 3, own_shape)(rows, held, inverse)
    own = call(lower_kernel, "lower_gram", [vmem] * 5, own_shape)(upper, rows, held, inverse, first)
    return call(
        finish_kernel,
        "finish",
        [vmem] * 4,
        shape((1, members, tile_rows, cols), bf16),
        [pltpu.VMEM((members * tile_rows, cols), f32)],
    )(own, second, lag_rows, lag_mean)


def solution(mesh):
    in_specs = (
        P("lag", None, "dom", None),
        P("lag", "dom", None),
        P("dom", None),
        P("dom"),
        P("dom", None),
        P("dom", None),
        P("dom"),
    )
    out_specs = P("lag", None, "dom", None)
    return jax.shard_map(shards, mesh=mesh, in_specs=in_specs, out_specs=out_specs, check_vma=False)
```

```python
import functools

import jax
import jax.numpy as jnp
from jax import lax
from jax.experimental import pallas as pl
from jax.experimental.pallas import tpu as pltpu
from jax.sharding import PartitionSpec as P

PATCH = 16
NS_STEPS = 4
RADIUS = 32
FAR = RADIUS - PATCH // 2
NEAR = FAR - PATCH
MIDDLE = (PATCH - 1) / 2

NT = (((1,), (1,)), ((), ()))
NN = (((1,), (0,)), ((), ()))
f32 = jnp.float32
bf16 = jnp.bfloat16


def mm(a, b, dims=NN):
    return lax.dot_general(a, b, dims, preferred_element_type=f32)


def split(x):
    high = x.astype(bf16)
    return high, (x - high.astype(f32)).astype(bf16)


def fields_kernel(cols, table_ref, part_ref, field_ref, sum_ref):
    sum_ref[...] = jnp.sum(part_ref[...].astype(f32), axis=0)
    patches, slots = table_ref.shape[1:]
    patch_cols = cols // PATCH
    patch_rows = patches // patch_cols
    spot = table_ref[2].astype(jnp.int32)
    row_in = spot // PATCH
    col_in = spot % PATCH
    iota_row = lax.broadcasted_iota(jnp.int32, (PATCH, slots), 0)
    iota_col = lax.broadcasted_iota(jnp.int32, (cols, slots), 0)
    for a in range(patch_rows):
        total = jnp.zeros((4 * PATCH, cols), f32)
        for b in range(patch_cols):
            p = a * patch_cols + b
            prec = table_ref[0, p : p + 1, :]
            level = table_ref[1, p : p + 1, :]
            prec_high = prec.astype(bf16).astype(f32)
            level_high = level.astype(bf16).astype(f32)
            on_row = row_in[p : p + 1, :] == iota_row
            pieces = [
                jnp.where(on_row, piece, 0.0).astype(bf16)
                for piece in (prec_high, prec - prec_high, level_high, level - level_high)
            ]
            on_col = jnp.where(col_in[p : p + 1, :] + b * PATCH == iota_col, 1.0, 0.0).astype(bf16)
            total = total + mm(jnp.concatenate(pieces, 0), on_col, NT)
        rows = slice(a * PATCH, (a + 1) * PATCH)
        field_ref[0, rows, :] = total[:PATCH] + total[PATCH : 2 * PATCH]
        field_ref[1, rows, :] = total[2 * PATCH : 3 * PATCH] + total[3 * PATCH :]


def state_kernel(hist_ref, lag_ref, mean_ref, flat_ref):
    members, tile_rows, cols = hist_ref.shape
    state = hist_ref[...].astype(f32)
    mean = jnp.sum(state, axis=0) / members
    mean_ref[...] = mean
    flat_ref[: members * tile_rows, :] = (state - mean[None]).reshape(members * tile_rows, cols)
    for r in range(tile_rows):
        lag_ref[r] = flat_ref[pl.ds(r, members, stride=tile_rows), :].astype(bf16)


def down_first():
    return 1 - lax.axis_index("lag") // (lax.axis_size("lag") // 2)


def ring(tiles, shares, turn):
    half = shares // 2
    pairs = []
    for t in range(tiles):
        for l in range(shares):
            target = t + (-1 if (l // half) ^ turn else 1)
            if 0 <= target < tiles:
                pairs.append((t * shares + l, target * shares + l))
            else:
                pairs.append((t * shares + l, t * shares + (l + half) % shares))
    return pairs


def taper_plan(centre_row, inverse_square):
    q_row = lax.broadcasted_iota(jnp.int32, inverse_square.shape, 0)
    col = lax.broadcasted_iota(jnp.int32, inverse_square.shape, 1)
    col_square = jnp.square(col.astype(f32) - (q_row.astype(f32) * PATCH + MIDDLE))
    return centre_row, col_square, inverse_square


def accumulate(total, plan, anomalies, weight, innovation, first_row):
    centre_row, col_square, inverse_square = plan
    patches, cols = col_square.shape
    lefts = []
    for i, anomaly in enumerate(anomalies):
        members = anomaly.shape[0]
        offset = (first_row + i).astype(f32) - centre_row
        taper = jnp.square(jnp.maximum(0.0, 1.0 - (offset * offset + col_square) * inverse_square))
        scale = taper * weight[i : i + 1]
        blocks = anomaly.reshape(members // PATCH, PATCH, cols)
        left = [
            (blocks * jnp.broadcast_to(scale[q : q + 1], (PATCH, cols)).astype(bf16)[None]).reshape(members, cols)
            for q in range(patches)
        ]
        tail = taper * innovation[i : i + 1]
        left.append(jnp.concatenate([tail, jnp.zeros((PATCH - patches, cols), f32)], 0).astype(bf16))
        lefts.append(jnp.concatenate(left, 0))
    return total + mm(jnp.concatenate(lefts, 1), jnp.concatenate(anomalies, 1), NT)


STEP = 8


def packed(totals, members, patch_cols):
    pairs = patch_cols // 2
    half = members // 2
    grams, sides = [], []
    for total in totals:
        for pair in range(pairs):
            at = 2 * pair * members
            grams.append(jnp.concatenate([total[at : at + members], total[at + members : at + 2 * members]], 1))
        for pair in range(pairs):
            at = patch_cols * members + 2 * pair
            sides.append(jnp.concatenate([total[at : at + 1], total[at + 1 : at + 2]], 1))
    lane = lax.broadcasted_iota(jnp.int32, (half, 2 * members), 1)
    tops = [gram[:half] for gram in grams]
    ends = [
        jnp.where(lane % members < half, pltpu.roll(a[half:], 2 * members - half, 1), b[half:])
        for a, b in zip(grams[::2], grams[1::2])
    ]
    return jnp.concatenate(tops + ends, 0), jnp.concatenate(sides, 0)


def unpacked(rows, members):
    half = members // 2
    wide = 2 * members
    count = rows.shape[0] * 2 // (3 * half)
    lane = lax.broadcasted_iota(jnp.int32, (half, wide), 1)
    tops = [rows[p * half : (p + 1) * half] for p in range(count)]
    ends = [rows[(count + k) * half : (count + k + 1) * half] for k in range(count // 2)]
    per_square = wide // half
    turned = [
        jnp.transpose(jnp.concatenate(tops[p : p + per_square], 0)) for p in range(0, count, per_square)
    ]
    grams = []
    for p in range(count):
        square, at = turned[p // per_square], (p % per_square) * half
        first = pltpu.roll(square[half:members], (wide - at) % wide, 1)
        second = pltpu.roll(square[members + half :], (members + wide - at) % wide, 1)
        corner = ends[p // 2] if p % 2 else pltpu.roll(ends[p // 2], half, 1)
        bottom = jnp.where(lane % members < half, jnp.where(lane < members, first, second), corner)
        grams.append(jnp.concatenate([tops[p], bottom], 0))
    return grams


def message_of(grams, sides):
    return jnp.concatenate([grams.astype(bf16), *split(sides)], 0)


def read_message(ref, side_count):
    at = ref.shape[0] - 2 * side_count
    high, low = ref[at : at + side_count, :].astype(f32), ref[at + side_count :, :].astype(f32)
    return jnp.concatenate([ref[:at, :].astype(f32), high + low], 0)


def arrived(ref, turn, side_count):
    tile = lax.axis_index("dom")
    there = jnp.where(down_first() ^ turn == 1, tile > 0, tile < lax.axis_size("dom") - 1)
    return jnp.where(there, read_message(ref, side_count), 0.0)


def outward(turn, rows_ref, held_ref, inverse_ref, message_ref, total_ref):
    tile_rows, members, cols = rows_ref.shape
    patch_cols = cols // PATCH
    down = down_first() ^ turn
    near = pl.multiple_of(down * (tile_rows - NEAR), 8)
    middle = jnp.where(down == 0, MIDDLE - PATCH, MIDDLE + tile_rows)
    plans = [
        taper_plan(middle, inverse_ref[1 - down]),
        taper_plan(middle + jnp.where(down == 0, -PATCH, PATCH).astype(f32), inverse_ref[down]),
    ]
    anomalies = [rows_ref[near + i] for i in range(NEAR)]
    fields = [held_ref[k, pl.ds(near, NEAR), :] for k in range(2)]
    blank = jnp.zeros(total_ref.shape[1:], f32)
    totals = [accumulate(blank, plan, anomalies, *fields, near) for plan in plans]
    for start in range(NEAR, FAR, STEP):
        anomalies = [rows_ref[start + i] for i in range(STEP)]
        fields = [held_ref[k, start : start + STEP, :] for k in range(2)]
        totals[0] = accumulate(totals[0], plans[0], anomalies, *fields, jnp.int32(start))
    total_ref[1 - down] = totals[0]
    total_ref[down] = totals[1]
    message_ref[...] = message_of(*packed([total_ref[0], total_ref[1]], members, patch_cols))


def first_kernel(shares, *refs):
    parts, refs = refs[:shares], refs[shares:]
    sum_ref, field_ref, inverse_ref, _, rows_ref, held_ref, message_ref, flat_ref, total_ref = refs
    share_members, tile_rows, cols = parts[0].shape
    members = share_members * shares
    lag = lax.axis_index("lag")
    states = [part[...].astype(f32) for part in parts]
    mean = functools.reduce(jnp.add, [jnp.sum(state, axis=0) for state in states[1:]], sum_ref[...]) / members
    for k, state in enumerate(states):
        at = pl.multiple_of(lax.rem(lag + k, shares) * (share_members * tile_rows), 8)
        flat_ref[pl.ds(at, share_members * tile_rows), :] = (state - mean[None]).reshape(-1, cols)
    weight = field_ref[0]
    held_ref[0] = weight
    held_ref[1] = field_ref[1] - mean * weight
    for r in range(tile_rows):
        rows_ref[r] = flat_ref[pl.ds(r, members, stride=tile_rows), :].astype(bf16)
    outward(0, rows_ref, held_ref, inverse_ref, message_ref, total_ref)


def second_kernel(rows_ref, held_ref, inverse_ref, message_ref, total_ref):
    outward(1, rows_ref, held_ref, inverse_ref, message_ref, total_ref)


def own_sums(rows, rows_ref, held_ref, inverse_ref):
    members, cols = rows_ref.shape[1:]
    patch_rows, patch_cols = inverse_ref.shape[:2]
    plans = [taper_plan(MIDDLE + a * PATCH, inverse_ref[a]) for a in range(patch_rows)]
    totals = [jnp.zeros((patch_cols * members + PATCH, members), f32) for _ in plans]
    for start in range(rows.start, rows.stop, STEP):
        anomalies = [rows_ref[start + i] for i in range(STEP)]
        fields = [held_ref[k, start : start + STEP, :] for k in range(2)]
        totals = [accumulate(total, plan, anomalies, *fields, jnp.int32(start)) for total, plan in zip(totals, plans)]
    return jnp.concatenate(packed(totals, members, patch_cols), 0)


def upper_kernel(rows_ref, held_ref, inverse_ref, out_ref):
    out_ref[...] = own_sums(slice(0, rows_ref.shape[0] // 2), rows_ref, held_ref, inverse_ref)


def lower_kernel(upper_ref, rows_ref, held_ref, inverse_ref, first_ref, out_ref):
    tile_rows = rows_ref.shape[0]
    sums = own_sums(slice(tile_rows // 2, tile_rows), rows_ref, held_ref, inverse_ref)
    out_ref[...] = upper_ref[...] + sums + arrived(first_ref, 0, inverse_ref.shape[1])


def finish_kernel(total_ref, second_ref, lag_ref, mean_ref, out_ref, flat_ref):
    tile_rows, members, cols = lag_ref.shape
    degree = members - 1.0
    pair_count = (tile_rows // PATCH) * (cols // PATCH) // 2
    grams_end = total_ref.shape[0] - pair_count
    row = lax.broadcasted_iota(jnp.int32, (members, cols), 0)
    lane = lax.broadcasted_iota(jnp.int32, (members, cols), 1)
    identity = jnp.where(row == lane % members, 1.0, 0.0)
    left_mask = jnp.where(lane < members, 1.0, 0.0).astype(bf16)
    right_mask = jnp.where(lane < members, 0.0, 1.0).astype(bf16)

    def splits(parts):
        highs = [part.astype(bf16) for part in parts]
        rests = [part - high.astype(f32) for part, high in zip(parts, highs)]
        return list(zip(highs, [rest.astype(bf16) for rest in rests]))

    def rights(parts):
        return [
            jnp.concatenate(
                [jnp.concatenate([half * mask for half in halves], 1) for mask in (left_mask, right_mask)], 0
            )
            for halves in splits(parts)
        ]

    def products(lefts, factors):
        stacks = [jnp.concatenate([half for halves in left for half in halves], 0) for left in lefts]
        boths = [mm(stack, factor) for stack, factor in zip(stacks, factors)]
        results = []
        for left, both in zip(lefts, boths):
            parts, at = [], 0
            for high, low in left:
                rows = high.shape[0]
                upper, lower = both[at : at + rows], both[at + rows : at + 2 * rows]
                parts.append(upper[:, :cols] + (upper[:, cols:] + lower[:, :cols]))
                at += 2 * rows
            results.append(parts)
        return results

    total = total_ref[...] + arrived(second_ref, 1, pair_count)
    pairs = range(pair_count)
    grams = unpacked(total[:grams_end], members)
    squares = jnp.concatenate([jnp.sum(gram * gram, axis=0, keepdims=True) for gram in grams], 0)
    at_left = lax.broadcasted_iota(jnp.int32, squares.shape, 1) < members
    norm_left = jnp.sum(jnp.where(at_left, squares, 0.0), axis=1, keepdims=True)
    norm_right = jnp.sum(jnp.where(at_left, 0.0, squares), axis=1, keepdims=True)
    bounds = degree + jnp.sqrt(jnp.where(at_left, norm_left, norm_right))
    inverses = 1.0 / bounds
    spreads = jnp.sqrt(degree * inverses)
    sides = [jnp.broadcast_to(total[grams_end + p : grams_end + p + 1], (PATCH, cols)) for p in pairs]
    iterates = [(grams[p] + degree * identity) * inverses[p : p + 1] for p in pairs]
    roots = [None for _ in pairs]
    for step in range(NS_STEPS):
        lefts = [[halves] for halves in splits(sides)]
        if step == 0:
            ahead = iterates
        else:
            root_halves = splits(roots)
            lefts = [left + [halves] for left, halves in zip(lefts, root_halves)]
            ahead = [parts[0] for parts in products([[halves] for halves in root_halves], rights(iterates))]
        if step < NS_STEPS - 1:
            lefts = [left + [halves] for left, halves in zip(lefts, splits(iterates))]
        corrections = [1.5 * identity - 0.5 * product for product in ahead]
        results = products(lefts, rights(corrections))
        sides = [parts[0] for parts in results]
        roots = corrections if step == 0 else [parts[1] for parts in results]
        iterates = [parts[-1] for parts in results]
    weights = [parts[0][:1] for parts in products([[halves] for halves in splits(sides)], rights(roots))]
    weights = [weights[p] * inverses[p : p + 1] for p in pairs]
    mixings = [(spreads[p : p + 1] * roots[p] + weights[p]).astype(bf16) for p in pairs]

    patch = lax.broadcasted_iota(jnp.int32, (members, cols), 1) // PATCH
    masks = [jnp.where(patch % 4 == k, 1.0, 0.0).astype(bf16) for k in range(4)]
    quads = cols // (4 * PATCH)
    for a in range(tile_rows // PATCH):
        mixing = jnp.concatenate(
            [jnp.concatenate(mixings[2 * q : 2 * q + 2], 1) for q in range(a * quads, (a + 1) * quads)], 0
        )
        for r in range(a * PATCH, (a + 1) * PATCH, 2):
            state = jnp.concatenate(
                [jnp.concatenate([lag_ref[i] * mask for mask in masks], 0) for i in (r, r + 1)], 1
            )
            spread_out = mm(mixing, state)
            for i in (0, 1):
                part = spread_out[:, i * cols : (i + 1) * cols]
                chosen = part[:members]
                for q in range(1, quads):
                    chosen = jnp.where(patch // 4 == q, part[q * members : (q + 1) * members], chosen)
                flat_ref[pl.ds(r + i, members, stride=tile_rows), :] = chosen + mean_ref[r + i : r + i + 1, :]
    out_ref[...] = flat_ref[: members * tile_rows, :].reshape(1, members, tile_rows, cols).astype(bf16)


def shards(history, forecast, spot, alive, levels, precision, radius):
    shares = lax.axis_size("lag")
    tiles = lax.axis_size("dom")
    share_members, tile_rows, cols = forecast.shape
    members = share_members * shares
    patch_cols = cols // PATCH
    def call(kernel, name, in_specs, out_shape, scratch=()):
        return pl.pallas_call(
            kernel,
            in_specs=in_specs,
            out_specs=jax.tree.map(lambda _: vmem, out_shape),
            out_shape=out_shape,
            scratch_shapes=scratch,
            compiler_params=pltpu.CompilerParams(vmem_limit_bytes=32 * 2**20),
            name=name,
        )

    shape = jax.ShapeDtypeStruct
    vmem = pl.BlockSpec(memory_space=pltpu.VMEM)
    parts = [forecast]
    for k in range(1, shares):
        parts.append(lax.ppermute(forecast, "lag", [((i + k) % shares, i) for i in range(shares)]))
    live = lax.broadcasted_iota(jnp.int32, spot.shape, 1) < alive[:, None]
    weights = jnp.where(live, precision, 0.0)
    kind = lax.broadcasted_iota(jnp.int32, (3, *spot.shape), 0)
    tables = jnp.where(kind == 0, weights[None], jnp.where(kind == 1, (weights * levels)[None], spot.astype(f32)[None]))
    inverse = jnp.broadcast_to(
        (1.0 / jnp.square(radius.astype(f32))).reshape(-1, patch_cols, 1), (tile_rows // PATCH, patch_cols, cols)
    )
    sent, tables = lax.optimization_barrier((inverse, tables))
    rings = [ring(tiles, shares, turn) for turn in range(2)]
    axes = ("dom", "lag")
    next_inverses = [lax.ppermute(sent, axes, [(t, s) for s, t in pairs]) for pairs in rings]
    fields, own_sum = call(
        functools.partial(fields_kernel, cols),
        "fields",
        [vmem, vmem],
        [shape((2, tile_rows, cols), f32), shape((tile_rows, cols), f32)],
    )(tables, forecast)
    packed_rows = patch_cols * members * 3 // 4
    message_shape = shape((packed_rows + 2 * patch_cols, 2 * members), bf16)
    total_scratch = pltpu.VMEM((2, patch_cols * members + PATCH, members), f32)
    lag_rows, lag_mean = call(
        state_kernel,
        "state",
        [vmem],
        [shape((tile_rows, members, cols), bf16), shape((tile_rows, cols), f32)],
        [pltpu.VMEM(((members + 1) * tile_rows, cols), f32)],
    )(history[0])
    rows, held, message = call(
        functools.partial(first_kernel, shares),
        "first_gram",
        [vmem] * (shares + 4),
        [shape((tile_rows, members, cols), bf16), shape((2, tile_rows, cols), f32), message_shape],
        [pltpu.VMEM(((members + 1) * tile_rows, cols), f32), total_scratch],
    )(*parts, own_sum, fields, next_inverses[0], lag_mean)
    first = lax.ppermute(message, axes, rings[0])
    message = call(second_kernel, "second_gram", [vmem] * 3, message_shape, [total_scratch])(rows, held, next_inverses[1])
    second = lax.ppermute(message, axes, rings[1])
    own_shape = shape((packed_rows + patch_cols, 2 * members), f32)
    upper = call(upper_kernel, "upper_gram", [vmem] * 3, own_shape)(rows, held, inverse)
    own = call(lower_kernel, "lower_gram", [vmem] * 5, own_shape)(upper, rows, held, inverse, first)
    return call(
        finish_kernel,
        "finish",
        [vmem] * 4,
        shape((1, members, tile_rows, cols), bf16),
        [pltpu.VMEM(((members + 1) * tile_rows, cols), f32)],
    )(own, second, lag_rows, lag_mean)


def solution(mesh):
    in_specs = (
        P("lag", None, "dom", None),
        P("lag", "dom", None),
        P("dom", None),
        P("dom"),
        P("dom", None),
        P("dom", None),
        P("dom"),
    )
    out_specs = P("lag", None, "dom", None)
    return jax.shard_map(shards, mesh=mesh, in_specs=in_specs, out_specs=out_specs, check_vma=False)
```

```python
import functools

import jax
import jax.numpy as jnp
from jax import lax
from jax.experimental import pallas as pl
from jax.experimental.pallas import tpu as pltpu
from jax.sharding import PartitionSpec as P

PATCH = 16
NS_STEPS = 4
RADIUS = 32
FAR = RADIUS - PATCH // 2
NEAR = FAR - PATCH
MIDDLE = (PATCH - 1) / 2

NT = (((1,), (1,)), ((), ()))
NN = (((1,), (0,)), ((), ()))
f32 = jnp.float32
bf16 = jnp.bfloat16


def mm(a, b, dims=NN):
    return lax.dot_general(a, b, dims, preferred_element_type=f32)


def split(x):
    high = x.astype(bf16)
    return high, (x - high.astype(f32)).astype(bf16)


def fields_kernel(cols, table_ref, part_ref, field_ref, sum_ref):
    sum_ref[...] = jnp.sum(part_ref[...].astype(f32), axis=0)
    patches, slots = table_ref.shape[1:]
    patch_cols = cols // PATCH
    patch_rows = patches // patch_cols
    spot = table_ref[2].astype(jnp.int32)
    row_in = spot // PATCH
    col_in = spot % PATCH
    iota_row = lax.broadcasted_iota(jnp.int32, (PATCH, slots), 0)
    iota_col = lax.broadcasted_iota(jnp.int32, (cols, slots), 0)
    for a in range(patch_rows):
        total = jnp.zeros((4 * PATCH, cols), f32)
        for b in range(patch_cols):
            p = a * patch_cols + b
            prec = table_ref[0, p : p + 1, :]
            level = table_ref[1, p : p + 1, :]
            prec_high = prec.astype(bf16).astype(f32)
            level_high = level.astype(bf16).astype(f32)
            on_row = row_in[p : p + 1, :] == iota_row
            pieces = [
                jnp.where(on_row, piece, 0.0).astype(bf16)
                for piece in (prec_high, prec - prec_high, level_high, level - level_high)
            ]
            on_col = jnp.where(col_in[p : p + 1, :] + b * PATCH == iota_col, 1.0, 0.0).astype(bf16)
            total = total + mm(jnp.concatenate(pieces, 0), on_col, NT)
        rows = slice(a * PATCH, (a + 1) * PATCH)
        field_ref[0, rows, :] = total[:PATCH] + total[PATCH : 2 * PATCH]
        field_ref[1, rows, :] = total[2 * PATCH : 3 * PATCH] + total[3 * PATCH :]


def state_kernel(hist_ref, lag_ref, mean_ref, flat_ref):
    members, tile_rows, cols = hist_ref.shape
    state = hist_ref[...].astype(f32)
    mean = jnp.sum(state, axis=0) / members
    mean_ref[...] = mean
    flat_ref[: members * tile_rows, :] = (state - mean[None]).reshape(members * tile_rows, cols)
    for r in range(tile_rows):
        lag_ref[r] = flat_ref[pl.ds(r, members, stride=tile_rows), :].astype(bf16)


def down_first():
    return 1 - lax.axis_index("lag") // (lax.axis_size("lag") // 2)


def ring(tiles, shares, turn):
    half = shares // 2
    pairs = []
    for t in range(tiles):
        for l in range(shares):
            target = t + (-1 if (l // half) ^ turn else 1)
            if 0 <= target < tiles:
                pairs.append((t * shares + l, target * shares + l))
            else:
                pairs.append((t * shares + l, t * shares + (l + half) % shares))
    return pairs


def taper_plan(centre_row, inverse_square):
    q_row = lax.broadcasted_iota(jnp.int32, inverse_square.shape, 0)
    col = lax.broadcasted_iota(jnp.int32, inverse_square.shape, 1)
    col_square = jnp.square(col.astype(f32) - (q_row.astype(f32) * PATCH + MIDDLE))
    return centre_row, col_square, inverse_square


def accumulate(total, plan, anomalies, weight, innovation, first_row):
    centre_row, col_square, inverse_square = plan
    patches, cols = col_square.shape
    lefts = []
    for i, anomaly in enumerate(anomalies):
        members = anomaly.shape[0]
        offset = (first_row + i).astype(f32) - centre_row
        taper = jnp.square(jnp.maximum(0.0, 1.0 - (offset * offset + col_square) * inverse_square))
        scale = taper * weight[i : i + 1]
        blocks = anomaly.reshape(members // PATCH, PATCH, cols)
        left = [
            (blocks * jnp.broadcast_to(scale[q : q + 1], (PATCH, cols)).astype(bf16)[None]).reshape(members, cols)
            for q in range(patches)
        ]
        tail = taper * innovation[i : i + 1]
        left.append(jnp.concatenate([tail, jnp.zeros((PATCH - patches, cols), f32)], 0).astype(bf16))
        lefts.append(jnp.concatenate(left, 0))
    return total + mm(jnp.concatenate(lefts, 1), jnp.concatenate(anomalies, 1), NT)


STEP = 8


def packed(totals, members, patch_cols):
    pairs = patch_cols // 2
    half = members // 2
    grams, sides = [], []
    for total in totals:
        for pair in range(pairs):
            at = 2 * pair * members
            grams.append(jnp.concatenate([total[at : at + members], total[at + members : at + 2 * members]], 1))
        for pair in range(pairs):
            at = patch_cols * members + 2 * pair
            sides.append(jnp.concatenate([total[at : at + 1], total[at + 1 : at + 2]], 1))
    lane = lax.broadcasted_iota(jnp.int32, (half, 2 * members), 1)
    tops = [gram[:half] for gram in grams]
    ends = [
        jnp.where(lane % members < half, pltpu.roll(a[half:], 2 * members - half, 1), b[half:])
        for a, b in zip(grams[::2], grams[1::2])
    ]
    return jnp.concatenate(tops + ends, 0), jnp.concatenate(sides, 0)


def unpacked(rows, members):
    half = members // 2
    wide = 2 * members
    count = rows.shape[0] * 2 // (3 * half)
    lane = lax.broadcasted_iota(jnp.int32, (half, wide), 1)
    tops = [rows[p * half : (p + 1) * half] for p in range(count)]
    ends = [rows[(count + k) * half : (count + k + 1) * half] for k in range(count // 2)]
    per_square = wide // half
    turned = [
        jnp.transpose(jnp.concatenate(tops[p : p + per_square], 0)) for p in range(0, count, per_square)
    ]
    grams = []
    for p in range(count):
        square, at = turned[p // per_square], (p % per_square) * half
        first = pltpu.roll(square[half:members], (wide - at) % wide, 1)
        second = pltpu.roll(square[members + half :], (members + wide - at) % wide, 1)
        corner = ends[p // 2] if p % 2 else pltpu.roll(ends[p // 2], half, 1)
        bottom = jnp.where(lane % members < half, jnp.where(lane < members, first, second), corner)
        grams.append(jnp.concatenate([tops[p], bottom], 0))
    return grams


def message_of(grams, sides):
    return jnp.concatenate([grams.astype(bf16), *split(sides)], 0)


def read_message(ref, side_count):
    at = ref.shape[0] - 2 * side_count
    high, low = ref[at : at + side_count, :].astype(f32), ref[at + side_count :, :].astype(f32)
    return jnp.concatenate([ref[:at, :].astype(f32), high + low], 0)


def arrived(ref, turn, side_count):
    tile = lax.axis_index("dom")
    there = jnp.where(down_first() ^ turn == 1, tile > 0, tile < lax.axis_size("dom") - 1)
    return jnp.where(there, read_message(ref, side_count), 0.0)


def outward(turn, rows_ref, held_ref, inverse_ref, message_ref, total_ref):
    tile_rows, members, cols = rows_ref.shape
    patch_cols = cols // PATCH
    down = down_first() ^ turn
    near = pl.multiple_of(down * (tile_rows - NEAR), 8)
    middle = jnp.where(down == 0, MIDDLE - PATCH, MIDDLE + tile_rows)
    plans = [
        taper_plan(middle, inverse_ref[1 - down]),
        taper_plan(middle + jnp.where(down == 0, -PATCH, PATCH).astype(f32), inverse_ref[down]),
    ]
    anomalies = [rows_ref[near + i] for i in range(NEAR)]
    fields = [held_ref[k, pl.ds(near, NEAR), :] for k in range(2)]
    blank = jnp.zeros(total_ref.shape[1:], f32)
    totals = [accumulate(blank, plan, anomalies, *fields, near) for plan in plans]
    for start in range(NEAR, FAR, STEP):
        anomalies = [rows_ref[start + i] for i in range(STEP)]
        fields = [held_ref[k, start : start + STEP, :] for k in range(2)]
        totals[0] = accumulate(totals[0], plans[0], anomalies, *fields, jnp.int32(start))
    total_ref[1 - down] = totals[0]
    total_ref[down] = totals[1]
    message_ref[...] = message_of(*packed([total_ref[0], total_ref[1]], members, patch_cols))


def first_kernel(shares, *refs):
    parts, refs = refs[:shares], refs[shares:]
    sum_ref, field_ref, inverse_ref, _, rows_ref, held_ref, message_ref, flat_ref, total_ref = refs
    share_members, tile_rows, cols = parts[0].shape
    members = share_members * shares
    lag = lax.axis_index("lag")
    states = [part[...].astype(f32) for part in parts]
    mean = functools.reduce(jnp.add, [jnp.sum(state, axis=0) for state in states[1:]], sum_ref[...]) / members
    for k, state in enumerate(states):
        at = pl.multiple_of(lax.rem(lag + k, shares) * (share_members * tile_rows), 8)
        flat_ref[pl.ds(at, share_members * tile_rows), :] = (state - mean[None]).reshape(-1, cols)
    weight = field_ref[0]
    held_ref[0] = weight
    held_ref[1] = field_ref[1] - mean * weight
    for r in range(tile_rows):
        rows_ref[r] = flat_ref[pl.ds(r, members, stride=tile_rows), :].astype(bf16)
    outward(0, rows_ref, held_ref, inverse_ref, message_ref, total_ref)


def second_kernel(rows_ref, held_ref, inverse_ref, message_ref, total_ref):
    outward(1, rows_ref, held_ref, inverse_ref, message_ref, total_ref)


def own_sums(rows, rows_ref, held_ref, inverse_ref):
    members, cols = rows_ref.shape[1:]
    patch_rows, patch_cols = inverse_ref.shape[:2]
    plans = [taper_plan(MIDDLE + a * PATCH, inverse_ref[a]) for a in range(patch_rows)]
    totals = [jnp.zeros((patch_cols * members + PATCH, members), f32) for _ in plans]
    for start in range(rows.start, rows.stop, STEP):
        anomalies = [rows_ref[start + i] for i in range(STEP)]
        fields = [held_ref[k, start : start + STEP, :] for k in range(2)]
        totals = [accumulate(total, plan, anomalies, *fields, jnp.int32(start)) for total, plan in zip(totals, plans)]
    return jnp.concatenate(packed(totals, members, patch_cols), 0)


def upper_kernel(rows_ref, held_ref, inverse_ref, out_ref):
    out_ref[...] = own_sums(slice(0, rows_ref.shape[0] // 2), rows_ref, held_ref, inverse_ref)


def lower_kernel(upper_ref, rows_ref, held_ref, inverse_ref, first_ref, out_ref):
    tile_rows = rows_ref.shape[0]
    sums = own_sums(slice(tile_rows // 2, tile_rows), rows_ref, held_ref, inverse_ref)
    out_ref[...] = upper_ref[...] + sums + arrived(first_ref, 0, inverse_ref.shape[1])


def finish_kernel(total_ref, second_ref, lag_ref, mean_ref, out_ref, flat_ref):
    tile_rows, members, cols = lag_ref.shape
    degree = members - 1.0
    pair_count = (tile_rows // PATCH) * (cols // PATCH) // 2
    grams_end = total_ref.shape[0] - pair_count
    row = lax.broadcasted_iota(jnp.int32, (members, cols), 0)
    lane = lax.broadcasted_iota(jnp.int32, (members, cols), 1)
    identity = jnp.where(row == lane % members, 1.0, 0.0)
    left_mask = jnp.where(lane < members, 1.0, 0.0).astype(bf16)
    right_mask = jnp.where(lane < members, 0.0, 1.0).astype(bf16)

    def splits(parts):
        highs = [part.astype(bf16) for part in parts]
        rests = [part - high.astype(f32) for part, high in zip(parts, highs)]
        return list(zip(highs, [rest.astype(bf16) for rest in rests]))

    def rights(parts):
        return [
            jnp.concatenate(
                [jnp.concatenate([half * mask for half in halves], 1) for mask in (left_mask, right_mask)], 0
            )
            for halves in splits(parts)
        ]

    def products(lefts, factors):
        stacks = [
            jnp.concatenate(
                [jnp.concatenate([half.astype(f32) for half in left[0]], 0).astype(bf16)]
                + [half for halves in left[1:] for half in halves]
                if left[0][0].shape[0] < PATCH
                else [half for halves in left for half in halves],
                0,
            )
            for left in lefts
        ]
        boths = [mm(stack, factor) for stack, factor in zip(stacks, factors)]
        results = []
        for left, both in zip(lefts, boths):
            parts, at = [], 0
            for high, low in left:
                rows = high.shape[0]
                upper, lower = both[at : at + rows], both[at + rows : at + 2 * rows]
                parts.append(upper[:, :cols] + (upper[:, cols:] + lower[:, :cols]))
                at += 2 * rows
            results.append(parts)
        return results

    total = total_ref[...] + arrived(second_ref, 1, pair_count)
    pairs = range(pair_count)
    grams = unpacked(total[:grams_end], members)
    squares = jnp.concatenate([jnp.sum(gram * gram, axis=0, keepdims=True) for gram in grams], 0)
    at_left = lax.broadcasted_iota(jnp.int32, squares.shape, 1) < members
    norm_left = jnp.sum(jnp.where(at_left, squares, 0.0), axis=1, keepdims=True)
    norm_right = jnp.sum(jnp.where(at_left, 0.0, squares), axis=1, keepdims=True)
    bounds = degree + jnp.sqrt(jnp.where(at_left, norm_left, norm_right))
    inverses = 1.0 / bounds
    spreads = jnp.sqrt(degree * inverses)
    sides = [jnp.broadcast_to(total[grams_end + p : grams_end + p + 1], (PATCH // 2, cols)) for p in pairs]
    iterates = [(grams[p] + degree * identity) * inverses[p : p + 1] for p in pairs]
    roots = [None for _ in pairs]
    for step in range(NS_STEPS):
        lefts = [[halves] for halves in splits(sides)]
        if step == 0:
            ahead = iterates
        else:
            root_halves = splits(roots)
            lefts = [left + [halves] for left, halves in zip(lefts, root_halves)]
            ahead = [parts[0] for parts in products([[halves] for halves in root_halves], rights(iterates))]
        if step < NS_STEPS - 1:
            lefts = [left + [halves] for left, halves in zip(lefts, splits(iterates))]
        corrections = [1.5 * identity - 0.5 * product for product in ahead]
        results = products(lefts, rights(corrections))
        sides = [parts[0] for parts in results]
        roots = corrections if step == 0 else [parts[1] for parts in results]
        iterates = [parts[-1] for parts in results]
    weights = [parts[0][:1] for parts in products([[halves] for halves in splits(sides)], rights(roots))]
    weights = [weights[p] * inverses[p : p + 1] for p in pairs]
    mixings = [(spreads[p : p + 1] * roots[p] + weights[p]).astype(bf16) for p in pairs]

    patch = lax.broadcasted_iota(jnp.int32, (members, cols), 1) // PATCH
    masks = [jnp.where(patch % 4 == k, 1.0, 0.0).astype(bf16) for k in range(4)]
    quads = cols // (4 * PATCH)
    for a in range(tile_rows // PATCH):
        mixing = jnp.concatenate(
            [jnp.concatenate(mixings[2 * q : 2 * q + 2], 1) for q in range(a * quads, (a + 1) * quads)], 0
        )
        for r in range(a * PATCH, (a + 1) * PATCH, 2):
            state = jnp.concatenate(
                [jnp.concatenate([lag_ref[i] * mask for mask in masks], 0) for i in (r, r + 1)], 1
            )
            spread_out = mm(mixing, state)
            for i in (0, 1):
                part = spread_out[:, i * cols : (i + 1) * cols]
                chosen = part[:members]
                for q in range(1, quads):
                    chosen = jnp.where(patch // 4 == q, part[q * members : (q + 1) * members], chosen)
                flat_ref[pl.ds(r + i, members, stride=tile_rows), :] = chosen + mean_ref[r + i : r + i + 1, :]
    out_ref[...] = flat_ref[: members * tile_rows, :].reshape(1, members, tile_rows, cols).astype(bf16)


def shards(history, forecast, spot, alive, levels, precision, radius):
    shares = lax.axis_size("lag")
    tiles = lax.axis_size("dom")
    share_members, tile_rows, cols = forecast.shape
    members = share_members * shares
    patch_cols = cols // PATCH
    def call(kernel, name, in_specs, out_shape, scratch=()):
        return pl.pallas_call(
            kernel,
            in_specs=in_specs,
            out_specs=jax.tree.map(lambda _: vmem, out_shape),
            out_shape=out_shape,
            scratch_shapes=scratch,
            compiler_params=pltpu.CompilerParams(vmem_limit_bytes=32 * 2**20),
            name=name,
        )

    shape = jax.ShapeDtypeStruct
    vmem = pl.BlockSpec(memory_space=pltpu.VMEM)
    parts = [forecast]
    for k in range(1, shares):
        parts.append(lax.ppermute(forecast, "lag", [((i + k) % shares, i) for i in range(shares)]))
    live = lax.broadcasted_iota(jnp.int32, spot.shape, 1) < alive[:, None]
    weights = jnp.where(live, precision, 0.0)
    kind = lax.broadcasted_iota(jnp.int32, (3, *spot.shape), 0)
    tables = jnp.where(kind == 0, weights[None], jnp.where(kind == 1, (weights * levels)[None], spot.astype(f32)[None]))
    inverse = jnp.broadcast_to(
        (1.0 / jnp.square(radius.astype(f32))).reshape(-1, patch_cols, 1), (tile_rows // PATCH, patch_cols, cols)
    )
    sent, tables = lax.optimization_barrier((inverse, tables))
    rings = [ring(tiles, shares, turn) for turn in range(2)]
    axes = ("dom", "lag")
    next_inverses = [lax.ppermute(sent, axes, [(t, s) for s, t in pairs]) for pairs in rings]
    fields, own_sum = call(
        functools.partial(fields_kernel, cols),
        "fields",
        [vmem, vmem],
        [shape((2, tile_rows, cols), f32), shape((tile_rows, cols), f32)],
    )(tables, forecast)
    packed_rows = patch_cols * members * 3 // 4
    message_shape = shape((packed_rows + 2 * patch_cols, 2 * members), bf16)
    total_scratch = pltpu.VMEM((2, patch_cols * members + PATCH, members), f32)
    lag_rows, lag_mean = call(
        state_kernel,
        "state",
        [vmem],
        [shape((tile_rows, members, cols), bf16), shape((tile_rows, cols), f32)],
        [pltpu.VMEM(((members + 1) * tile_rows, cols), f32)],
    )(history[0])
    rows, held, message = call(
        functools.partial(first_kernel, shares),
        "first_gram",
        [vmem] * (shares + 4),
        [shape((tile_rows, members, cols), bf16), shape((2, tile_rows, cols), f32), message_shape],
        [pltpu.VMEM(((members + 1) * tile_rows, cols), f32), total_scratch],
    )(*parts, own_sum, fields, next_inverses[0], lag_mean)
    first = lax.ppermute(message, axes, rings[0])
    message = call(second_kernel, "second_gram", [vmem] * 3, message_shape, [total_scratch])(rows, held, next_inverses[1])
    second = lax.ppermute(message, axes, rings[1])
    own_shape = shape((packed_rows + patch_cols, 2 * members), f32)
    upper = call(upper_kernel, "upper_gram", [vmem] * 3, own_shape)(rows, held, inverse)
    own = call(lower_kernel, "lower_gram", [vmem] * 5, own_shape)(upper, rows, held, inverse, first)
    return call(
        finish_kernel,
        "finish",
        [vmem] * 4,
        shape((1, members, tile_rows, cols), bf16),
        [pltpu.VMEM(((members + 1) * tile_rows, cols), f32)],
    )(own, second, lag_rows, lag_mean)


def solution(mesh):
    in_specs = (
        P("lag", None, "dom", None),
        P("lag", "dom", None),
        P("dom", None),
        P("dom"),
        P("dom", None),
        P("dom", None),
        P("dom"),
    )
    out_specs = P("lag", None, "dom", None)
    return jax.shard_map(shards, mesh=mesh, in_specs=in_specs, out_specs=out_specs, check_vma=False)
```
